32 devices in a mesh: dp: 4 (over z), mp: 8 (over y, x, core).
Axes of the slice: x: 2, y: 2, z: 4, core: 2. Of those that a mesh axis runs over, the one named last changes fastest.
Arguments:
- code_ids: int32 [16, 1024], P('dp'), may hold values from 0 to 8191
- code_mask: int32 [16, 1024], P('dp'), may hold values from 0 to 1
- caption_ids: int32 [8, 128], P('dp'), may hold values from 0 to 15999
- caption_segments: int32 [8, 128], P('dp'), may hold values from 0 to 15, as said below
- image_row: int32 [16], P('dp'), may hold values from 0 to 7, as said below
- attention_master: float32 [3, 4, 1024, 1024], P(None, None, 'dp', 'mp')
- attention_momentum: float32 [3, 4, 1024, 1024], P(None, None, 'dp', 'mp'), may hold values from -1.9073486e-05 to 1.9073486e-05
- attention_average: float32 [3, 4, 1024, 1024], P(None, None, 'dp', 'mp')
- dense_master: float32 [2, 2, 1024, 4096], P(None, None, 'dp', 'mp'), may hold values from -0.1875 to 0.1875
- dense_momentum: float32 [2, 2, 1024, 4096], P(None, None, 'dp', 'mp'), may hold values from -1.9073486e-05 to 1.9073486e-05
- dense_average: float32 [2, 2, 1024, 4096], P(None, None, 'dp', 'mp'), may hold values from -0.1875 to 0.1875
- text_master: float32 [16000, 1024], P('mp', 'dp'), may hold values from -1 to 1
- text_momentum: float32 [16000, 1024], P('mp', 'dp'), may hold values from -1.9073486e-05 to 1.9073486e-05
- text_average: float32 [16000, 1024], P('mp', 'dp'), may hold values from -1 to 1
- code_master: float32 [2, 8192, 1024], P(None, 'mp', 'dp'), may hold values from -1 to 1
- code_momentum: float32 [2, 8192, 1024], P(None, 'mp', 'dp'), may hold values from -1.9073486e-05 to 1.9073486e-05
- code_average: float32 [2, 8192, 1024], P(None, 'mp', 'dp'), may hold values from -1 to 1
- gain_master: float32 [7, 1024], P(None, ('dp', 'mp'))
- gain_momentum: float32 [7, 1024], P(None, ('dp', 'mp')), may hold values from -0.00018310547 to 0.00018310547
- gain_average: float32 [7, 1024], P(None, ('dp', 'mp')), may hold values from 0.5 to 1.5
Outputs:
- loss: float32 [], replicated
- clip_norm: float32 [], replicated
- attention_new: float32 [3, 4, 1024, 1024], P(None, None, 'dp', 'mp')
- attention_moment: float32 [3, 4, 1024, 1024], P(None, None, 'dp', 'mp')
- attention_mean: float32 [3, 4, 1024, 1024], P(None, None, 'dp', 'mp')
- attention_copy: bfloat16 [3, 4, 1024, 1024], P(None, None, 'dp', 'mp')
- dense_new: float32 [2, 2, 1024, 4096], P(None, None, 'dp', 'mp')
- dense_moment: float32 [2, 2, 1024, 4096], P(None, None, 'dp', 'mp')
- dense_mean: float32 [2, 2, 1024, 4096], P(None, None, 'dp', 'mp')
- dense_copy: bfloat16 [2, 2, 1024, 4096], P(None, None, 'dp', 'mp')
- text_new: float32 [16000, 1024], P('mp', 'dp')
- text_moment: float32 [16000, 1024], P('mp', 'dp')
- text_mean: float32 [16000, 1024], P('mp', 'dp')
- text_copy: bfloat16 [16000, 1024], P('mp', 'dp')
- code_new: float32 [2, 8192, 1024], P(None, 'mp', 'dp')
- code_moment: float32 [2, 8192, 1024], P(None, 'mp', 'dp')
- code_mean: float32 [2, 8192, 1024], P(None, 'mp', 'dp')
- code_copy: bfloat16 [2, 8192, 1024], P(None, 'mp', 'dp')
- gain_new: float32 [7, 1024], P(None, ('dp', 'mp'))
- gain_moment: float32 [7, 1024], P(None, ('dp', 'mp'))
- gain_mean: float32 [7, 1024], P(None, ('dp', 'mp'))
- gain_copy: bfloat16 [7, 1024], P(None, ('dp', 'mp'))
- token_loss: float32 [16, 1024], P('dp')
The draws below stay inside these ranges and needn't reach their ends.
Inputs may be any that keep to these rules, and one draw needn't show every extreme that they name: `caption_segments`: each caption row holds the captions of two images, one after the other, each of 32 or more tokens; the images of a row lie in the same group of 4 consecutive images, and every image has its caption in exactly one row. image_row[i] is the row that holds image i's caption.
All inputs are finite; a program needn't handle non-finite values.
Results may differ from the reference program's by a relative error of at most 0.014.
Values may be sent and summed in bfloat16 or wider, within the bound.
A program may use at most 320 MiB of HBM per device.

```python
import math
import jax
import jax.numpy as jnp
import numpy as np
from jax import lax

D = 1024
HEADS = 16
HEAD_DIM = 64
FF = 4096
VC = 8192
VT = 16000
CODE_LEN = 1024
ENC_LEN = 128
IMG_DEV = 4
IMAGES = 16
ROWS = 8


def packing(key):
    blocks = IMAGES // IMG_DEV
    shuffle_key = jax.random.fold_in(key, 11)
    cut_key = jax.random.fold_in(key, 13)
    scores = jax.random.randint(shuffle_key, (blocks, IMG_DEV), 0, 1 << 20) * IMG_DEV + jnp.arange(IMG_DEV, dtype=jnp.int32)[None, :]
    order = jnp.argsort(scores, axis=1).astype(jnp.int32) + (jnp.arange(blocks, dtype=jnp.int32) * IMG_DEV)[:, None]
    pairs = order.reshape(ROWS, 2)
    cuts = jax.random.randint(cut_key, (ROWS,), ENC_LEN // 4, 3 * ENC_LEN // 4 + 1)
    places = jnp.arange(ENC_LEN, dtype=jnp.int32)[None, :]
    segments = jnp.where(places < cuts[:, None], pairs[:, 0:1], pairs[:, 1:2]).astype(jnp.int32)
    owners = jnp.repeat(jnp.arange(ROWS, dtype=jnp.int32), 2)
    image_row = jnp.zeros((IMAGES,), jnp.int32).at[pairs.reshape(-1)].set(owners)
    return (segments, image_row)


def draw_caption_segments(key, part):
    return packing(key)[0]


def draw_image_row(key, part):
    return packing(key)[1]


def draw_code_mask(key, part):
    images = jnp.arange(IMAGES, dtype=jnp.int32)
    last = max(IMAGES - 1, 1)
    chance = 100 + 800 * images * images // (last * last)
    rolls = jax.random.randint(jax.random.fold_in(key, 17), (IMAGES, CODE_LEN), 0, 1000)
    return (rolls < chance[:, None]).astype(jnp.int32)


def draw_gain_master(key, part):
    place = jnp.arange(D, dtype=jnp.float32) / (D - 1)
    inner = jax.random.fold_in(key, 19)
    ramp = 0.5 * jnp.exp(math.log(3.0) * place)
    noise = jax.random.uniform(inner, (7, D), jnp.float32, 0.8, 1.2)
    return noise * ramp[None, :]


def attention_law(key):
    factor = jnp.array([1.0, 1.0, 1.0, 5.0], jnp.float32).reshape(1, 4, 1, 1) / math.sqrt(D)
    base = jnp.clip(jax.random.normal(key, (3, 4, D, D), jnp.float32), -6.0, 6.0)
    return base * factor


def draw_attention_master(key, part):
    return attention_law(jax.random.fold_in(key, 3))


def draw_attention_average(key, part):
    return attention_law(jax.random.fold_in(key, 5))


def with_ends(drawn, own_key, least, top_value):
    index_at = [jax.random.randint(jax.random.fold_in(own_key, axis), (), 0, length) for axis, length in enumerate(drawn.shape)]
    longest = drawn.shape.index(max(drawn.shape))
    beside = index_at[:longest] + [(index_at[longest] + 1) % drawn.shape[longest]] + index_at[longest + 1:]
    return drawn.at[tuple(index_at)].set(least).at[tuple(beside)].set(top_value)


def block_scale(rng, dims, cuts, least, high):
    def one(axis_at, blocks):
        draws = jax.random.uniform(jax.random.fold_in(jax.random.fold_in(rng, 6), axis_at), (blocks,), jnp.float32, least / len(cuts), high / len(cuts))
        return jnp.repeat(jnp.exp(draws), dims[axis_at] // blocks).reshape((-1,) + (1,) * (len(dims) - axis_at - 1))

    factor_of = one(*cuts[0])
    for cut in cuts[1:]:
        factor_of = factor_of * one(*cut)
    return factor_of


def rank_table(number_of, skew):
    weights = [(1 << 20) // math.isqrt(standing ** skew) + 1 for standing in range(1, number_of + 1)]
    spread = 1 + sum(weights) // (1 << 30)
    return np.cumsum(np.array([max(1, weight // spread) for weight in weights]))


def ranked_ids(rng, extent, number_of, skew):
    table = rank_table(number_of, skew)
    pick = jax.random.randint(jax.random.fold_in(rng, 1), extent, 0, int(table[number_of - 1]))
    rank = jnp.searchsorted(jnp.asarray(table, jnp.int32), pick, side="right")
    return jax.random.permutation(jax.random.fold_in(rng, 2), number_of)[rank].astype(jnp.int32)


def gaussian(key, dims, spread, most, pieces=(), kind=jnp.bfloat16):
    loudness = block_scale(key, dims, pieces, -0.22, 0.18) if pieces else 1.0
    values = jax.random.normal(key, dims, jnp.float32) * spread * loudness
    return jnp.minimum(jnp.maximum(values, -most), most).astype(kind)


def setup_inputs(seed: int = 0) -> dict:
    splits = jax.random.split(jax.random.key(seed), 21)
    return {
        "code_ids": with_ends(ranked_ids(splits[0], (IMAGES, CODE_LEN), VC, 1), jax.random.fold_in(splits[0], 3), 0, VC - 1).astype(jnp.int32),
        "code_mask": draw_code_mask(jax.random.fold_in(splits[20], 71), 0),
        "caption_ids": with_ends(ranked_ids(splits[2], (ROWS, ENC_LEN), VT, 2), jax.random.fold_in(splits[2], 3), 0, VT - 1).astype(jnp.int32),
        "caption_segments": draw_caption_segments(jax.random.fold_in(splits[20], 71), 0),
        "image_row": draw_image_row(jax.random.fold_in(splits[20], 71), 0),
        "attention_master": draw_attention_master(jax.random.fold_in(splits[20], 71), 0),
        "attention_momentum": gaussian(splits[6], (3, 4, D, D), (1.3e-6), 1.9073486328125e-05, ((2, 4), (3, 8)), jnp.float32),
        "attention_average": draw_attention_average(jax.random.fold_in(splits[20], 71), 0),
        "dense_master": gaussian(splits[8], (2, 2, D, FF), D ** -0.5, 0.1875, ((2, 4), (3, 8)), jnp.float32),
        "dense_momentum": gaussian(splits[9], (2, 2, D, FF), (1.3e-6), 1.9073486328125e-05, ((2, 4), (3, 8)), jnp.float32),
        "dense_average": gaussian(splits[10], (2, 2, D, FF), D ** -0.5, 0.1875, ((2, 4), (3, 8)), jnp.float32),
        "text_master": gaussian(splits[11], (VT, D), 0.0625, 1.0, ((0, 8), (1, 4)), jnp.float32),
        "text_momentum": gaussian(splits[12], (VT, D), (1.3e-6), 1.9073486328125e-05, ((0, 8), (1, 4)), jnp.float32),
        "text_average": gaussian(splits[13], (VT, D), 0.0625, 1.0, ((0, 8), (1, 4)), jnp.float32),
        "code_master": gaussian(splits[14], (2, VC, D), 0.0625, 1.0, ((1, 8), (2, 4)), jnp.float32),
        "code_momentum": gaussian(splits[15], (2, VC, D), (1.3e-6), 1.9073486328125e-05, ((1, 8), (2, 4)), jnp.float32),
        "code_average": gaussian(splits[16], (2, VC, D), 0.0625, 1.0, ((1, 8), (2, 4)), jnp.float32),
        "gain_master": draw_gain_master(jax.random.fold_in(splits[20], 71), 0),
        "gain_momentum": gaussian(splits[18], (7, D), (1.3e-5), 0.00018310547, ((1, 32),), jnp.float32),
        "gain_average": jnp.clip(1.0 + 0.1 * jax.random.normal(splits[19], (7, D), jnp.float32), 0.5, 1.5),
    }


HIGH = lax.Precision.HIGHEST
EPS = 1e-06
CLIP = 0.01
MOMENT = 0.9
DECAY = 0.75
SMOOTH = 0.1
Z_WEIGHT = 0.01
NEGATIVE = -1e+30

@jax.custom_vjp
def low(v):
    return lax.optimization_barrier(v.astype(jnp.bfloat16)).astype(jnp.float32)

@jax.custom_vjp
def low_back(v):
    return v

def low_keep(v):
    return (low(v), None)

def low_pass(kept, grad):
    return (grad,)

def back_keep(v):
    return (v, None)

def back_low(kept, grad):
    return (low(grad),)
low.defvjp(low_keep, low_pass)
low_back.defvjp(back_keep, back_low)

def matmul(left, right):
    return jnp.dot(left, right, precision=HIGH, preferred_element_type=jnp.float32)

def rms_norm(values, gain):
    return values * lax.rsqrt(lax.optimization_barrier(jnp.mean(values * values, axis=-1, keepdims=True)) + EPS) * gain

def attention(queries_in, keys_in, weights, allowed):
    query = low_back(low(matmul(queries_in, weights[0])))
    key = low_back(low(matmul(keys_in, weights[1])))
    value = low_back(low(matmul(keys_in, weights[2])))
    query = query.reshape(query.shape[0], HEADS, HEAD_DIM)
    key = key.reshape(key.shape[0], HEADS, HEAD_DIM)
    value = value.reshape(value.shape[0], HEADS, HEAD_DIM)
    scores = jnp.einsum('qhe,khe->hqk', query, key, precision=HIGH) * HEAD_DIM ** (-0.5)
    scores = jnp.where(allowed[None], low_back(scores), NEGATIVE)
    shares = low(jax.nn.softmax(scores, axis=-1))
    mixed = jnp.einsum('hqk,khe->qhe', shares, value, precision=HIGH).reshape(-1, D)
    mixed = low_back(low(mixed))
    return low_back(matmul(mixed, weights[3].T))

def feed_forward(normed, weights):
    hidden = low_back(matmul(normed, weights[0]))
    active = low(jax.nn.gelu(hidden, approximate=False))
    return low_back(matmul(active, weights[1].T))

def one_image(params, encoded, caption_segments, codes, valid, image, row):
    attention_set, dense_set, code_tables, gain_set = params
    previous = jnp.concatenate([jnp.zeros((1, D), jnp.float32), code_tables[0][codes[:-1]]], axis=0)
    hidden = low_back(previous)
    causal = jnp.tril(jnp.ones((CODE_LEN, CODE_LEN), bool))
    normed = low(rms_norm(hidden, gain_set[3]))
    hidden = hidden + attention(normed, normed, attention_set[1], causal)
    normed = low(rms_norm(hidden, gain_set[4]))
    context = lax.dynamic_index_in_dim(encoded, row, 0, keepdims=False)
    owners = lax.dynamic_index_in_dim(caption_segments, row, 0, keepdims=False)
    allowed = jnp.broadcast_to((owners == image)[None, :], (CODE_LEN, ENC_LEN))
    hidden = hidden + attention(normed, context, attention_set[2], allowed)
    hidden = hidden + feed_forward(low(rms_norm(hidden, gain_set[5])), dense_set[1])
    final = low(rms_norm(hidden, gain_set[6]))
    logits = low_back(matmul(final, code_tables[1].T))
    partition = jax.nn.logsumexp(logits, axis=-1)
    target = jnp.take_along_axis(logits, codes[:, None], axis=-1)[:, 0]
    per_token = partition - (1.0 - SMOOTH) * target - SMOOTH * lax.optimization_barrier(jnp.mean(logits, axis=-1)) + Z_WEIGHT * partition * partition
    return (jnp.sum(per_token * valid), per_token)

def loss_of(weights, code_ids, code_mask, caption_ids, caption_segments, image_row):
    attention_set, dense_set, text_table, code_tables, gain_set = weights
    segments = caption_segments.reshape(-1)
    encoder = low_back(text_table[caption_ids.reshape(-1)])
    same = segments[:, None] == segments[None, :]
    normed = low(rms_norm(encoder, gain_set[0]))
    encoder = encoder + attention(normed, normed, attention_set[0], same)
    encoder = encoder + feed_forward(low(rms_norm(encoder, gain_set[1])), dense_set[0])
    encoded = low(rms_norm(encoder, gain_set[2])).reshape(ROWS, ENC_LEN, D)
    stepper = jax.checkpoint(one_image)

    def scan_body(running, inputs):
        codes, valid, image, row = inputs
        params = (attention_set, dense_set, code_tables, gain_set)
        value, per_token = stepper(params, encoded, caption_segments, codes, valid, image, row)
        return (running + value, per_token)
    inputs = (code_ids, code_mask.astype(jnp.float32), jnp.arange(IMAGES, dtype=jnp.int32), image_row)
    summed, token_losses = lax.scan(scan_body, jnp.zeros((), jnp.float32), inputs)
    return (summed / jnp.sum(code_mask).astype(jnp.float32), token_losses)

def update(master, moment, average, gradient, factor, rate):
    clipped = gradient * factor
    moment_new = MOMENT * moment + clipped
    master_new = master - rate * (clipped + MOMENT * moment_new)
    average_new = DECAY * average + (1.0 - DECAY) * master_new
    return (master_new, moment_new, average_new, master_new.astype(jnp.bfloat16))

def reference(code_ids, code_mask, caption_ids, caption_segments, image_row, attention_master, attention_momentum, attention_average, dense_master, dense_momentum, dense_average, text_master, text_momentum, text_average, code_master, code_momentum, code_average, gain_master, gain_momentum, gain_average):
    masters = (attention_master, dense_master, text_master, code_master, gain_master)
    weights = tuple((lax.optimization_barrier(master.astype(jnp.bfloat16)).astype(jnp.float32) for master in masters))

    def objective(attention_set, dense_set, text_table, code_tables, gain_set):
        return loss_of((attention_set, dense_set, text_table, code_tables, gain_set), code_ids, code_mask, caption_ids, caption_segments, image_row)
    loss, pull, token_loss = jax.vjp(objective, weights[0], weights[1], weights[2], weights[3], weights[4], has_aux=True)
    gradients = pull(jnp.ones((), jnp.float32))
    squares = jnp.zeros((), jnp.float32)
    for gradient in gradients:
        squares = squares + jnp.sum(gradient * gradient)
    norm = jnp.sqrt(squares)
    factor = jnp.minimum(1.0, CLIP / norm)
    rate = 0.012 * math.sqrt(12 * D * D + 4 * D * FF + VT * D + 2 * VC * D + 7 * D) / CLIP
    attention_out = update(attention_master, attention_momentum, attention_average, gradients[0], factor, rate)
    dense_out = update(dense_master, dense_momentum, dense_average, gradients[1], factor, rate)
    text_out = update(text_master, text_momentum, text_average, gradients[2], factor, rate)
    code_out = update(code_master, code_momentum, code_average, gradients[3], factor, rate)
    gain_out = update(gain_master, gain_momentum, gain_average, gradients[4], factor, rate)
    return (loss, norm, attention_out[0], attention_out[1], attention_out[2], attention_out[3], dense_out[0], dense_out[1], dense_out[2], dense_out[3], text_out[0], text_out[1], text_out[2], text_out[3], code_out[0], code_out[1], code_out[2], code_out[3], gain_out[0], gain_out[1], gain_out[2], gain_out[3], token_loss)
```

```python
from functools import partial
import math

import jax
import jax.numpy as jnp
from jax import lax
from jax.experimental import pallas as pl
from jax.experimental.pallas import tpu as pltpu
from jax.sharding import Mesh, PartitionSpec as P

D = 1024
HEAD_DIM = 64
FF = 4096
VC = 8192
VT = 16000


EPS = 1e-06
CLIP = 0.01
MOMENT = 0.9
DECAY = 0.75
SMOOTH = 0.1
Z_WEIGHT = 0.01
NEGATIVE = -1e30
LAST = (((1,), (1,)), ((), ()))
FIRST = (((0,), (0,)), ((), ()))


MESH = pl.DeviceIdType.MESH
ORDERS = ((0, 1, 2), (0, 2, 1), (1, 0, 2), (2, 0, 1))


def sources(n):
    return [(far, bits) for far in range(1 - n, n) for bits in range(4)]


def hops(far, bits):
    return abs(far) + (bits & 1) + (bits >> 1)


def arrival(order, far, bits):
    last = None
    for dim in order:
        if (dim == 0 and far != 0) or (dim > 0 and bits & dim):
            last = dim
    return last


def passes(order, far, bits):
    came = arrival(order, far, bits)
    place = -1 if came is None else order.index(came)
    found = [(0, -1 if far > 0 else 1)] if came == 0 else []
    for dim in order[place + 1 :]:
        found += [(0, 1), (0, -1)] if dim == 0 else [(dim, 0)]
    return found


def cut_slabs(shapes, gap):
    slabs = []
    base = 0.0
    for which, (rows, _) in enumerate(shapes):
        small = max(16, rows // 6 // 16 * 16)
        large = (rows - 2 * small) // 2 // 16 * 16
        begin = 0
        for order, count in zip(ORDERS, (small, small, large, rows - 2 * small - large)):
            slabs.append((which, begin, count, order, base))
            begin += count
        base += gap
    return slabs


def wide(shape, n):
    _, rows, columns = shape
    return (n * rows, 4 * columns) if columns % 128 == 0 else (4 * n * rows, columns)


def placed(whole, shape, z, i, begin, rows):
    if shape[2] % 128 == 0:
        return whole.at[
            :,
            pl.ds(pl.multiple_of(z * shape[1] + begin, 16), rows),
            pl.ds(pl.multiple_of(i * shape[2], 128), shape[2]),
        ]
    return whole.at[:, pl.ds(pl.multiple_of((z * 4 + i) * shape[1] + begin, 16), rows)]


class Here:
    def __init__(self, n):
        self.n = n
        self.z = lax.axis_index("dp")
        self.i = lax.axis_index("img")
        self.t = lax.axis_index("t")

    def device(self, dim, step):
        if dim == 0:
            return (self.z + step, self.i, self.t)
        return (self.z, jnp.bitwise_xor(self.i, dim), self.t)

    def below(self):
        return self.z > 0

    def above(self):
        return self.z < self.n - 1

    def side(self, step):
        return self.above() if step > 0 else self.below()

    def greet(self):
        barrier = pltpu.get_barrier_semaphore()

        def tell(device):
            pl.semaphore_signal(barrier, inc=1, device_id=device, device_id_type=MESH)

        pl.when(self.below())(lambda: tell(self.device(0, -1)))
        pl.when(self.above())(lambda: tell(self.device(0, 1)))
        tell(self.device(1, 0))
        tell(self.device(2, 0))
        pl.semaphore_wait(
            barrier, 2 + jnp.where(self.below(), 1, 0) + jnp.where(self.above(), 1, 0)
        )

    def exists(self, far):
        if far == 0:
            return None
        return (self.z + far >= 0) if far < 0 else (self.z + far < self.n)


def guarded(condition, action):
    if condition is None:
        action()
    else:
        pl.when(condition)(action)


def both(first, second):
    if first is None or second is None:
        return second if first is None else first
    return jnp.logical_and(first, second)


def gather_kernel(n, slabs, count, *refs):
    ins, outs = refs[:count], refs[count : 2 * count]
    send_sem, recv_sem, local_sem = refs[2 * count :]
    here = Here(n)
    here.greet()
    local = []
    for which in range(count):
        shape = ins[which].shape
        copy = pltpu.make_async_copy(
            ins[which], placed(outs[which], shape, here.z, here.i, 0, shape[1]), local_sem.at[which]
        )
        copy.start()
        local.append(copy)

    def block(slab, far, bits):
        which, begin, rows = slabs[slab][:3]
        return placed(
            outs[which], ins[which].shape, here.z + far, jnp.bitwise_xor(here.i, bits), begin, rows
        )

    def name(far, bits):
        return (here.z + far) * 4 + jnp.bitwise_xor(here.i, bits)

    def copy_of(slab, far, bits, dim, step):
        which, begin, rows = slabs[slab][:3]
        target = block(slab, far, bits)
        own = far == 0 and bits == 0
        return pltpu.make_async_remote_copy(
            src_ref=ins[which].at[:, pl.ds(begin, rows)] if own else target,
            dst_ref=target,
            send_sem=send_sem.at[slab, name(far, bits), (1 + step) // 2 if dim == 0 else 1 + dim],
            recv_sem=recv_sem.at[slab, name(far, bits)],
            device_id=here.device(dim, step),
            device_id_type=MESH,
        )

    def arrive(slab, far, bits):
        target = block(slab, far, bits)
        pltpu.make_async_remote_copy(
            src_ref=target,
            dst_ref=target,
            send_sem=send_sem.at[slab, 0, 0],
            recv_sem=recv_sem.at[slab, name(far, bits)],
            device_id=here.device(1, 0),
            device_id_type=MESH,
        ).wait_recv()

    events = sorted(
        (slabs[slab][4] + hops(far, bits), slab, far, bits)
        for slab in range(len(slabs))
        for far, bits in sources(n)
    )
    sent = []
    final = []
    for _, slab, far, bits in events:
        onward = passes(slabs[slab][3], far, bits)
        own = far == 0 and bits == 0
        if not onward:
            final.append((slab, far, bits))
            continue

        def act(slab=slab, far=far, bits=bits, onward=onward, own=own):
            if not own:
                arrive(slab, far, bits)
            for dim, step in onward:
                guarded(
                    here.side(step) if dim == 0 else None,
                    lambda dim=dim, step=step: copy_of(slab, far, bits, dim, step).start(),
                )

        guarded(here.exists(far), act)
        sent += [(slab, far, bits, dim, step) for dim, step in onward]
    for slab, far, bits in final:
        guarded(here.exists(far), lambda at=(slab, far, bits): arrive(*at))
    for slab, far, bits, dim, step in sent:
        guarded(
            both(here.exists(far), here.side(step) if dim == 0 else None),
            lambda at=(slab, far, bits, dim, step): copy_of(*at).wait_send(),
        )
    for copy in local:
        copy.wait()


def gather(arrays, n, gap, collective_id):
    count = len(arrays)
    slabs = cut_slabs([a.shape[1:] for a in arrays], gap)
    size = sum(a.size * a.dtype.itemsize for a in arrays) * 4 * n
    return pl.pallas_call(
        partial(gather_kernel, n, slabs, count),
        out_shape=[
            jax.ShapeDtypeStruct((a.shape[0],) + wide(a.shape, n), a.dtype) for a in arrays
        ],
        in_specs=[pl.BlockSpec(memory_space=pl.ANY)] * count,
        out_specs=[pl.BlockSpec(memory_space=pl.ANY)] * count,
        scratch_shapes=[
            pltpu.SemaphoreType.DMA((len(slabs), 4 * n, 4)),
            pltpu.SemaphoreType.DMA((len(slabs), 4 * n)),
            pltpu.SemaphoreType.DMA((count,)),
        ],
        compiler_params=pltpu.CompilerParams(
            collective_id=collective_id, has_side_effects=True
        ),
        cost_estimate=pl.CostEstimate(flops=0, bytes_accessed=size * 16, transcendentals=0),
        name="gather",
    )(*arrays)


def places(n, order):
    table = {}
    used = 0
    line = [b for b in range(4) if any(dim == 0 for dim, _ in passes(order, 0, b))]
    for rank, bits in enumerate(line):
        for far in range(1 - n, n):
            for dim, step in passes(order, far, bits):
                if dim == 0:
                    second = far == 0 and step < 0
                    table[far, bits, dim, step] = (
                        (used + n, False) if second else (used + far, True)
                    )
        used += n + 1
    for flip in (1, 2):
        pairs = [p for p in sources(n) if (flip, 0) in passes(order, *p)]
        spread = any(far for far, _ in pairs)
        for bits in sorted({b for _, b in pairs}):
            for far, other in pairs:
                if other == bits:
                    table[far, bits, flip, 0] = (used + far, True) if spread else (used, False)
            used += n if spread else 1
    return table, used


def scatter_kernel(n, slabs, members, *refs):
    total = sum(members)
    count = len(members)
    ins, refs = refs[:total], refs[total:]
    outs, owns, gots = refs[:count], refs[count : 2 * count], refs[2 * count : 3 * count]
    send_sem, recv_sem, local_sem = refs[3 * count :]
    here = Here(n)
    tables = {order: places(n, order)[0] for order in ORDERS}
    loads = []
    for which in range(count):
        for member in range(members[which]):
            matrix = ins[sum(members[:which]) + member]
            rows = owns[which].shape[2] // members[which]
            columns = owns[which].shape[3]
            for z in range(n):
                for i in range(4):
                    copy = pltpu.make_async_copy(
                        matrix.at[pl.ds(z * rows, rows), pl.ds(i * columns, columns)]
                        if matrix.shape[0] == n * rows
                        else matrix.at[pl.ds((z * 4 + i) * rows, rows)],
                        owns[which].at[z, i, pl.ds(member * rows, rows)],
                        local_sem.at[len(loads)],
                    )
                    copy.start()
                    loads.append(copy)
    here.greet()
    for copy in loads:
        copy.wait()

    def own(slab, far, bits):
        which, begin, rows = slabs[slab][:3]
        return owns[which].at[
            here.z + far, jnp.bitwise_xor(here.i, bits), pl.ds(begin, rows)
        ]

    def slot(slab, number):
        which, _, rows, _, _, first = slabs[slab]
        return gots[which].at[pl.ds(pl.multiple_of(first + number * rows, 16), rows)]

    def number_at(order, z, key):
        constant, counts = tables[order][key]
        return constant + z if counts else constant

    def copy_of(slab, far, bits):
        order = slabs[slab][3]
        dim = arrival(order, far, bits)
        step = 0 if dim else (1 if far > 0 else -1)
        number = number_at(order, here.z + step, (far - step, bits ^ dim, dim, -step))
        return pltpu.make_async_remote_copy(
            src_ref=own(slab, far, bits),
            dst_ref=slot(slab, number),
            send_sem=send_sem.at[slab, (here.z + far) * 4 + bits],
            recv_sem=recv_sem.at[slab, number],
            device_id=here.device(dim, step),
            device_id_type=MESH,
        )

    events = sorted(
        (slabs[slab][4] + n + 1 - hops(far, bits), slab, far, bits)
        for slab in range(len(slabs))
        for far, bits in sources(n)
    )

    def add_up(slab, far, bits, parts):
        which, begin, rows, order = slabs[slab][:4]
        numbers = [number_at(order, here.z, (far, bits) + part) for part in parts]
        for number in numbers:
            landed = slot(slab, number)
            pltpu.make_async_remote_copy(
                src_ref=landed,
                dst_ref=landed,
                send_sem=send_sem.at[slab, 0],
                recv_sem=recv_sem.at[slab, number],
                device_id=here.device(1, 0),
                device_id_type=MESH,
            ).wait_recv()
        root = far == 0 and bits == 0
        if not parts and not root:
            return
        mine = own(slab, far, bits)
        landed = [slot(slab, number) for number in numbers]

        @pl.loop(0, rows // 16)
        def _(row):
            at = pl.ds(pl.multiple_of(row * 16, 16), 16)
            added = mine[at].astype(jnp.float32)
            for part in landed:
                added = added + part[at].astype(jnp.float32)
            if root:
                outs[which][pl.ds(pl.multiple_of(begin + row * 16, 16), 16)] = added
            else:
                mine[at] = added.astype(jnp.bfloat16)

    for _, slab, far, bits in events:

        def act(slab=slab, far=far, bits=bits):
            parts = passes(slabs[slab][3], far, bits)
            fixed = [p for p in parts if p[0]]
            line = [p for p in parts if not p[0]]
            if not line:
                add_up(slab, far, bits, fixed)
            elif len(line) == 1:
                there = here.side(line[0][1])
                pl.when(there)(lambda: add_up(slab, far, bits, line + fixed))
                pl.when(jnp.logical_not(there))(lambda: add_up(slab, far, bits, fixed))
            else:
                low, high = here.below(), here.above()
                up, down = line
                pl.when(jnp.logical_and(low, high))(
                    lambda: add_up(slab, far, bits, line + fixed)
                )
                pl.when(jnp.logical_not(low))(lambda: add_up(slab, far, bits, [up] + fixed))
                pl.when(jnp.logical_not(high))(lambda: add_up(slab, far, bits, [down] + fixed))
            if far or bits:
                copy_of(slab, far, bits).start()

        guarded(here.exists(far), act)
    for _, slab, far, bits in events:
        if far or bits:
            guarded(
                here.exists(far),
                lambda at=(slab, far, bits): copy_of(*at).wait_send(),
            )


def scatter(groups, shapes, n, gap, collective_id):
    members = [len(group) for group in groups]
    slabs = []
    totals = [0] * len(groups)
    most = 0
    sizes = [(m * rows, columns) for m, (rows, columns) in zip(members, shapes)]
    for which, begin, rows, order, base in cut_slabs(sizes, gap):
        used = places(n, order)[1]
        slabs.append((which, begin, rows, order, base, totals[which]))
        totals[which] += rows * used
        most = max(most, used)
    size = sum(rows * columns for rows, columns in sizes) * 8 * n
    return pl.pallas_call(
        partial(scatter_kernel, n, slabs, members),
        out_shape=[jax.ShapeDtypeStruct(size, jnp.float32) for size in sizes],
        in_specs=[pl.BlockSpec(memory_space=pl.ANY)] * sum(members),
        out_specs=[pl.BlockSpec(memory_space=pltpu.VMEM)] * len(groups),
        scratch_shapes=[pltpu.VMEM((n, 4) + size, jnp.bfloat16) for size in sizes]
        + [pltpu.VMEM((total, size[1]), jnp.bfloat16) for size, total in zip(sizes, totals)]
        + [
            pltpu.SemaphoreType.DMA((len(slabs), 4 * n)),
            pltpu.SemaphoreType.DMA((len(slabs), most)),
            pltpu.SemaphoreType.DMA((4 * n * sum(members),)),
        ],
        compiler_params=pltpu.CompilerParams(
            collective_id=collective_id, has_side_effects=True, vmem_limit_bytes=58 * 2**20
        ),
        cost_estimate=pl.CostEstimate(flops=0, bytes_accessed=size * 16, transcendentals=0),
        name="scatter",
    )(*[matrix for group in groups for matrix in group])


class Row:
    def __init__(self, size):
        self.size = size
        self.parts = size // 4
        self.me = lax.axis_index("img") * self.parts + lax.axis_index("t")

    def other(self, step):
        return lax.rem(self.me + step, self.size)

    def device(self, index):
        return (lax.axis_index("dp"), index // self.parts, lax.rem(index, self.parts))


class Column:
    def __init__(self, size):
        self.size = size
        self.me = lax.axis_index("dp")

    def other(self, step):
        return lax.rem(self.me + step, self.size)

    def device(self, index):
        return (index, lax.axis_index("img"), lax.axis_index("t"))


def greet(*groups):
    barrier = pltpu.get_barrier_semaphore()
    for group in groups:
        for step in range(1, group.size):
            pl.semaphore_signal(
                barrier, inc=1, device_id=group.device(group.other(step)), device_id_type=MESH
            )
    pl.semaphore_wait(barrier, sum(group.size - 1 for group in groups))


def exchange(group, source, target, send_sem, recv_sem):
    def copy_of(step):
        index = group.other(step)
        return pltpu.make_async_remote_copy(
            src_ref=source(index),
            dst_ref=target(group.me),
            send_sem=send_sem.at[step],
            recv_sem=recv_sem.at[group.me],
            device_id=group.device(index),
            device_id_type=MESH,
        )

    for step in range(1, group.size):
        copy_of(step).start()
    for step in range(1, group.size):
        index = group.other(step)
        pltpu.make_async_remote_copy(
            src_ref=target(index),
            dst_ref=target(index),
            send_sem=send_sem.at[step],
            recv_sem=recv_sem.at[index],
            device_id=group.device(index),
            device_id_type=MESH,
        ).wait_recv()
    for step in range(1, group.size):
        copy_of(step).wait_send()


def row_block(ref, rows, index):
    return ref.at[pl.ds(pl.multiple_of(index * rows, 16), rows)]


def small_call(kernel, out_shape, scratch, operands, collective_id, name):
    vmem = pl.BlockSpec(memory_space=pltpu.VMEM)
    return pl.pallas_call(
        kernel,
        out_shape=out_shape,
        in_specs=[vmem] * len(operands),
        out_specs=vmem,
        scratch_shapes=scratch,
        compiler_params=pltpu.CompilerParams(
            collective_id=collective_id, has_side_effects=True
        ),
        cost_estimate=pl.CostEstimate(flops=0, bytes_accessed=2**24, transcendentals=0),
        name=name,
    )(*operands)


def semaphores(size):
    return [pltpu.SemaphoreType.DMA((size,)), pltpu.SemaphoreType.DMA((size,))]


def row_spread_kernel(size, mine, every, send_sem, recv_sem):
    row = Row(size)
    rows = mine.shape[0]
    greet(row)
    row_block(every, rows, row.me)[...] = mine[...]
    exchange(row, lambda _: mine, lambda index: row_block(every, rows, index), send_sem, recv_sem)


def row_spread(values):
    size = lax.axis_size("img") * lax.axis_size("t")
    return small_call(
        partial(row_spread_kernel, size),
        jax.ShapeDtypeStruct((size * values.shape[0], values.shape[1]), values.dtype),
        semaphores(size),
        [values],
        3,
        "row_spread",
    )


def row_sum(row, short, got, result, send_sem, recv_sem):
    rows = result.shape[0]
    row_block(got, rows, row.me)[...] = row_block(short, rows, row.me)[...]
    exchange(
        row,
        lambda index: row_block(short, rows, index),
        lambda index: row_block(got, rows, index),
        send_sem,
        recv_sem,
    )
    total = got[pl.ds(0, rows)].astype(jnp.float32)
    for index in range(1, row.size):
        total = total + got[pl.ds(index * rows, rows)].astype(jnp.float32)
    result[...] = total


def row_collect_kernel(size, values, result, short, got, send_sem, recv_sem):
    row = Row(size)
    short[...] = values[...].astype(jnp.bfloat16)
    greet(row)
    row_sum(row, short, got, result, send_sem, recv_sem)


def row_collect(values):
    size = lax.axis_size("img") * lax.axis_size("t")
    short = pltpu.VMEM(values.shape, jnp.bfloat16)
    return small_call(
        partial(row_collect_kernel, size),
        jax.ShapeDtypeStruct((values.shape[0] // size, values.shape[1]), jnp.float32),
        [short, short] + semaphores(size),
        [values],
        4,
        "row_collect",
    )


def text_in_kernel(n, size, picked, result, short, got, *sems):
    row, column = Row(size), Column(n)
    width = picked.shape[2]
    greet(row, column)

    def columns(index):
        return short.at[:, pl.ds(pl.multiple_of(index * width, 128), width)]

    columns(column.me)[...] = picked[column.me]
    exchange(column, lambda index: picked.at[index], columns, *sems[:2])
    row_sum(row, short, got, result, *sems[2:])


def text_in(picked):
    n, tokens, width = picked.shape
    size = lax.axis_size("img") * lax.axis_size("t")
    short = pltpu.VMEM((tokens, n * width), jnp.bfloat16)
    return small_call(
        partial(text_in_kernel, n, size),
        jax.ShapeDtypeStruct((tokens // size, n * width), jnp.float32),
        [short, short] + semaphores(n) + semaphores(size),
        [picked],
        5,
        "text_in",
    )


def text_back_kernel(n, size, mine, result, every, *sems):
    row, column = Row(size), Column(n)
    rows, width = mine.shape[0], result.shape[2]
    greet(row, column)
    row_block(every, rows, row.me)[...] = mine[...]
    exchange(row, lambda _: mine, lambda index: row_block(every, rows, index), *sems[:2])

    def columns(index):
        return every.at[:, pl.ds(pl.multiple_of(index * width, 128), width)]

    result[column.me] = columns(column.me)[...]
    exchange(column, columns, lambda index: result.at[index], *sems[2:])


def text_back(values):
    n = lax.axis_size("dp")
    size = lax.axis_size("img") * lax.axis_size("t")
    tokens = size * values.shape[0]
    width = values.shape[1] // n
    return small_call(
        partial(text_back_kernel, n, size),
        jax.ShapeDtypeStruct((n, tokens, width), values.dtype),
        [pltpu.VMEM((tokens, n * width), values.dtype)] + semaphores(size) + semaphores(n),
        [values],
        6,
        "text_back",
    )


def share_kernel(n, size, mine, every, *sems):
    row, column = Row(size), Column(n)
    greet(row, column)
    every[column.me, row.me] = mine[...]
    exchange(row, lambda _: mine, lambda index: every.at[column.me, index], *sems[:2])
    exchange(
        column, lambda _: every.at[column.me], lambda index: every.at[index], *sems[2:]
    )


def share(values):
    n = lax.axis_size("dp")
    size = lax.axis_size("img") * lax.axis_size("t")
    return small_call(
        partial(share_kernel, n, size),
        jax.ShapeDtypeStruct((n, size) + values.shape, values.dtype),
        semaphores(size) + semaphores(n),
        [values],
        7,
        "share",
    )


def total_kernel(n, size, mine, result, row_got, column_got, part, *sems):
    row, column = Row(size), Column(n)
    greet(row, column)
    row_got[row.me] = mine[...]
    exchange(row, lambda _: mine, lambda index: row_got.at[index], *sems[:2])
    added = row_got[0]
    for index in range(1, size):
        added = added + row_got[index]
    part[...] = added
    column_got[column.me] = added
    exchange(column, lambda _: part, lambda index: column_got.at[index], *sems[2:])
    added = column_got[0]
    for index in range(1, n):
        added = added + column_got[index]
    result[...] = added


def total_of(values):
    n = lax.axis_size("dp")
    size = lax.axis_size("img") * lax.axis_size("t")
    return small_call(
        partial(total_kernel, n, size),
        jax.ShapeDtypeStruct(values.shape, values.dtype),
        [
            pltpu.VMEM((size,) + values.shape, values.dtype),
            pltpu.VMEM((n,) + values.shape, values.dtype),
            pltpu.VMEM(values.shape, values.dtype),
        ]
        + semaphores(size)
        + semaphores(n),
        [values],
        8,
        "total",
    )


def rms_norm(values, gain):
    return values * lax.rsqrt(jnp.mean(values * values, axis=-1, keepdims=True) + EPS) * gain


def norm_back(values, gain, upstream):
    _, pull = jax.vjp(rms_norm, values, gain)
    return pull(upstream)


def gelu_exact(values):
    return jax.nn.gelu(values, approximate=False)


ROW = ("img", "t")


def spread(values, axis):
    if axis == "t" and lax.axis_size("t") == 2:
        other = lax.ppermute(values, "t", [(0, 1), (1, 0)])
        first = lax.axis_index("t") == 0
        return jnp.concatenate(
            [jnp.where(first, values, other), jnp.where(first, other, values)], axis=0
        )
    if axis == ROW:
        return row_spread(values)
    return lax.all_gather(values, axis, axis=0, tiled=True)


def collect(values, axis):
    if axis == "t" and lax.axis_size("t") == 2:
        half = values.shape[0] // 2
        place = lax.axis_index("t")
        away = lax.dynamic_slice_in_dim(values, (1 - place) * half, half, 0)
        came = lax.ppermute(away.astype(jnp.bfloat16), "t", [(0, 1), (1, 0)])
        return lax.dynamic_slice_in_dim(values, place * half, half, 0) + came.astype(jnp.float32)
    if axis == ROW:
        return row_collect(values)
    return lax.psum_scatter(
        values.astype(jnp.bfloat16), axis, scatter_dimension=0, tiled=True
    ).astype(jnp.float32)


def product(left, right, dims):
    return lax.dot_general(left, right, dims, preferred_element_type=jnp.float32)


def split_heads(values, groups):
    return values.reshape(groups, values.shape[0] // groups, values.shape[1] // HEAD_DIM, HEAD_DIM)


def core_forward(query, key, value, allowed, scale):
    scores = jnp.einsum("bqhe,bkhe->bhqk", query, key, preferred_element_type=jnp.float32) * scale
    scores = jnp.where(allowed[:, None], scores, NEGATIVE)
    highest = jnp.max(scores, axis=-1, keepdims=True)
    weight = jnp.exp(scores - highest)
    totals = jnp.sum(weight, axis=-1, keepdims=True)
    shares = (weight / totals).astype(jnp.bfloat16)
    mixed = jnp.einsum("bhqk,bkhe->bqhe", shares, value, preferred_element_type=jnp.float32)
    return (mixed.astype(jnp.bfloat16), highest + jnp.log(totals))


def core_backward(query, key, value, allowed, scale, partition, upstream):
    scores = jnp.einsum("bqhe,bkhe->bhqk", query, key, preferred_element_type=jnp.float32) * scale
    scores = jnp.where(allowed[:, None], scores, NEGATIVE)
    shares = jnp.exp(scores - partition)
    grad_value = jnp.einsum(
        "bhqk,bqhe->bkhe", shares.astype(jnp.bfloat16), upstream, preferred_element_type=jnp.float32
    )
    grad_shares = jnp.einsum("bqhe,bkhe->bhqk", upstream, value, preferred_element_type=jnp.float32)
    inner = jnp.sum(shares * grad_shares, axis=-1, keepdims=True)
    grad_scores = (shares * (grad_shares - inner)).astype(jnp.bfloat16)
    grad_query = (
        jnp.einsum("bhqk,bkhe->bqhe", grad_scores, key, preferred_element_type=jnp.float32) * scale
    )
    grad_key = (
        jnp.einsum("bhqk,bqhe->bkhe", grad_scores, query, preferred_element_type=jnp.float32)
        * scale
    )
    return (grad_query, grad_key, grad_value)


def causal_forward(parts, scale):
    query, key, value = parts
    length = query.shape[0]
    block = min(512, length)
    places = jnp.arange(length)
    outputs = []
    partitions = []
    for begin in range(0, length, block):
        allowed = begin + places[:block, None] >= places[None, :]
        mixed, partition = core_forward(
            query[None, begin : begin + block], key[None], value[None], allowed[None], scale
        )
        outputs.append(mixed[0])
        partitions.append(partition[0])
    return (jnp.concatenate(outputs, axis=0), jnp.concatenate(partitions, axis=1))


def causal_backward(parts, scale):
    query, key, value, partition, upstream = parts
    length = query.shape[0]
    block = min(512, length)
    places = jnp.arange(length)
    query_parts = []
    grad_key = jnp.zeros(key.shape, jnp.float32)
    grad_value = jnp.zeros(value.shape, jnp.float32)
    for begin in range(0, length, block):
        allowed = begin + places[:block, None] >= places[None, :]
        part_query, part_key, part_value = core_backward(
            query[None, begin : begin + block],
            key[None],
            value[None],
            allowed[None],
            scale,
            partition[None, :, begin : begin + block],
            upstream[None, begin : begin + block],
        )
        query_parts.append(part_query[0])
        grad_key = grad_key + part_key[0]
        grad_value = grad_value + part_value[0]
    return (jnp.concatenate(query_parts, axis=0), grad_key, grad_value)


def mix_forward(query, key, value, kind, context):
    scale = HEAD_DIM ** (-0.5)
    width = query.shape[1]
    query, key, value = (split_heads(part, 1) for part in (query, key, value))
    if kind == "self":
        mixed, partition = causal_forward((query[0], key[0], value[0]), scale)
        partition = partition[None]
    else:
        mixed, partition = core_forward(query, key, value, context["allowed"], scale)
    return (mixed.reshape(-1, width), partition)


def mix_backward(query, key, value, partition, upstream, kind, context):
    scale = HEAD_DIM ** (-0.5)
    width = query.shape[1]
    query, key, value, upstream = (split_heads(part, 1) for part in (query, key, value, upstream))
    if kind == "self":
        grads = causal_backward((query[0], key[0], value[0], partition[0], upstream[0]), scale)
    else:
        grads = core_backward(
            query, key, value, context["allowed"], scale, partition, upstream
        )
    return tuple(grad.reshape(-1, width).astype(jnp.bfloat16) for grad in grads)


def attention_forward(values, gain, weights, kind, axis, context, source=None):
    normed = rms_norm(values, gain).astype(jnp.bfloat16)
    inputs = spread(normed, axis)
    if source is None:
        source = inputs
    query = jnp.dot(inputs, weights[0], preferred_element_type=jnp.float32).astype(jnp.bfloat16)
    key = jnp.dot(source, weights[1], preferred_element_type=jnp.float32).astype(jnp.bfloat16)
    value = jnp.dot(source, weights[2], preferred_element_type=jnp.float32).astype(jnp.bfloat16)
    mixed, partition = mix_forward(query, key, value, kind, context)
    output = collect(product(mixed, weights[3], LAST), axis)
    return (output, (inputs, source, query, key, value, mixed, partition))


def attention_backward(upstream, values, gain, weights, kind, axis, context, kept):
    inputs, source, query, key, value, mixed, partition = kept
    grad_rows = spread(upstream.astype(jnp.bfloat16), axis)
    grad_out = product(grad_rows, mixed, FIRST)
    grad_mixed = jnp.dot(grad_rows, weights[3], preferred_element_type=jnp.float32).astype(
        jnp.bfloat16
    )
    grad_query, grad_key, grad_value = mix_backward(
        query, key, value, partition, grad_mixed, kind, context
    )
    grads = [
        product(inputs, grad_query, FIRST).astype(jnp.bfloat16),
        product(source, grad_key, FIRST).astype(jnp.bfloat16),
        product(source, grad_value, FIRST).astype(jnp.bfloat16),
        grad_out.astype(jnp.bfloat16),
    ]
    from_query = product(grad_query, weights[0], LAST)
    from_source = product(grad_key, weights[1], LAST) + product(grad_value, weights[2], LAST)
    if kind == "cross":
        grad_normed = collect(from_query, axis)
    else:
        grad_normed = collect(from_query + from_source, axis)
    grad_values, grad_gain = norm_back(values, gain, grad_normed)
    return (grad_values, grad_gain, grads, from_source)


def dense_forward(values, gain, weights, axis):
    normed = rms_norm(values, gain).astype(jnp.bfloat16)
    inputs = spread(normed, axis)
    hidden = jnp.dot(inputs, weights[0], preferred_element_type=jnp.float32)
    active = gelu_exact(hidden).astype(jnp.bfloat16)
    output = collect(product(active, weights[1], LAST), axis)
    return (output, (inputs, weights, hidden, active))


def dense_backward(upstream, values, gain, axis, kept):
    inputs, matrices, hidden, active = kept
    grad_rows = spread(upstream.astype(jnp.bfloat16), axis)
    grad_active = jnp.dot(grad_rows, matrices[1], preferred_element_type=jnp.float32)
    _, pull = jax.vjp(gelu_exact, hidden)
    grad_hidden = pull(grad_active)[0].astype(jnp.bfloat16)
    grads = [
        product(inputs, grad_hidden, FIRST).astype(jnp.bfloat16),
        product(grad_rows, active, FIRST).astype(jnp.bfloat16),
    ]
    grad_normed = collect(product(grad_hidden, matrices[0], LAST), axis)
    grad_values, grad_gain = norm_back(values, gain, grad_normed)
    return (grad_values, grad_gain, grads)


def code_hits(token_ids, usable, vocab):
    local = token_ids - lax.axis_index(ROW) * vocab
    places = jnp.arange(vocab, dtype=jnp.int32)
    return ((local[:, None] == places[None, :]) & usable[:, None]).astype(jnp.bfloat16)


def code_forward(token_ids, usable, table):
    hits = code_hits(token_ids, usable, table.shape[0])
    picked = jnp.dot(hits, table, preferred_element_type=jnp.float32).astype(jnp.bfloat16)
    return lax.psum_scatter(picked, ROW, scatter_dimension=0, tiled=True).astype(jnp.float32)


def code_backward(upstream, token_ids, usable, vocab):
    rows = lax.all_gather(upstream.astype(jnp.bfloat16), ROW, axis=0, tiled=True)
    return product(code_hits(token_ids, usable, vocab), rows, FIRST)


def merge_stats(first, second):
    highest = jnp.maximum(first[0], second[0])
    mass = first[1] * jnp.exp(first[0] - highest) + second[1] * jnp.exp(second[0] - highest)
    return (highest, mass, first[2] + second[2], first[3] + second[3])


def joined(stats):
    if lax.axis_size("t") == 2:
        other = lax.ppermute(jnp.stack(stats), "t", [(0, 1), (1, 0)])
        return merge_stats(stats, tuple(other))
    every = lax.all_gather(jnp.stack(stats), "t")
    state = tuple(every[0])
    for place in range(1, every.shape[0]):
        state = merge_stats(state, tuple(every[place]))
    return state


def matrices_of(gathered, n):
    count, rows, columns = gathered.shape
    if rows <= D:
        return gathered
    parts = gathered.reshape(count, n, 4, rows // n // 4, columns)
    return jnp.transpose(parts, (0, 1, 3, 2, 4)).reshape(count, rows // 4, 4 * columns)


def blocks_of(matrix, columns, n):
    if columns % 128 == 0:
        return matrix
    rows = matrix.shape[0]
    parts = matrix.reshape(n, rows // n, 4, columns)
    return jnp.transpose(parts, (0, 2, 1, 3)).reshape(4 * rows, columns)


def update(master, moment, average, gradient, factor, rate):
    clipped = gradient * factor
    moment_new = MOMENT * moment + clipped
    master_new = master - rate * (clipped + MOMENT * moment_new)
    average_new = DECAY * average + (1.0 - DECAY) * master_new
    return (master_new, moment_new, average_new, master_new.astype(jnp.bfloat16))


def per_device(
    code_ids,
    code_mask,
    caption_ids,
    caption_segments,
    image_row,
    attention_master,
    attention_momentum,
    attention_average,
    dense_master,
    dense_momentum,
    dense_average,
    text_master,
    text_momentum,
    text_average,
    code_master,
    code_momentum,
    code_average,
    gain_master,
    gain_momentum,
    gain_average,
):
    n = lax.axis_size("dp")
    z, image, part = lax.axis_index("dp"), lax.axis_index("img"), lax.axis_index("t")
    attention_shape = attention_master.shape[1:]
    dense_shape = dense_master.shape[1:]
    code_shape = code_master.shape[1:]
    images, length = code_ids.shape
    caption_rows, caption_length = caption_ids.shape
    text_rows, text_width = text_master.shape
    text_count = caption_ids.size
    mask = code_mask.astype(jnp.float32)
    gain_width = gain_master.shape[1]
    note = jnp.zeros((16, 128), jnp.float32)
    note = note.at[:7, :gain_width].set(gain_master)
    note = note.at[7, 0].set(jnp.sum(mask))
    note = note.at[8 : 8 + text_count // 128].set(
        caption_ids.astype(jnp.float32).reshape(-1, 128)
    )
    notes = share(note)
    gain_set = (
        jnp.transpose(notes[:, :, :7, :gain_width], (2, 0, 1, 3))
        .reshape(7, D)
    )
    gain_set = lax.reduce_precision(gain_set, exponent_bits=8, mantissa_bits=7)
    count = jnp.sum(notes[:, 0, 7, 0])
    all_text = notes[:, 0, 8 : 8 + text_count // 128].reshape(-1).astype(jnp.int32)
    encoder_attention, encoder_dense, code_table = (
        lax.all_gather(attention_master[0].astype(jnp.bfloat16), "dp", axis=1, tiled=True),
        lax.all_gather(dense_master[0].astype(jnp.bfloat16), "dp", axis=1, tiled=True),
        lax.all_gather(code_master[0].astype(jnp.bfloat16), "dp", axis=1, tiled=True),
    )
    self_weights, cross_weights, dense_weights = gather(
        [
            attention_master[1].astype(jnp.bfloat16),
            attention_master[2].astype(jnp.bfloat16),
            dense_master[1].astype(jnp.bfloat16),
        ],
        n,
        2.0,
        0,
    )
    self_weights, cross_weights, dense_weights = (
        matrices_of(weights, n) for weights in (self_weights, cross_weights, dense_weights)
    )
    out_part, self_weights = lax.optimization_barrier(
        (code_master[1].astype(jnp.bfloat16), self_weights)
    )
    out_table = lax.all_gather(
        lax.all_gather(out_part, "dp", axis=1, tiled=True), "img", axis=0, tiled=True
    )
    segments = caption_segments.reshape(-1)
    encoder_context = {"allowed": (segments[:, None] == segments[None, :])[None]}
    row = jnp.sum(jnp.where(jnp.arange(images) == image, image_row, 0)) - z * caption_rows
    owners = lax.dynamic_index_in_dim(caption_segments, row, 0, False)
    cross_context = {"allowed": (owners == z * images + image)[None, None, :]}
    text_local = all_text - lax.axis_index(ROW) * text_rows
    text_inside = (text_local >= 0) & (text_local < text_rows)
    picked = jnp.take(text_master, jnp.clip(text_local, 0, text_rows - 1), axis=0)
    picked = jnp.where(text_inside[:, None], picked, 0.0).astype(jnp.bfloat16)
    encoder_in = text_in(picked.reshape(n, text_count, text_width))
    branch, encoder_attention_keep = attention_forward(
        encoder_in, gain_set[0], encoder_attention, "encoder", ROW, encoder_context
    )
    encoder_mid = encoder_in + branch
    branch, encoder_dense_keep = dense_forward(encoder_mid, gain_set[1], encoder_dense, ROW)
    encoder_top = encoder_mid + branch
    encoded = spread(rms_norm(encoder_top, gain_set[2]).astype(jnp.bfloat16), ROW)
    caption = lax.dynamic_slice_in_dim(encoded, row * caption_length, caption_length, 0)
    previous = jnp.concatenate(
        [jnp.zeros((images, 1), jnp.int32), code_ids[:, :-1]], axis=1
    ).reshape(-1)
    starting = jnp.broadcast_to(jnp.arange(length) > 0, (images, length)).reshape(-1)
    code_table, encoder_in = lax.optimization_barrier((code_table, encoder_in))
    decoder_in = code_forward(previous, starting, code_table)
    branch, self_keep = attention_forward(
        decoder_in, gain_set[3], self_weights, "self", "t", None
    )
    decoder_one = decoder_in + branch
    branch, cross_keep = attention_forward(
        decoder_one, gain_set[4], cross_weights, "cross", "t", cross_context, caption
    )
    decoder_two = decoder_one + branch
    branch, decoder_dense_keep = dense_forward(decoder_two, gain_set[5], dense_weights, "t")
    decoder_top = decoder_two + branch
    final = spread(rms_norm(decoder_top, gain_set[6]).astype(jnp.bfloat16), "t")
    logits = product(final, out_table, LAST)
    rows = code_shape[0]
    codes = lax.dynamic_index_in_dim(code_ids, image, 0, False)
    held = codes // rows
    local_target = jnp.where(
        held % lax.axis_size("t") == part, held // lax.axis_size("t") * rows + codes % rows, -1
    )
    hits = jnp.arange(logits.shape[1], dtype=jnp.int32)[None, :] == local_target[:, None]
    highest = jnp.max(logits, axis=-1)
    highest, mass, target_logit, logit_total = joined(
        (
            highest,
            jnp.sum(jnp.exp(logits - highest[:, None]), axis=-1),
            jnp.sum(jnp.where(hits, logits, 0.0), axis=-1),
            jnp.sum(logits, axis=-1),
        )
    )
    partition = highest + jnp.log(mass)
    valid = lax.dynamic_index_in_dim(mask, image, 0, False)
    per_token = (
        partition
        - (1.0 - SMOOTH) * target_logit
        - SMOOTH * logit_total / VC
        + Z_WEIGHT * partition * partition
    )
    per_image = lax.all_gather(per_token, "img")
    loss_part = jnp.sum(per_token * valid) / lax.axis_size("t")
    weighting = valid / count
    grad_logits = weighting[:, None] * (
        (1.0 + 2.0 * Z_WEIGHT * partition)[:, None] * jnp.exp(logits - partition[:, None])
        - (1.0 - SMOOTH) * hits.astype(jnp.float32)
        - SMOOTH / VC
    )
    grad_logits = grad_logits.astype(jnp.bfloat16)
    grad_out_table = product(grad_logits, final, FIRST).astype(jnp.bfloat16)
    out_grads = lax.psum_scatter(
        lax.psum_scatter(grad_out_table, "img", scatter_dimension=0, tiled=True),
        "dp",
        scatter_dimension=1,
        tiled=True,
    ).astype(jnp.float32)
    grad_final = collect(
        jnp.dot(grad_logits, out_table, preferred_element_type=jnp.float32), "t"
    )
    grad_top, gain_six = norm_back(decoder_top, gain_set[6], grad_final)
    grad_branch, gain_five, dense_one = dense_backward(
        grad_top, decoder_two, gain_set[5], "t", decoder_dense_keep
    )
    grad_two = grad_top + grad_branch
    grad_branch, gain_four, attention_two, grad_caption = attention_backward(
        grad_two, decoder_one, gain_set[4], cross_weights, "cross", "t", cross_context, cross_keep
    )
    grad_one = grad_two + grad_branch
    grad_branch, gain_three, attention_one, _ = attention_backward(
        grad_one, decoder_in, gain_set[3], self_weights, "self", "t", None, self_keep
    )
    grad_start = grad_one + grad_branch
    narrow = attention_shape[2]
    one_grads, two_grads, dense_one_grads = scatter(
        [
            [blocks_of(matrix, narrow, n) for matrix in attention_one],
            [blocks_of(matrix, narrow, n) for matrix in attention_two],
            dense_one,
        ],
        [attention_shape[1:], attention_shape[1:], dense_shape[1:]],
        n,
        2.0,
        2,
    )
    grad_code_in = code_backward(grad_start, previous, starting, code_shape[0])
    grad_encoded = collect(
        lax.dynamic_update_slice_in_dim(
            jnp.zeros(encoded.shape, jnp.float32), grad_caption, row * caption_length, 0
        ),
        ROW,
    )
    grad_encoder_top, gain_two = norm_back(encoder_top, gain_set[2], grad_encoded)
    grad_branch, gain_one, dense_zero = dense_backward(
        grad_encoder_top, encoder_mid, gain_set[1], ROW, encoder_dense_keep
    )
    grad_encoder_mid = grad_encoder_top + grad_branch
    grad_branch, gain_zero, attention_zero, _ = attention_backward(
        grad_encoder_mid,
        encoder_in,
        gain_set[0],
        encoder_attention,
        "encoder",
        ROW,
        encoder_context,
        encoder_attention_keep,
    )
    text_rows_back = text_back((grad_encoder_mid + grad_branch).astype(jnp.bfloat16))
    text_hits = jnp.arange(text_rows, dtype=jnp.int32)[:, None] == text_local[None, :]
    text_grads = jnp.dot(
        text_hits.astype(jnp.bfloat16),
        text_rows_back.reshape(-1, text_width),
        preferred_element_type=jnp.float32,
    )

    def owned(values, axis):
        return lax.psum_scatter(
            values.astype(jnp.bfloat16), "dp", scatter_dimension=axis, tiled=True
        ).astype(jnp.float32)

    attention_grads = jnp.stack(
        [
            owned(jnp.stack(attention_zero), 1),
            one_grads.reshape(attention_shape),
            two_grads.reshape(attention_shape),
        ]
    )
    dense_grads = jnp.stack([owned(jnp.stack(dense_zero), 1), dense_one_grads.reshape(dense_shape)])
    code_grads = jnp.stack([owned(grad_code_in, 1), out_grads.reshape(code_shape)])
    squares = (
        jnp.sum(attention_grads * attention_grads)
        + jnp.sum(dense_grads * dense_grads)
        + jnp.sum(text_grads * text_grads)
        + jnp.sum(code_grads * code_grads)
    )
    sums = jnp.stack([gain_zero, gain_one, gain_two, gain_three, gain_four, gain_five, gain_six])
    tail = jnp.zeros((1, D), jnp.float32).at[0, 0].set(squares).at[0, 1].set(loss_part)
    sums = total_of(jnp.concatenate([sums, tail], axis=0))
    gain_sums = sums[:7]
    loss = sums[7, 1] / count
    norm = jnp.sqrt(sums[7, 0] + jnp.sum(gain_sums * gain_sums))
    gain_grads = lax.dynamic_slice_in_dim(
        gain_sums, lax.axis_index(("dp",) + ROW) * gain_width, gain_width, 1
    )
    factor = jnp.minimum(1.0, CLIP / norm)
    rate = 0.012 * math.sqrt(12 * D * D + 4 * D * FF + VT * D + 2 * VC * D + 7 * D) / CLIP
    attention_out = update(
        attention_master, attention_momentum, attention_average, attention_grads, factor, rate
    )
    dense_out = update(dense_master, dense_momentum, dense_average, dense_grads, factor, rate)
    text_out = update(text_master, text_momentum, text_average, text_grads, factor, rate)
    code_out = update(code_master, code_momentum, code_average, code_grads, factor, rate)
    gain_out = update(gain_master, gain_momentum, gain_average, gain_grads, factor, rate)
    return (
        loss,
        norm,
        attention_out[0],
        attention_out[1],
        attention_out[2],
        attention_out[3],
        dense_out[0],
        dense_out[1],
        dense_out[2],
        dense_out[3],
        text_out[0],
        text_out[1],
        text_out[2],
        text_out[3],
        code_out[0],
        code_out[1],
        code_out[2],
        code_out[3],
        gain_out[0],
        gain_out[1],
        gain_out[2],
        gain_out[3],
        per_image,
    )


def solution(mesh):
    n, m = mesh.shape["dp"], mesh.shape["mp"]
    view = Mesh(mesh.devices.reshape(n, 4, m // 4), ("dp",) + ROW)
    return jax.shard_map(
        per_device,
        mesh=view,
        in_specs=(
            P("dp", None),
            P("dp", None),
            P("dp", None),
            P("dp", None),
            P("dp"),
            P(None, None, "dp", ROW),
            P(None, None, "dp", ROW),
            P(None, None, "dp", ROW),
            P(None, None, "dp", ROW),
            P(None, None, "dp", ROW),
            P(None, None, "dp", ROW),
            P(ROW, "dp"),
            P(ROW, "dp"),
            P(ROW, "dp"),
            P(None, ROW, "dp"),
            P(None, ROW, "dp"),
            P(None, ROW, "dp"),
            P(None, ("dp",) + ROW),
            P(None, ("dp",) + ROW),
            P(None, ("dp",) + ROW),
        ),
        out_specs=(
            P(),
            P(),
            P(None, None, "dp", ROW),
            P(None, None, "dp", ROW),
            P(None, None, "dp", ROW),
            P(None, None, "dp", ROW),
            P(None, None, "dp", ROW),
            P(None, None, "dp", ROW),
            P(None, None, "dp", ROW),
            P(None, None, "dp", ROW),
            P(ROW, "dp"),
            P(ROW, "dp"),
            P(ROW, "dp"),
            P(ROW, "dp"),
            P(None, ROW, "dp"),
            P(None, ROW, "dp"),
            P(None, ROW, "dp"),
            P(None, ROW, "dp"),
            P(None, ("dp",) + ROW),
            P(None, ("dp",) + ROW),
            P(None, ("dp",) + ROW),
            P(None, ("dp",) + ROW),
            P("dp", None),
        ),
        check_vma=False,
    )
```

```python
from functools import partial
import math

import jax
import jax.numpy as jnp
from jax import lax
from jax.experimental import pallas as pl
from jax.experimental.pallas import tpu as pltpu
from jax.sharding import Mesh, PartitionSpec as P

D = 1024
HEAD_DIM = 64
FF = 4096
VC = 8192
VT = 16000


EPS = 1e-06
CLIP = 0.01
MOMENT = 0.9
DECAY = 0.75
SMOOTH = 0.1
Z_WEIGHT = 0.01
NEGATIVE = -1e30
LAST = (((1,), (1,)), ((), ()))
FIRST = (((0,), (0,)), ((), ()))


MESH = pl.DeviceIdType.MESH
ORDERS = ((0, 1, 2), (0, 2, 1), (1, 0, 2), (2, 0, 1))


def sources(n):
    return [(far, bits) for far in range(1 - n, n) for bits in range(4)]


def hops(far, bits):
    return abs(far) + (bits & 1) + (bits >> 1)


def arrival(order, far, bits):
    last = None
    for dim in order:
        if (dim == 0 and far != 0) or (dim > 0 and bits & dim):
            last = dim
    return last


def passes(order, far, bits):
    came = arrival(order, far, bits)
    place = -1 if came is None else order.index(came)
    found = [(0, -1 if far > 0 else 1)] if came == 0 else []
    for dim in order[place + 1 :]:
        found += [(0, 1), (0, -1)] if dim == 0 else [(dim, 0)]
    return found


def cut_slabs(shapes, gap):
    slabs = []
    base = 0.0
    for which, (rows, _) in enumerate(shapes):
        small = max(16, rows // 6 // 16 * 16)
        large = (rows - 2 * small) // 2 // 16 * 16
        begin = 0
        for order, count in zip(ORDERS, (small, small, large, rows - 2 * small - large)):
            slabs.append((which, begin, count, order, base))
            begin += count
        base += gap
    return slabs


def wide(shape, n):
    _, rows, columns = shape
    return (n * rows, 4 * columns) if columns % 128 == 0 else (4 * n * rows, columns)


def placed(whole, shape, z, i, begin, rows):
    if shape[2] % 128 == 0:
        return whole.at[
            :,
            pl.ds(pl.multiple_of(z * shape[1] + begin, 16), rows),
            pl.ds(pl.multiple_of(i * shape[2], 128), shape[2]),
        ]
    return whole.at[:, pl.ds(pl.multiple_of((z * 4 + i) * shape[1] + begin, 16), rows)]


class Here:
    def __init__(self, n):
        self.n = n
        self.z = lax.axis_index("dp")
        self.i = lax.axis_index("img")
        self.t = lax.axis_index("t")

    def device(self, dim, step):
        if dim == 0:
            return (self.z + step, self.i, self.t)
        return (self.z, jnp.bitwise_xor(self.i, dim), self.t)

    def below(self):
        return self.z > 0

    def above(self):
        return self.z < self.n - 1

    def side(self, step):
        return self.above() if step > 0 else self.below()

    def greet(self):
        barrier = pltpu.get_barrier_semaphore()

        def tell(device):
            pl.semaphore_signal(barrier, inc=1, device_id=device, device_id_type=MESH)

        pl.when(self.below())(lambda: tell(self.device(0, -1)))
        pl.when(self.above())(lambda: tell(self.device(0, 1)))
        tell(self.device(1, 0))
        tell(self.device(2, 0))
        pl.semaphore_wait(
            barrier, 2 + jnp.where(self.below(), 1, 0) + jnp.where(self.above(), 1, 0)
        )

    def exists(self, far):
        if far == 0:
            return None
        return (self.z + far >= 0) if far < 0 else (self.z + far < self.n)


def guarded(condition, action):
    if condition is None:
        action()
    else:
        pl.when(condition)(action)


def both(first, second):
    if first is None or second is None:
        return second if first is None else first
    return jnp.logical_and(first, second)


def gather_kernel(n, slabs, count, *refs):
    ins, outs = refs[:count], refs[count : 2 * count]
    send_sem, recv_sem, local_sem = refs[2 * count :]
    here = Here(n)
    here.greet()
    local = []
    for which in range(count):
        shape = ins[which].shape
        copy = pltpu.make_async_copy(
            ins[which], placed(outs[which], shape, here.z, here.i, 0, shape[1]), local_sem.at[which]
        )
        copy.start()
        local.append(copy)

    def block(slab, far, bits):
        which, begin, rows = slabs[slab][:3]
        return placed(
            outs[which], ins[which].shape, here.z + far, jnp.bitwise_xor(here.i, bits), begin, rows
        )

    def name(far, bits):
        return (here.z + far) * 4 + jnp.bitwise_xor(here.i, bits)

    def copy_of(slab, far, bits, dim, step):
        which, begin, rows = slabs[slab][:3]
        target = block(slab, far, bits)
        own = far == 0 and bits == 0
        return pltpu.make_async_remote_copy(
            src_ref=ins[which].at[:, pl.ds(begin, rows)] if own else target,
            dst_ref=target,
            send_sem=send_sem.at[slab, name(far, bits), (1 + step) // 2 if dim == 0 else 1 + dim],
            recv_sem=recv_sem.at[slab, name(far, bits)],
            device_id=here.device(dim, step),
            device_id_type=MESH,
        )

    def arrive(slab, far, bits):
        target = block(slab, far, bits)
        pltpu.make_async_remote_copy(
            src_ref=target,
            dst_ref=target,
            send_sem=send_sem.at[slab, 0, 0],
            recv_sem=recv_sem.at[slab, name(far, bits)],
            device_id=here.device(1, 0),
            device_id_type=MESH,
        ).wait_recv()

    events = sorted(
        (slabs[slab][4] + hops(far, bits), slab, far, bits)
        for slab in range(len(slabs))
        for far, bits in sources(n)
    )
    sent = []
    final = []
    for _, slab, far, bits in events:
        onward = passes(slabs[slab][3], far, bits)
        own = far == 0 and bits == 0
        if not onward:
            final.append((slab, far, bits))
            continue

        def act(slab=slab, far=far, bits=bits, onward=onward, own=own):
            if not own:
                arrive(slab, far, bits)
            for dim, step in onward:
                guarded(
                    here.side(step) if dim == 0 else None,
                    lambda dim=dim, step=step: copy_of(slab, far, bits, dim, step).start(),
                )

        guarded(here.exists(far), act)
        sent += [(slab, far, bits, dim, step) for dim, step in onward]
    for slab, far, bits in final:
        guarded(here.exists(far), lambda at=(slab, far, bits): arrive(*at))
    for slab, far, bits, dim, step in sent:
        guarded(
            both(here.exists(far), here.side(step) if dim == 0 else None),
            lambda at=(slab, far, bits, dim, step): copy_of(*at).wait_send(),
        )
    for copy in local:
        copy.wait()


def gather(arrays, n, gap, collective_id):
    count = len(arrays)
    slabs = cut_slabs([a.shape[1:] for a in arrays], gap)
    size = sum(a.size * a.dtype.itemsize for a in arrays) * 4 * n
    return pl.pallas_call(
        partial(gather_kernel, n, slabs, count),
        out_shape=[
            jax.ShapeDtypeStruct((a.shape[0],) + wide(a.shape, n), a.dtype) for a in arrays
        ],
        in_specs=[pl.BlockSpec(memory_space=pl.ANY)] * count,
        out_specs=[pl.BlockSpec(memory_space=pl.ANY)] * count,
        scratch_shapes=[
            pltpu.SemaphoreType.DMA((len(slabs), 4 * n, 4)),
            pltpu.SemaphoreType.DMA((len(slabs), 4 * n)),
            pltpu.SemaphoreType.DMA((count,)),
        ],
        compiler_params=pltpu.CompilerParams(
            collective_id=collective_id, has_side_effects=True
        ),
        cost_estimate=pl.CostEstimate(flops=0, bytes_accessed=size * 16, transcendentals=0),
        name="gather",
    )(*arrays)


def places(n, order):
    table = {}
    used = 0
    line = [b for b in range(4) if any(dim == 0 for dim, _ in passes(order, 0, b))]
    for rank, bits in enumerate(line):
        for far in range(1 - n, n):
            for dim, step in passes(order, far, bits):
                if dim == 0:
                    second = far == 0 and step < 0
                    table[far, bits, dim, step] = (
                        (used + n, False) if second else (used + far, True)
                    )
        used += n + 1
    for flip in (1, 2):
        pairs = [p for p in sources(n) if (flip, 0) in passes(order, *p)]
        spread = any(far for far, _ in pairs)
        for bits in sorted({b for _, b in pairs}):
            for far, other in pairs:
                if other == bits:
                    table[far, bits, flip, 0] = (used + far, True) if spread else (used, False)
            used += n if spread else 1
    return table, used


def scatter_kernel(n, slabs, members, *refs):
    total = sum(members)
    count = len(members)
    ins, refs = refs[:total], refs[total:]
    outs, owns, gots = refs[:count], refs[count : 2 * count], refs[2 * count : 3 * count]
    send_sem, recv_sem, local_sem = refs[3 * count :]
    here = Here(n)
    tables = {order: places(n, order)[0] for order in ORDERS}
    loads = []
    for which in range(count):
        for member in range(members[which]):
            matrix = ins[sum(members[:which]) + member]
            rows = owns[which].shape[2] // members[which]
            columns = owns[which].shape[3]
            for z in range(n):
                for i in range(4):
                    copy = pltpu.make_async_copy(
                        matrix.at[pl.ds(z * rows, rows), pl.ds(i * columns, columns)]
                        if matrix.shape[0] == n * rows
                        else matrix.at[pl.ds((z * 4 + i) * rows, rows)],
                        owns[which].at[z, i, pl.ds(member * rows, rows)],
                        local_sem.at[len(loads)],
                    )
                    copy.start()
                    loads.append(copy)
    here.greet()
    for copy in loads:
        copy.wait()

    def own(slab, far, bits):
        which, begin, rows = slabs[slab][:3]
        return owns[which].at[
            here.z + far, jnp.bitwise_xor(here.i, bits), pl.ds(begin, rows)
        ]

    def slot(slab, number):
        which, _, rows, _, _, first = slabs[slab]
        return gots[which].at[pl.ds(pl.multiple_of(first + number * rows, 16), rows)]

    def number_at(order, z, key):
        constant, counts = tables[order][key]
        return constant + z if counts else constant

    def copy_of(slab, far, bits):
        order = slabs[slab][3]
        dim = arrival(order, far, bits)
        step = 0 if dim else (1 if far > 0 else -1)
        number = number_at(order, here.z + step, (far - step, bits ^ dim, dim, -step))
        return pltpu.make_async_remote_copy(
            src_ref=own(slab, far, bits),
            dst_ref=slot(slab, number),
            send_sem=send_sem.at[slab, (here.z + far) * 4 + bits],
            recv_sem=recv_sem.at[slab, number],
            device_id=here.device(dim, step),
            device_id_type=MESH,
        )

    events = sorted(
        (slabs[slab][4] + n + 1 - hops(far, bits), slab, far, bits)
        for slab in range(len(slabs))
        for far, bits in sources(n)
    )

    def add_up(slab, far, bits, parts):
        which, begin, rows, order = slabs[slab][:4]
        numbers = [number_at(order, here.z, (far, bits) + part) for part in parts]
        for number in numbers:
            landed = slot(slab, number)
            pltpu.make_async_remote_copy(
                src_ref=landed,
                dst_ref=landed,
                send_sem=send_sem.at[slab, 0],
                recv_sem=recv_sem.at[slab, number],
                device_id=here.device(1, 0),
                device_id_type=MESH,
            ).wait_recv()
        root = far == 0 and bits == 0
        if not parts and not root:
            return
        mine = own(slab, far, bits)
        landed = [slot(slab, number) for number in numbers]

        @pl.loop(0, rows // 16)
        def _(row):
            at = pl.ds(pl.multiple_of(row * 16, 16), 16)
            added = mine[at].astype(jnp.float32)
            for part in landed:
                added = added + part[at].astype(jnp.float32)
            if root:
                outs[which][pl.ds(pl.multiple_of(begin + row * 16, 16), 16)] = added
            else:
                mine[at] = added.astype(jnp.bfloat16)

    for _, slab, far, bits in events:

        def act(slab=slab, far=far, bits=bits):
            parts = passes(slabs[slab][3], far, bits)
            fixed = [p for p in parts if p[0]]
            line = [p for p in parts if not p[0]]
            if not line:
                add_up(slab, far, bits, fixed)
            elif len(line) == 1:
                there = here.side(line[0][1])
                pl.when(there)(lambda: add_up(slab, far, bits, line + fixed))
                pl.when(jnp.logical_not(there))(lambda: add_up(slab, far, bits, fixed))
            else:
                low, high = here.below(), here.above()
                up, down = line
                pl.when(jnp.logical_and(low, high))(
                    lambda: add_up(slab, far, bits, line + fixed)
                )
                pl.when(jnp.logical_not(low))(lambda: add_up(slab, far, bits, [up] + fixed))
                pl.when(jnp.logical_not(high))(lambda: add_up(slab, far, bits, [down] + fixed))
            if far or bits:
                copy_of(slab, far, bits).start()

        guarded(here.exists(far), act)
    for _, slab, far, bits in events:
        if far or bits:
            guarded(
                here.exists(far),
                lambda at=(slab, far, bits): copy_of(*at).wait_send(),
            )


def scatter(groups, shapes, n, gap, collective_id):
    members = [len(group) for group in groups]
    slabs = []
    totals = [0] * len(groups)
    most = 0
    sizes = [(m * rows, columns) for m, (rows, columns) in zip(members, shapes)]
    for which, begin, rows, order, base in cut_slabs(sizes, gap):
        used = places(n, order)[1]
        slabs.append((which, begin, rows, order, base, totals[which]))
        totals[which] += rows * used
        most = max(most, used)
    size = sum(rows * columns for rows, columns in sizes) * 8 * n
    return pl.pallas_call(
        partial(scatter_kernel, n, slabs, members),
        out_shape=[jax.ShapeDtypeStruct(size, jnp.float32) for size in sizes],
        in_specs=[pl.BlockSpec(memory_space=pl.ANY)] * sum(members),
        out_specs=[pl.BlockSpec(memory_space=pltpu.VMEM)] * len(groups),
        scratch_shapes=[pltpu.VMEM((n, 4) + size, jnp.bfloat16) for size in sizes]
        + [pltpu.VMEM((total, size[1]), jnp.bfloat16) for size, total in zip(sizes, totals)]
        + [
            pltpu.SemaphoreType.DMA((len(slabs), 4 * n)),
            pltpu.SemaphoreType.DMA((len(slabs), most)),
            pltpu.SemaphoreType.DMA((4 * n * sum(members),)),
        ],
        compiler_params=pltpu.CompilerParams(
            collective_id=collective_id, has_side_effects=True, vmem_limit_bytes=58 * 2**20
        ),
        cost_estimate=pl.CostEstimate(flops=0, bytes_accessed=size * 16, transcendentals=0),
        name="scatter",
    )(*[matrix for group in groups for matrix in group])


class Row:
    def __init__(self, size):
        self.size = size
        self.parts = size // 4
        self.me = lax.axis_index("img") * self.parts + lax.axis_index("t")

    def other(self, step):
        return lax.rem(self.me + step, self.size)

    def device(self, index):
        return (lax.axis_index("dp"), index // self.parts, lax.rem(index, self.parts))


class Column:
    def __init__(self, size):
        self.size = size
        self.me = lax.axis_index("dp")

    def other(self, step):
        return lax.rem(self.me + step, self.size)

    def device(self, index):
        return (index, lax.axis_index("img"), lax.axis_index("t"))


def greet(*groups):
    barrier = pltpu.get_barrier_semaphore()
    for group in groups:
        for step in range(1, group.size):
            pl.semaphore_signal(
                barrier, inc=1, device_id=group.device(group.other(step)), device_id_type=MESH
            )
    pl.semaphore_wait(barrier, sum(group.size - 1 for group in groups))


class Exchange:
    def __init__(self, group, source, target, send_sem, recv_sem):
        self.group, self.source, self.target = group, source, target
        self.send_sem, self.recv_sem = send_sem, recv_sem

    def copy_of(self, step):
        index = self.group.other(step)
        return pltpu.make_async_remote_copy(
            src_ref=self.source(index),
            dst_ref=self.target(self.group.me),
            send_sem=self.send_sem.at[step],
            recv_sem=self.recv_sem.at[self.group.me],
            device_id=self.group.device(index),
            device_id_type=MESH,
        )

    def start(self):
        for step in range(1, self.group.size):
            self.copy_of(step).start()
        return self

    def finish(self):
        for step in range(1, self.group.size):
            index = self.group.other(step)
            pltpu.make_async_remote_copy(
                src_ref=self.target(index),
                dst_ref=self.target(index),
                send_sem=self.send_sem.at[step],
                recv_sem=self.recv_sem.at[index],
                device_id=self.group.device(index),
                device_id_type=MESH,
            ).wait_recv()
        for step in range(1, self.group.size):
            self.copy_of(step).wait_send()


def exchange(*parts):
    Exchange(*parts).start().finish()


def row_block(ref, rows, index):
    return ref.at[pl.ds(pl.multiple_of(index * rows, 16), rows)]


def small_call(kernel, out_shape, scratch, operands, collective_id, name):
    vmem = pl.BlockSpec(memory_space=pltpu.VMEM)
    return pl.pallas_call(
        kernel,
        out_shape=out_shape,
        in_specs=[vmem] * len(operands),
        out_specs=vmem,
        scratch_shapes=scratch,
        compiler_params=pltpu.CompilerParams(
            collective_id=collective_id, has_side_effects=True
        ),
        cost_estimate=pl.CostEstimate(flops=0, bytes_accessed=2**24, transcendentals=0),
        name=name,
    )(*operands)


def semaphores(size):
    return [pltpu.SemaphoreType.DMA((size,)), pltpu.SemaphoreType.DMA((size,))]


class RowSpread:
    def __init__(self, row, mine, every, *sems):
        self.mine, self.every, self.rows, self.me = mine, every, mine.shape[0], row.me
        self.work = Exchange(row, lambda _: mine, self.block, *sems)

    def block(self, index):
        return row_block(self.every, self.rows, index)

    def start(self, values):
        self.mine[...] = values
        self.block(self.me)[...] = values
        self.work.start()

    def finish(self):
        self.work.finish()
        return self.every[...]


class RowSum:
    def __init__(self, row, short, got, rows, *sems):
        self.short, self.got, self.rows, self.row = short, got, rows, row
        self.work = Exchange(
            row,
            lambda index: row_block(short, rows, index),
            lambda index: row_block(got, rows, index),
            *sems,
        )

    def start(self, values=None):
        if values is not None:
            self.short[...] = values.astype(jnp.bfloat16)
        mine = row_block(self.short, self.rows, self.row.me)
        row_block(self.got, self.rows, self.row.me)[...] = mine[...]
        self.work.start()

    def finish(self):
        self.work.finish()
        total = self.got[pl.ds(0, self.rows)].astype(jnp.float32)
        for index in range(1, self.row.size):
            total = total + self.got[pl.ds(index * self.rows, self.rows)].astype(jnp.float32)
        return total


def head_lanes(width):
    lanes = lax.broadcasted_iota(jnp.int32, (1, width), 1) // HEAD_DIM
    return [lanes == head for head in range(width // HEAD_DIM)]


def only(lanes, values):
    return jnp.where(lanes, values, jnp.zeros_like(values))


def full_shares(query, key, allowed, lanes):
    scores = product(only(lanes, query), key, LAST) * HEAD_DIM ** (-0.5)
    scores = jnp.where(allowed > 0, scores, NEGATIVE)
    weight = jnp.exp(scores - jnp.max(scores, axis=-1, keepdims=True))
    return weight / jnp.sum(weight, axis=-1, keepdims=True)


def encoder_kernel(
    n, size, picked, gains, attention, dense, allowed,
    encoded, first, middle, top, inputs, query, key, value, mixed, dense_in, hidden, active,
    short, mine, got_text, got_mixed, got_dense, *sems,
):
    row, column = Row(size), Column(n)
    rows, width = first.shape[0], picked.shape[2]
    greet(row, column)

    def columns(index):
        return short.at[:, pl.ds(pl.multiple_of(index * width, 128), width)]

    columns(column.me)[...] = picked[column.me]
    exchange(column, lambda index: picked.at[index], columns, *sems[:2])
    text = RowSum(row, short, got_text, rows, *sems[2:4])
    text.start()
    values = text.finish()
    first[...] = values
    spread_one = RowSpread(row, mine, inputs, *sems[4:6])
    spread_one.start(rms_norm(values, gains[0:1]).astype(jnp.bfloat16))
    every = spread_one.finish()
    query[...] = jnp.dot(
        every, attention[0], preferred_element_type=jnp.float32
    ).astype(jnp.bfloat16)
    key[...] = jnp.dot(every, attention[1], preferred_element_type=jnp.float32).astype(jnp.bfloat16)
    value[...] = jnp.dot(
        every, attention[2], preferred_element_type=jnp.float32
    ).astype(jnp.bfloat16)
    out = jnp.zeros(query.shape, jnp.float32)
    for lanes in head_lanes(query.shape[1]):
        shares = full_shares(query[...], key[...], allowed[...], lanes).astype(jnp.bfloat16)
        out = out + jnp.dot(shares, only(lanes, value[...]), preferred_element_type=jnp.float32)
    mixed[...] = out.astype(jnp.bfloat16)
    branch = RowSum(row, short, got_mixed, rows, *sems[6:8])
    branch.start(product(mixed[...], attention[3], LAST))
    values = values + branch.finish()
    middle[...] = values
    spread_two = RowSpread(row, mine, dense_in, *sems[8:10])
    spread_two.start(rms_norm(values, gains[1:2]).astype(jnp.bfloat16))
    every = spread_two.finish()
    hidden[...] = jnp.dot(every, dense[0], preferred_element_type=jnp.float32)
    inner = hidden[...]
    active[...] = (0.5 * inner * (1.0 + lax.erf(inner * math.sqrt(0.5)))).astype(jnp.bfloat16)
    branch = RowSum(row, short, got_dense, rows, *sems[10:12])
    branch.start(product(active[...], dense[1], LAST))
    values = values + branch.finish()
    top[...] = values
    spread_three = RowSpread(row, mine, encoded, *sems[12:14])
    spread_three.start(rms_norm(values, gains[2:3]).astype(jnp.bfloat16))
    spread_three.finish()


def encoder_call(kernel, out_shape, scratch, operands, collective_id, name):
    vmem = pl.BlockSpec(memory_space=pltpu.VMEM)
    return pl.pallas_call(
        kernel,
        out_shape=out_shape,
        in_specs=[vmem] * len(operands),
        out_specs=[vmem] * len(out_shape),
        scratch_shapes=scratch,
        compiler_params=pltpu.CompilerParams(
            collective_id=collective_id, has_side_effects=True, vmem_limit_bytes=48 * 2**20
        ),
        cost_estimate=pl.CostEstimate(flops=0, bytes_accessed=2**27, transcendentals=0),
        name=name,
    )(*operands)


def encoder_forward(picked, gains, attention, dense, allowed):
    n, tokens, _ = picked.shape
    size = lax.axis_size("img") * lax.axis_size("t")
    width, inner = attention.shape[2], dense.shape[2]
    own = jax.ShapeDtypeStruct((tokens // size, D), jnp.float32)
    every = jax.ShapeDtypeStruct((tokens, D), jnp.bfloat16)
    head = jax.ShapeDtypeStruct((tokens, width), jnp.bfloat16)
    wide_out = [jax.ShapeDtypeStruct((tokens, inner), kind) for kind in (jnp.float32, jnp.bfloat16)]
    whole = pltpu.VMEM((tokens, D), jnp.bfloat16)
    outs = encoder_call(
        partial(encoder_kernel, n, size),
        [every, own, own, own, every, head, head, head, head, every] + wide_out,
        [whole, pltpu.VMEM((tokens // size, D), jnp.bfloat16), whole, whole, whole]
        + semaphores(n)
        + semaphores(size) * 6,
        [picked, gains, attention, dense, allowed],
        3,
        "encoder",
    )
    return outs[0], outs[1:]


def norm_back_sums(values, gain, upstream):
    scale = lax.rsqrt(jnp.mean(values * values, axis=-1, keepdims=True) + EPS)
    unit = values * scale
    inner = upstream * gain
    grad = scale * (inner - unit * jnp.mean(inner * unit, axis=-1, keepdims=True))
    return grad, jnp.sum(upstream * unit, axis=0, keepdims=True)


def encoder_back_kernel(
    n, size, grad_encoded, gains, attention, dense, allowed,
    first, middle, top, inputs, query, key, value, mixed, dense_in, hidden, active,
    text_rows, gain_grads, attention_grads, dense_grads,
    short, mine, got_encoded, got_dense, got_mixed, every_dense, every_mixed, every_text, *sems,
):
    row, column = Row(size), Column(n)
    rows, width = first.shape[0], text_rows.shape[2]
    short[...] = grad_encoded[...].astype(jnp.bfloat16)
    greet(row, column)
    gain_grads[...] = jnp.zeros(gain_grads.shape, jnp.float32)
    work = RowSum(row, short, got_encoded, rows, *sems[:2])
    work.start()
    grad, gain = norm_back_sums(top[...], gains[2:3], work.finish())
    gain_grads[2:3] = gain
    work = RowSpread(row, mine, every_dense, *sems[2:4])
    work.start(grad.astype(jnp.bfloat16))
    upstream = work.finish()
    inner = hidden[...]
    share = 0.5 * (1.0 + lax.erf(inner * math.sqrt(0.5)))
    slope = share + inner * jnp.exp(-0.5 * inner * inner) * (1.0 / math.sqrt(2.0 * math.pi))
    grad_hidden = (
        slope * jnp.dot(upstream, dense[1], preferred_element_type=jnp.float32)
    ).astype(jnp.bfloat16)
    work = RowSum(row, short, got_dense, rows, *sems[4:6])
    work.start(product(grad_hidden, dense[0], LAST))
    dense_grads[0] = product(dense_in[...], grad_hidden, FIRST).astype(jnp.bfloat16)
    dense_grads[1] = product(upstream, active[...], FIRST).astype(jnp.bfloat16)
    part, gain = norm_back_sums(middle[...], gains[1:2], work.finish())
    gain_grads[1:2] = gain
    grad = grad + part
    work = RowSpread(row, mine, every_mixed, *sems[6:8])
    work.start(grad.astype(jnp.bfloat16))
    upstream = work.finish()
    grad_mixed = jnp.dot(upstream, attention[3], preferred_element_type=jnp.float32).astype(
        jnp.bfloat16
    )
    scale = HEAD_DIM ** (-0.5)
    grad_query = grad_key = grad_value = jnp.zeros(query.shape, jnp.float32)
    for lanes in head_lanes(query.shape[1]):
        shares = full_shares(query[...], key[...], allowed[...], lanes)
        head_up = only(lanes, grad_mixed)
        grad_value = grad_value + product(shares.astype(jnp.bfloat16), head_up, FIRST)
        grad_shares = product(head_up, value[...], LAST)
        delta = jnp.sum(shares * grad_shares, axis=-1, keepdims=True)
        grad_scores = (shares * (grad_shares - delta)).astype(jnp.bfloat16)
        grad_query = grad_query + scale * jnp.dot(
            grad_scores, only(lanes, key[...]), preferred_element_type=jnp.float32
        )
        grad_key = grad_key + scale * product(grad_scores, only(lanes, query[...]), FIRST)
    grad_query = grad_query.astype(jnp.bfloat16)
    grad_key = grad_key.astype(jnp.bfloat16)
    grad_value = grad_value.astype(jnp.bfloat16)
    work = RowSum(row, short, got_mixed, rows, *sems[8:10])
    work.start(
        product(grad_query, attention[0], LAST)
        + product(grad_key, attention[1], LAST)
        + product(grad_value, attention[2], LAST)
    )
    for which, part in enumerate((grad_query, grad_key, grad_value)):
        attention_grads[which] = product(inputs[...], part, FIRST).astype(jnp.bfloat16)
    attention_grads[3] = product(upstream, mixed[...], FIRST).astype(jnp.bfloat16)
    part, gain = norm_back_sums(first[...], gains[0:1], work.finish())
    gain_grads[0:1] = gain
    work = RowSpread(row, mine, every_text, *sems[10:12])
    work.start((grad + part).astype(jnp.bfloat16))
    work.finish()

    def columns(index):
        return every_text.at[:, pl.ds(pl.multiple_of(index * width, 128), width)]

    text_rows[column.me] = columns(column.me)[...]
    exchange(column, columns, lambda index: text_rows.at[index], *sems[12:14])


def encoder_backward(grad_encoded, gains, attention, dense, allowed, kept):
    n = lax.axis_size("dp")
    tokens = grad_encoded.shape[0]
    size = lax.axis_size("img") * lax.axis_size("t")
    whole = pltpu.VMEM((tokens, D), jnp.bfloat16)
    return encoder_call(
        partial(encoder_back_kernel, n, size),
        [
            jax.ShapeDtypeStruct((n, tokens, D // n), jnp.bfloat16),
            jax.ShapeDtypeStruct((8, D), jnp.float32),
            jax.ShapeDtypeStruct(attention.shape, jnp.bfloat16),
            jax.ShapeDtypeStruct(dense.shape, jnp.bfloat16),
        ],
        [whole, pltpu.VMEM((tokens // size, D), jnp.bfloat16)]
        + [whole] * 6
        + semaphores(size) * 6
        + semaphores(n),
        [grad_encoded, gains, attention, dense, allowed, *kept],
        4,
        "encoder_back",
    )


def causal_kernel(query, key, value, mixed, partition):
    length = query.shape[0]
    block = min(256, length)
    scale = HEAD_DIM ** (-0.5)
    halves = head_lanes(query.shape[1])
    for begin in range(0, length, block):
        at, end = pl.ds(begin, block), begin + block
        ahead = lax.broadcasted_iota(jnp.int32, (block, end), 1) > begin + (
            lax.broadcasted_iota(jnp.int32, (block, end), 0)
        )
        out = jnp.zeros((block, query.shape[1]), jnp.float32)
        logs = jnp.zeros((block, query.shape[1]), jnp.float32)
        for lanes in halves:
            scores = product(only(lanes, query[at]), key[:end], LAST) * scale
            scores = jnp.where(ahead, NEGATIVE, scores)
            highest = jnp.max(scores, axis=-1, keepdims=True)
            weight = jnp.exp(scores - highest)
            total = jnp.sum(weight, axis=-1, keepdims=True)
            shares = (weight * (1.0 / total)).astype(jnp.bfloat16)
            out = out + jnp.dot(
                shares, only(lanes, value[:end]), preferred_element_type=jnp.float32
            )
            logs = jnp.where(lanes, highest + jnp.log(total), logs)
        mixed[at] = out.astype(jnp.bfloat16)
        partition[at] = logs


def causal_back_kernel(
    query, key, value, upstream, partition, out_query, out_key, out_value, grad_key, grad_value
):
    length = query.shape[0]
    block = min(256, length)
    scale = HEAD_DIM ** (-0.5)
    halves = head_lanes(query.shape[1])
    grad_key[...] = jnp.zeros(grad_key.shape, jnp.float32)
    grad_value[...] = jnp.zeros(grad_value.shape, jnp.float32)
    for begin in range(0, length, block):
        at, end = pl.ds(begin, block), begin + block
        ahead = lax.broadcasted_iota(jnp.int32, (block, end), 1) > begin + (
            lax.broadcasted_iota(jnp.int32, (block, end), 0)
        )
        grad_query = jnp.zeros((block, query.shape[1]), jnp.float32)
        for head, lanes in enumerate(halves):
            head_query, head_up = only(lanes, query[at]), only(lanes, upstream[at])
            log = partition[at, head * HEAD_DIM : head * HEAD_DIM + 1]
            scores = product(head_query, key[:end], LAST) * scale
            shares = jnp.exp(jnp.where(ahead, NEGATIVE, scores) - log)
            grad_value[:end] += product(shares.astype(jnp.bfloat16), head_up, FIRST)
            grad_shares = product(head_up, value[:end], LAST)
            delta = jnp.sum(shares * grad_shares, axis=-1, keepdims=True)
            grad_scores = (shares * (grad_shares - delta)).astype(jnp.bfloat16)
            grad_query = grad_query + jnp.dot(
                grad_scores, only(lanes, key[:end]), preferred_element_type=jnp.float32
            )
            grad_key[:end] += product(grad_scores, head_query, FIRST)
        out_query[at] = (grad_query * scale).astype(jnp.bfloat16)
    out_key[...] = (grad_key[...] * scale).astype(jnp.bfloat16)
    out_value[...] = grad_value[...].astype(jnp.bfloat16)


def by_heads(kernel, operands, kinds, scratch):
    length, width = operands[0].shape
    lanes = min(128, width)
    spec = pl.BlockSpec((length, lanes), lambda pair: (0, pair))
    return pl.pallas_call(
        kernel,
        grid=(width // lanes,),
        out_shape=[jax.ShapeDtypeStruct((length, width), kind) for kind in kinds],
        in_specs=[spec] * len(operands),
        out_specs=[spec] * len(kinds),
        scratch_shapes=[pltpu.VMEM((length, lanes), jnp.float32)] * scratch,
        compiler_params=pltpu.CompilerParams(vmem_limit_bytes=40 * 2**20),
        cost_estimate=pl.CostEstimate(
            flops=4 * length * length * width, bytes_accessed=2**25, transcendentals=length * length
        ),
        name="causal",
    )(*operands)


def causal_forward(query, key, value):
    return by_heads(causal_kernel, (query, key, value), (jnp.bfloat16, jnp.float32), 0)


def causal_backward(query, key, value, partition, upstream):
    return by_heads(
        causal_back_kernel, (query, key, value, upstream, partition), (jnp.bfloat16,) * 3, 2
    )


def table_kernel(blocks, table):
    table[...] = blocks[0, 0]


def table_of(blocks):
    n, images, rows, columns = blocks.shape
    return pl.pallas_call(
        table_kernel,
        grid=(images, n),
        out_shape=jax.ShapeDtypeStruct((images * rows, n * columns), blocks.dtype),
        in_specs=[pl.BlockSpec((1, 1, rows, columns), lambda i, z: (z, i, 0, 0))],
        out_specs=pl.BlockSpec((rows, columns), lambda i, z: (i, z)),
        cost_estimate=pl.CostEstimate(flops=0, bytes_accessed=2**24, transcendentals=0),
        name="table",
    )(blocks)


def share_kernel(n, size, mine, every, *sems):
    row, column = Row(size), Column(n)
    greet(row, column)
    every[column.me, row.me] = mine[...]
    exchange(row, lambda _: mine, lambda index: every.at[column.me, index], *sems[:2])
    exchange(
        column, lambda _: every.at[column.me], lambda index: every.at[index], *sems[2:]
    )


def share(values):
    n = lax.axis_size("dp")
    size = lax.axis_size("img") * lax.axis_size("t")
    return small_call(
        partial(share_kernel, n, size),
        jax.ShapeDtypeStruct((n, size) + values.shape, values.dtype),
        semaphores(size) + semaphores(n),
        [values],
        7,
        "share",
    )


def total_kernel(n, size, mine, result, row_got, column_got, part, *sems):
    row, column = Row(size), Column(n)
    greet(row, column)
    row_got[row.me] = mine[...]
    exchange(row, lambda _: mine, lambda index: row_got.at[index], *sems[:2])
    added = row_got[0]
    for index in range(1, size):
        added = added + row_got[index]
    part[...] = added
    column_got[column.me] = added
    exchange(column, lambda _: part, lambda index: column_got.at[index], *sems[2:])
    added = column_got[0]
    for index in range(1, n):
        added = added + column_got[index]
    result[...] = added


def total_of(values):
    n = lax.axis_size("dp")
    size = lax.axis_size("img") * lax.axis_size("t")
    return small_call(
        partial(total_kernel, n, size),
        jax.ShapeDtypeStruct(values.shape, values.dtype),
        [
            pltpu.VMEM((size,) + values.shape, values.dtype),
            pltpu.VMEM((n,) + values.shape, values.dtype),
            pltpu.VMEM(values.shape, values.dtype),
        ]
        + semaphores(size)
        + semaphores(n),
        [values],
        8,
        "total",
    )


def rms_norm(values, gain):
    return values * lax.rsqrt(jnp.mean(values * values, axis=-1, keepdims=True) + EPS) * gain


def norm_back(values, gain, upstream):
    _, pull = jax.vjp(rms_norm, values, gain)
    return pull(upstream)


def gelu_exact(values):
    return jax.nn.gelu(values, approximate=False)


ROW = ("img", "t")


def spread(values, axis):
    if axis == "t" and lax.axis_size("t") == 2:
        other = lax.ppermute(values, "t", [(0, 1), (1, 0)])
        first = lax.axis_index("t") == 0
        return jnp.concatenate(
            [jnp.where(first, values, other), jnp.where(first, other, values)], axis=0
        )
    return lax.all_gather(values, axis, axis=0, tiled=True)


def collect(values, axis):
    if axis == "t" and lax.axis_size("t") == 2:
        half = values.shape[0] // 2
        place = lax.axis_index("t")
        away = lax.dynamic_slice_in_dim(values, (1 - place) * half, half, 0)
        came = lax.ppermute(away.astype(jnp.bfloat16), "t", [(0, 1), (1, 0)])
        return lax.dynamic_slice_in_dim(values, place * half, half, 0) + came.astype(jnp.float32)
    return lax.psum_scatter(
        values.astype(jnp.bfloat16), axis, scatter_dimension=0, tiled=True
    ).astype(jnp.float32)


def product(left, right, dims):
    return lax.dot_general(left, right, dims, preferred_element_type=jnp.float32)


def split_heads(values, groups):
    return values.reshape(groups, values.shape[0] // groups, values.shape[1] // HEAD_DIM, HEAD_DIM)


def core_forward(query, key, value, allowed, scale):
    scores = jnp.einsum("bqhe,bkhe->bhqk", query, key, preferred_element_type=jnp.float32) * scale
    scores = jnp.where(allowed[:, None], scores, NEGATIVE)
    highest = jnp.max(scores, axis=-1, keepdims=True)
    weight = jnp.exp(scores - highest)
    totals = jnp.sum(weight, axis=-1, keepdims=True)
    shares = (weight / totals).astype(jnp.bfloat16)
    mixed = jnp.einsum("bhqk,bkhe->bqhe", shares, value, preferred_element_type=jnp.float32)
    return (mixed.astype(jnp.bfloat16), highest + jnp.log(totals))


def core_backward(query, key, value, allowed, scale, partition, upstream):
    scores = jnp.einsum("bqhe,bkhe->bhqk", query, key, preferred_element_type=jnp.float32) * scale
    scores = jnp.where(allowed[:, None], scores, NEGATIVE)
    shares = jnp.exp(scores - partition)
    grad_value = jnp.einsum(
        "bhqk,bqhe->bkhe", shares.astype(jnp.bfloat16), upstream, preferred_element_type=jnp.float32
    )
    grad_shares = jnp.einsum("bqhe,bkhe->bhqk", upstream, value, preferred_element_type=jnp.float32)
    inner = jnp.sum(shares * grad_shares, axis=-1, keepdims=True)
    grad_scores = (shares * (grad_shares - inner)).astype(jnp.bfloat16)
    grad_query = (
        jnp.einsum("bhqk,bkhe->bqhe", grad_scores, key, preferred_element_type=jnp.float32) * scale
    )
    grad_key = (
        jnp.einsum("bhqk,bqhe->bkhe", grad_scores, query, preferred_element_type=jnp.float32)
        * scale
    )
    return (grad_query, grad_key, grad_value)


def mix_forward(query, key, value, kind, context):
    scale = HEAD_DIM ** (-0.5)
    width = query.shape[1]
    if kind == "self":
        return causal_forward(query, key, value)
    query, key, value = (split_heads(part, 1) for part in (query, key, value))
    mixed, partition = core_forward(query, key, value, context["allowed"], scale)
    return (mixed.reshape(-1, width), partition)


def mix_backward(query, key, value, partition, upstream, kind, context):
    scale = HEAD_DIM ** (-0.5)
    width = query.shape[1]
    if kind == "self":
        return causal_backward(query, key, value, partition, upstream)
    query, key, value, upstream = (split_heads(part, 1) for part in (query, key, value, upstream))
    grads = core_backward(query, key, value, context["allowed"], scale, partition, upstream)
    return tuple(grad.reshape(-1, width).astype(jnp.bfloat16) for grad in grads)


def attention_forward(values, gain, weights, kind, axis, context, source=None):
    normed = rms_norm(values, gain).astype(jnp.bfloat16)
    inputs = spread(normed, axis)
    if source is None:
        source = inputs
    query = jnp.dot(inputs, weights[0], preferred_element_type=jnp.float32).astype(jnp.bfloat16)
    key = jnp.dot(source, weights[1], preferred_element_type=jnp.float32).astype(jnp.bfloat16)
    value = jnp.dot(source, weights[2], preferred_element_type=jnp.float32).astype(jnp.bfloat16)
    mixed, partition = mix_forward(query, key, value, kind, context)
    output = collect(product(mixed, weights[3], LAST), axis)
    return (output, (inputs, source, query, key, value, mixed, partition))


def attention_backward(upstream, values, gain, weights, kind, axis, context, kept):
    inputs, source, query, key, value, mixed, partition = kept
    grad_rows = spread(upstream.astype(jnp.bfloat16), axis)
    grad_out = product(grad_rows, mixed, FIRST)
    grad_mixed = jnp.dot(grad_rows, weights[3], preferred_element_type=jnp.float32).astype(
        jnp.bfloat16
    )
    grad_query, grad_key, grad_value = mix_backward(
        query, key, value, partition, grad_mixed, kind, context
    )
    grads = [
        product(inputs, grad_query, FIRST).astype(jnp.bfloat16),
        product(source, grad_key, FIRST).astype(jnp.bfloat16),
        product(source, grad_value, FIRST).astype(jnp.bfloat16),
        grad_out.astype(jnp.bfloat16),
    ]
    from_query = product(grad_query, weights[0], LAST)
    from_source = product(grad_key, weights[1], LAST) + product(grad_value, weights[2], LAST)
    if kind == "cross":
        grad_normed = collect(from_query, axis)
    else:
        grad_normed = collect(from_query + from_source, axis)
    grad_values, grad_gain = norm_back(values, gain, grad_normed)
    return (grad_values, grad_gain, grads, from_source)


def dense_forward(values, gain, weights, axis):
    normed = rms_norm(values, gain).astype(jnp.bfloat16)
    inputs = spread(normed, axis)
    hidden = jnp.dot(inputs, weights[0], preferred_element_type=jnp.float32)
    active = gelu_exact(hidden).astype(jnp.bfloat16)
    output = collect(product(active, weights[1], LAST), axis)
    return (output, (inputs, weights, hidden, active))


def dense_backward(upstream, values, gain, axis, kept):
    inputs, matrices, hidden, active = kept
    grad_rows = spread(upstream.astype(jnp.bfloat16), axis)
    grad_active = jnp.dot(grad_rows, matrices[1], preferred_element_type=jnp.float32)
    _, pull = jax.vjp(gelu_exact, hidden)
    grad_hidden = pull(grad_active)[0].astype(jnp.bfloat16)
    grads = [
        product(inputs, grad_hidden, FIRST).astype(jnp.bfloat16),
        product(grad_rows, active, FIRST).astype(jnp.bfloat16),
    ]
    grad_normed = collect(product(grad_hidden, matrices[0], LAST), axis)
    grad_values, grad_gain = norm_back(values, gain, grad_normed)
    return (grad_values, grad_gain, grads)


def code_hits(token_ids, usable, vocab):
    local = token_ids - lax.axis_index(ROW) * vocab
    places = jnp.arange(vocab, dtype=jnp.int32)
    return ((local[:, None] == places[None, :]) & usable[:, None]).astype(jnp.bfloat16)


def code_forward(token_ids, usable, table):
    hits = code_hits(token_ids, usable, table.shape[0])
    picked = jnp.dot(hits, table, preferred_element_type=jnp.float32).astype(jnp.bfloat16)
    return lax.psum_scatter(picked, ROW, scatter_dimension=0, tiled=True).astype(jnp.float32)


def code_backward(upstream, token_ids, usable, vocab):
    rows = lax.all_gather(upstream.astype(jnp.bfloat16), ROW, axis=0, tiled=True)
    return product(code_hits(token_ids, usable, vocab), rows, FIRST)


def merge_stats(first, second):
    highest = jnp.maximum(first[0], second[0])
    mass = first[1] * jnp.exp(first[0] - highest) + second[1] * jnp.exp(second[0] - highest)
    return (highest, mass, first[2] + second[2], first[3] + second[3])


def joined(stats):
    if lax.axis_size("t") == 2:
        other = lax.ppermute(jnp.stack(stats), "t", [(0, 1), (1, 0)])
        return merge_stats(stats, tuple(other))
    every = lax.all_gather(jnp.stack(stats), "t")
    state = tuple(every[0])
    for place in range(1, every.shape[0]):
        state = merge_stats(state, tuple(every[place]))
    return state


def matrices_of(gathered, n):
    count, rows, columns = gathered.shape
    if rows <= D:
        return gathered
    parts = gathered.reshape(count, n, 4, rows // n // 4, columns)
    return jnp.transpose(parts, (0, 1, 3, 2, 4)).reshape(count, rows // 4, 4 * columns)


def blocks_of(matrix, columns, n):
    if columns % 128 == 0:
        return matrix
    rows = matrix.shape[0]
    parts = matrix.reshape(n, rows // n, 4, columns)
    return jnp.transpose(parts, (0, 2, 1, 3)).reshape(4 * rows, columns)


def update(master, moment, average, gradient, factor, rate):
    clipped = gradient * factor
    moment_new = MOMENT * moment + clipped
    master_new = master - rate * (clipped + MOMENT * moment_new)
    average_new = DECAY * average + (1.0 - DECAY) * master_new
    return (master_new, moment_new, average_new, master_new.astype(jnp.bfloat16))


def per_device(
    code_ids,
    code_mask,
    caption_ids,
    caption_segments,
    image_row,
    attention_master,
    attention_momentum,
    attention_average,
    dense_master,
    dense_momentum,
    dense_average,
    text_master,
    text_momentum,
    text_average,
    code_master,
    code_momentum,
    code_average,
    gain_master,
    gain_momentum,
    gain_average,
):
    n = lax.axis_size("dp")
    z, image, part = lax.axis_index("dp"), lax.axis_index("img"), lax.axis_index("t")
    attention_shape = attention_master.shape[1:]
    dense_shape = dense_master.shape[1:]
    code_shape = code_master.shape[1:]
    images, length = code_ids.shape
    caption_rows, caption_length = caption_ids.shape
    text_rows, text_width = text_master.shape
    text_count = caption_ids.size
    mask = code_mask.astype(jnp.float32)
    encoder_attention, encoder_dense, code_table = (
        lax.all_gather(attention_master[0].astype(jnp.bfloat16), "dp", axis=1, tiled=True),
        lax.all_gather(dense_master[0].astype(jnp.bfloat16), "dp", axis=1, tiled=True),
        lax.all_gather(code_master[0].astype(jnp.bfloat16), "dp", axis=1, tiled=True),
    )
    self_weights, cross_weights, dense_weights = gather(
        [
            attention_master[1].astype(jnp.bfloat16),
            attention_master[2].astype(jnp.bfloat16),
            dense_master[1].astype(jnp.bfloat16),
        ],
        n,
        2.0,
        0,
    )
    self_weights, cross_weights, dense_weights = (
        matrices_of(weights, n) for weights in (self_weights, cross_weights, dense_weights)
    )
    previous = jnp.concatenate(
        [jnp.zeros((images, 1), jnp.int32), code_ids[:, :-1]], axis=1
    ).reshape(-1)
    starting = jnp.broadcast_to(jnp.arange(length) > 0, (images, length)).reshape(-1)
    code_table, self_weights, mask, encoder_attention, encoder_dense = lax.optimization_barrier(
        (code_table, self_weights, mask, encoder_attention, encoder_dense)
    )
    decoder_in = code_forward(previous, starting, code_table)
    out_part, decoder_in = lax.optimization_barrier(
        (code_master[1].astype(jnp.bfloat16), decoder_in)
    )
    out_table = table_of(
        lax.all_gather(out_part, ("dp", "img")).reshape((n, 4) + code_shape)
    )
    gain_width = gain_master.shape[1]
    note = jnp.zeros((16, 128), jnp.float32)
    note = note.at[:7, :gain_width].set(gain_master)
    note = note.at[7, 0].set(jnp.sum(mask))
    note = note.at[8 : 8 + text_count // 128].set(
        caption_ids.astype(jnp.float32).reshape(-1, 128)
    )
    notes = share(note)
    gain_set = (
        jnp.transpose(notes[:, :, :7, :gain_width], (2, 0, 1, 3))
        .reshape(7, D)
    )
    gain_set = lax.reduce_precision(gain_set, exponent_bits=8, mantissa_bits=7)
    count = jnp.sum(notes[:, 0, 7, 0])
    all_text = notes[:, 0, 8 : 8 + text_count // 128].reshape(-1).astype(jnp.int32)
    segments = caption_segments.reshape(-1)
    same = (segments[:, None] == segments[None, :]).astype(jnp.float32)
    row = jnp.sum(jnp.where(jnp.arange(images) == image, image_row, 0)) - z * caption_rows
    owners = lax.dynamic_index_in_dim(caption_segments, row, 0, False)
    cross_context = {"allowed": (owners == z * images + image)[None, None, :]}
    text_local = all_text - lax.axis_index(ROW) * text_rows
    text_inside = (text_local >= 0) & (text_local < text_rows)
    picked = jnp.take(text_master, jnp.clip(text_local, 0, text_rows - 1), axis=0)
    picked = jnp.where(text_inside[:, None], picked, 0.0).astype(jnp.bfloat16)
    encoder_gains = jnp.concatenate([gain_set, jnp.zeros((1, D), jnp.float32)])
    encoded, encoder_keep = encoder_forward(
        picked.reshape(n, text_count, text_width),
        encoder_gains,
        encoder_attention,
        encoder_dense,
        same,
    )
    caption = lax.dynamic_slice_in_dim(encoded, row * caption_length, caption_length, 0)
    branch, self_keep = attention_forward(
        decoder_in, gain_set[3], self_weights, "self", "t", None
    )
    decoder_one = decoder_in + branch
    branch, cross_keep = attention_forward(
        decoder_one, gain_set[4], cross_weights, "cross", "t", cross_context, caption
    )
    decoder_two = decoder_one + branch
    branch, decoder_dense_keep = dense_forward(decoder_two, gain_set[5], dense_weights, "t")
    decoder_top = decoder_two + branch
    final = spread(rms_norm(decoder_top, gain_set[6]).astype(jnp.bfloat16), "t")
    logits = product(final, out_table, LAST)
    rows = code_shape[0]
    codes = lax.dynamic_index_in_dim(code_ids, image, 0, False)
    held = codes // rows
    local_target = jnp.where(
        held % lax.axis_size("t") == part, held // lax.axis_size("t") * rows + codes % rows, -1
    )
    hits = jnp.arange(logits.shape[1], dtype=jnp.int32)[None, :] == local_target[:, None]
    highest = jnp.max(logits, axis=-1)
    highest, mass, target_logit, logit_total = joined(
        (
            highest,
            jnp.sum(jnp.exp(logits - highest[:, None]), axis=-1),
            jnp.sum(jnp.where(hits, logits, 0.0), axis=-1),
            jnp.sum(logits, axis=-1),
        )
    )
    partition = highest + jnp.log(mass)
    valid = lax.dynamic_index_in_dim(mask, image, 0, False)
    per_token = (
        partition
        - (1.0 - SMOOTH) * target_logit
        - SMOOTH * logit_total / VC
        + Z_WEIGHT * partition * partition
    )
    per_image = lax.all_gather(per_token, "img")
    loss_part = jnp.sum(per_token * valid) / lax.axis_size("t")
    weighting = valid / count
    grad_logits = weighting[:, None] * (
        (1.0 + 2.0 * Z_WEIGHT * partition)[:, None] * jnp.exp(logits - partition[:, None])
        - (1.0 - SMOOTH) * hits.astype(jnp.float32)
        - SMOOTH / VC
    )
    grad_logits = grad_logits.astype(jnp.bfloat16)
    grad_out_table = product(grad_logits, final, FIRST).astype(jnp.bfloat16)
    out_grads = lax.psum_scatter(
        lax.psum_scatter(grad_out_table, "img", scatter_dimension=0, tiled=True),
        "dp",
        scatter_dimension=1,
        tiled=True,
    ).astype(jnp.float32)
    grad_final = collect(
        jnp.dot(grad_logits, out_table, preferred_element_type=jnp.float32), "t"
    )
    grad_top, gain_six = norm_back(decoder_top, gain_set[6], grad_final)
    grad_branch, gain_five, dense_one = dense_backward(
        grad_top, decoder_two, gain_set[5], "t", decoder_dense_keep
    )
    grad_two = grad_top + grad_branch
    grad_branch, gain_four, attention_two, grad_caption = attention_backward(
        grad_two, decoder_one, gain_set[4], cross_weights, "cross", "t", cross_context, cross_keep
    )
    grad_one = grad_two + grad_branch
    grad_branch, gain_three, attention_one, _ = attention_backward(
        grad_one, decoder_in, gain_set[3], self_weights, "self", "t", None, self_keep
    )
    grad_start = grad_one + grad_branch
    narrow = attention_shape[2]
    one_grads, two_grads, dense_one_grads = scatter(
        [
            [blocks_of(matrix, narrow, n) for matrix in attention_one],
            [blocks_of(matrix, narrow, n) for matrix in attention_two],
            dense_one,
        ],
        [attention_shape[1:], attention_shape[1:], dense_shape[1:]],
        n,
        2.0,
        2,
    )
    grad_code_in = code_backward(grad_start, previous, starting, code_shape[0])
    grad_encoded = lax.dynamic_update_slice_in_dim(
        jnp.zeros(encoded.shape, jnp.float32), grad_caption, row * caption_length, 0
    )
    text_rows_back, encoder_gain_grads, attention_zero, dense_zero = encoder_backward(
        grad_encoded, encoder_gains, encoder_attention, encoder_dense, same, encoder_keep
    )
    text_hits = jnp.arange(text_rows, dtype=jnp.int32)[:, None] == text_local[None, :]
    text_grads = jnp.dot(
        text_hits.astype(jnp.bfloat16),
        text_rows_back.reshape(-1, text_width),
        preferred_element_type=jnp.float32,
    )

    def owned(values, axis):
        return lax.psum_scatter(
            values.astype(jnp.bfloat16), "dp", scatter_dimension=axis, tiled=True
        ).astype(jnp.float32)

    attention_grads = jnp.stack(
        [
            owned(attention_zero, 1),
            one_grads.reshape(attention_shape),
            two_grads.reshape(attention_shape),
        ]
    )
    dense_grads = jnp.stack([owned(dense_zero, 1), dense_one_grads.reshape(dense_shape)])
    code_grads = jnp.stack([owned(grad_code_in, 1), out_grads.reshape(code_shape)])
    squares = (
        jnp.sum(attention_grads * attention_grads)
        + jnp.sum(dense_grads * dense_grads)
        + jnp.sum(text_grads * text_grads)
        + jnp.sum(code_grads * code_grads)
    )
    sums = jnp.concatenate(
        [
            encoder_gain_grads[:3],
            jnp.stack([gain_three, gain_four, gain_five, gain_six]),
        ]
    )
    tail = jnp.zeros((1, D), jnp.float32).at[0, 0].set(squares).at[0, 1].set(loss_part)
    sums = total_of(jnp.concatenate([sums, tail], axis=0))
    gain_sums = sums[:7]
    loss = sums[7, 1] / count
    norm = jnp.sqrt(sums[7, 0] + jnp.sum(gain_sums * gain_sums))
    gain_grads = lax.dynamic_slice_in_dim(
        gain_sums, lax.axis_index(("dp",) + ROW) * gain_width, gain_width, 1
    )
    factor = jnp.minimum(1.0, CLIP / norm)
    rate = 0.012 * math.sqrt(12 * D * D + 4 * D * FF + VT * D + 2 * VC * D + 7 * D) / CLIP
    attention_out = update(
        attention_master, attention_momentum, attention_average, attention_grads, factor, rate
    )
    dense_out = update(dense_master, dense_momentum, dense_average, dense_grads, factor, rate)
    text_out = update(text_master, text_momentum, text_average, text_grads, factor, rate)
    code_out = update(code_master, code_momentum, code_average, code_grads, factor, rate)
    gain_out = update(gain_master, gain_momentum, gain_average, gain_grads, factor, rate)
    return (
        loss,
        norm,
        attention_out[0],
        attention_out[1],
        attention_out[2],
        attention_out[3],
        dense_out[0],
        dense_out[1],
        dense_out[2],
        dense_out[3],
        text_out[0],
        text_out[1],
        text_out[2],
        text_out[3],
        code_out[0],
        code_out[1],
        code_out[2],
        code_out[3],
        gain_out[0],
        gain_out[1],
        gain_out[2],
        gain_out[3],
        per_image,
    )


def solution(mesh):
    n, m = mesh.shape["dp"], mesh.shape["mp"]
    view = Mesh(mesh.devices.reshape(n, 4, m // 4), ("dp",) + ROW)
    return jax.shard_map(
        per_device,
        mesh=view,
        in_specs=(
            P("dp", None),
            P("dp", None),
            P("dp", None),
            P("dp", None),
            P("dp"),
            P(None, None, "dp", ROW),
            P(None, None, "dp", ROW),
            P(None, None, "dp", ROW),
            P(None, None, "dp", ROW),
            P(None, None, "dp", ROW),
            P(None, None, "dp", ROW),
            P(ROW, "dp"),
            P(ROW, "dp"),
            P(ROW, "dp"),
            P(None, ROW, "dp"),
            P(None, ROW, "dp"),
            P(None, ROW, "dp"),
            P(None, ("dp",) + ROW),
            P(None, ("dp",) + ROW),
            P(None, ("dp",) + ROW),
        ),
        out_specs=(
            P(),
            P(),
            P(None, None, "dp", ROW),
            P(None, None, "dp", ROW),
            P(None, None, "dp", ROW),
            P(None, None, "dp", ROW),
            P(None, None, "dp", ROW),
            P(None, None, "dp", ROW),
            P(None, None, "dp", ROW),
            P(None, None, "dp", ROW),
            P(ROW, "dp"),
            P(ROW, "dp"),
            P(ROW, "dp"),
            P(ROW, "dp"),
            P(None, ROW, "dp"),
            P(None, ROW, "dp"),
            P(None, ROW, "dp"),
            P(None, ROW, "dp"),
            P(None, ("dp",) + ROW),
            P(None, ("dp",) + ROW),
            P(None, ("dp",) + ROW),
            P(None, ("dp",) + ROW),
            P("dp", None),
        ),
        check_vma=False,
    )
```

```python
from functools import partial
import math

import jax
import jax.numpy as jnp
from jax import lax
from jax.experimental import pallas as pl
from jax.experimental.pallas import tpu as pltpu
from jax.sharding import Mesh, PartitionSpec as P

D = 1024
HEAD_DIM = 64
FF = 4096
VC = 8192
VT = 16000


EPS = 1e-06
CLIP = 0.01
MOMENT = 0.9
DECAY = 0.75
SMOOTH = 0.1
Z_WEIGHT = 0.01
NEGATIVE = -1e30
LAST = (((1,), (1,)), ((), ()))
FIRST = (((0,), (0,)), ((), ()))


MESH = pl.DeviceIdType.MESH
ORDERS = ((0, 1, 2), (0, 2, 1))


def sources(n):
    return [(far, bits) for far in range(1 - n, n) for bits in range(4)]


def hops(far, bits):
    return abs(far) + (bits & 1) + (bits >> 1)


def arrival(order, far, bits):
    last = None
    for dim in order:
        if (dim == 0 and far != 0) or (dim > 0 and bits & dim):
            last = dim
    return last


def passes(order, far, bits):
    came = arrival(order, far, bits)
    place = -1 if came is None else order.index(came)
    found = [(0, -1 if far > 0 else 1)] if came == 0 else []
    for dim in order[place + 1 :]:
        found += [(0, 1), (0, -1)] if dim == 0 else [(dim, 0)]
    return found


def cut_slabs(shapes, gap):
    slabs = []
    base = 0.0
    for which, (rows, _) in enumerate(shapes):
        count = 4 if rows % 64 == 0 else 2
        for part in range(count):
            size = rows // count
            order = ORDERS[part % len(ORDERS)]
            slabs.append((which, part * size, size, order, base + gap * (part // 2)))
        base += gap * (count // 2)
    return slabs


def wide(shape, table, n):
    _, rows, columns = shape
    if table:
        return (4 * rows, n * columns)
    return (n * rows, 4 * columns) if columns % 128 == 0 else (4 * n * rows, columns)


def placed(whole, shape, table, z, i, begin, rows):
    if table or shape[2] % 128 == 0:
        down, right = (i, z) if table else (z, i)
        return whole.at[
            :,
            pl.ds(pl.multiple_of(down * shape[1] + begin, 16), rows),
            pl.ds(pl.multiple_of(right * shape[2], 128), shape[2]),
        ]
    return whole.at[:, pl.ds(pl.multiple_of((z * 4 + i) * shape[1] + begin, 16), rows)]


class Here:
    def __init__(self, n):
        self.n = n
        self.z = lax.axis_index("dp")
        self.i = lax.axis_index("img")
        self.t = lax.axis_index("t")

    def device(self, dim, step):
        if dim == 0:
            return (self.z + step, self.i, self.t)
        return (self.z, jnp.bitwise_xor(self.i, dim), self.t)

    def below(self):
        return self.z > 0

    def above(self):
        return self.z < self.n - 1

    def side(self, step):
        return self.above() if step > 0 else self.below()

    def greet(self):
        barrier = pltpu.get_barrier_semaphore()

        def tell(device):
            pl.semaphore_signal(barrier, inc=1, device_id=device, device_id_type=MESH)

        pl.when(self.below())(lambda: tell(self.device(0, -1)))
        pl.when(self.above())(lambda: tell(self.device(0, 1)))
        tell(self.device(1, 0))
        tell(self.device(2, 0))
        pl.semaphore_wait(
            barrier, 2 + jnp.where(self.below(), 1, 0) + jnp.where(self.above(), 1, 0)
        )

    def exists(self, far):
        if far == 0:
            return None
        return (self.z + far >= 0) if far < 0 else (self.z + far < self.n)


def guarded(condition, action):
    if condition is None:
        action()
    else:
        pl.when(condition)(action)


def both(first, second):
    if first is None or second is None:
        return second if first is None else first
    return jnp.logical_and(first, second)


def gather_kernel(n, slabs, tables, *refs):
    count = len(tables)
    ins, outs = refs[:count], refs[count : 2 * count]
    send_sem, recv_sem, local_sem = refs[2 * count :]
    here = Here(n)
    here.greet()
    local = []
    for which in range(count):
        shape = ins[which].shape
        copy = pltpu.make_async_copy(
            ins[which],
            placed(outs[which], shape, tables[which], here.z, here.i, 0, shape[1]),
            local_sem.at[which],
        )
        copy.start()
        local.append(copy)

    def block(slab, far, bits):
        which, begin, rows = slabs[slab][:3]
        z, i = here.z + far, jnp.bitwise_xor(here.i, bits)
        return placed(outs[which], ins[which].shape, tables[which], z, i, begin, rows)

    def name(far, bits):
        return (here.z + far) * 4 + jnp.bitwise_xor(here.i, bits)

    def copy_of(slab, far, bits, dim, step):
        which, begin, rows = slabs[slab][:3]
        target = block(slab, far, bits)
        own = far == 0 and bits == 0
        return pltpu.make_async_remote_copy(
            src_ref=ins[which].at[:, pl.ds(begin, rows)] if own else target,
            dst_ref=target,
            send_sem=send_sem.at[slab, name(far, bits), (1 + step) // 2 if dim == 0 else 1 + dim],
            recv_sem=recv_sem.at[slab, name(far, bits)],
            device_id=here.device(dim, step),
            device_id_type=MESH,
        )

    def arrive(slab, far, bits):
        target = block(slab, far, bits)
        pltpu.make_async_remote_copy(
            src_ref=target,
            dst_ref=target,
            send_sem=send_sem.at[slab, 0, 0],
            recv_sem=recv_sem.at[slab, name(far, bits)],
            device_id=here.device(1, 0),
            device_id_type=MESH,
        ).wait_recv()

    events = sorted(
        (slabs[slab][4] + hops(far, bits), slab, far, bits)
        for slab in range(len(slabs))
        for far, bits in sources(n)
    )
    sent = []
    final = []
    for _, slab, far, bits in events:
        onward = passes(slabs[slab][3], far, bits)
        own = far == 0 and bits == 0
        if not onward:
            final.append((slab, far, bits))
            continue

        def act(slab=slab, far=far, bits=bits, onward=onward, own=own):
            if not own:
                arrive(slab, far, bits)
            for dim, step in onward:
                guarded(
                    here.side(step) if dim == 0 else None,
                    lambda dim=dim, step=step: copy_of(slab, far, bits, dim, step).start(),
                )

        guarded(here.exists(far), act)
        sent += [(slab, far, bits, dim, step) for dim, step in onward]
    for slab, far, bits in final:
        guarded(here.exists(far), lambda at=(slab, far, bits): arrive(*at))
    for slab, far, bits, dim, step in sent:
        guarded(
            both(here.exists(far), here.side(step) if dim == 0 else None),
            lambda at=(slab, far, bits, dim, step): copy_of(*at).wait_send(),
        )
    for copy in local:
        copy.wait()


def gather(arrays, tables, n, gap, collective_id):
    count = len(arrays)
    slabs = cut_slabs([a.shape[1:] for a in arrays], gap)
    size = sum(a.size * a.dtype.itemsize for a in arrays) * 4 * n
    return pl.pallas_call(
        partial(gather_kernel, n, slabs, tables),
        out_shape=[
            jax.ShapeDtypeStruct((a.shape[0],) + wide(a.shape, table, n), a.dtype)
            for a, table in zip(arrays, tables)
        ],
        in_specs=[pl.BlockSpec(memory_space=pl.ANY)] * count,
        out_specs=[pl.BlockSpec(memory_space=pl.ANY)] * count,
        scratch_shapes=[
            pltpu.SemaphoreType.DMA((len(slabs), 4 * n, 4)),
            pltpu.SemaphoreType.DMA((len(slabs), 4 * n)),
            pltpu.SemaphoreType.DMA((count,)),
        ],
        compiler_params=pltpu.CompilerParams(
            collective_id=collective_id, has_side_effects=True
        ),
        cost_estimate=pl.CostEstimate(flops=0, bytes_accessed=size * 16, transcendentals=0),
        name="gather",
    )(*arrays)


def places(n, order):
    table = {}
    used = 0
    line = [b for b in range(4) if any(dim == 0 for dim, _ in passes(order, 0, b))]
    for rank, bits in enumerate(line):
        for far in range(1 - n, n):
            for dim, step in passes(order, far, bits):
                if dim == 0:
                    second = far == 0 and step < 0
                    table[far, bits, dim, step] = (
                        (used + n, False) if second else (used + far, True)
                    )
        used += n + 1
    for flip in (1, 2):
        pairs = [p for p in sources(n) if (flip, 0) in passes(order, *p)]
        spread = any(far for far, _ in pairs)
        for bits in sorted({b for _, b in pairs}):
            for far, other in pairs:
                if other == bits:
                    table[far, bits, flip, 0] = (used + far, True) if spread else (used, False)
            used += n if spread else 1
    return table, used


def scatter_kernel(n, slabs, members, *refs):
    total = sum(members)
    count = len(members)
    ins, refs = refs[:total], refs[total:]
    outs, owns, gots = refs[:count], refs[count : 2 * count], refs[2 * count : 3 * count]
    send_sem, recv_sem, local_sem = refs[3 * count :]
    here = Here(n)
    tables = {order: places(n, order)[0] for order in ORDERS}
    loads = []
    for which in range(count):
        for member in range(members[which]):
            matrix = ins[sum(members[:which]) + member]
            rows = owns[which].shape[2] // members[which]
            columns = owns[which].shape[3]
            for z in range(n):
                for i in range(4):
                    copy = pltpu.make_async_copy(
                        matrix.at[pl.ds(z * rows, rows), pl.ds(i * columns, columns)]
                        if matrix.shape[0] == n * rows
                        else matrix.at[pl.ds((z * 4 + i) * rows, rows)],
                        owns[which].at[z, i, pl.ds(member * rows, rows)],
                        local_sem.at[len(loads)],
                    )
                    copy.start()
                    loads.append(copy)
    here.greet()
    for copy in loads:
        copy.wait()

    def own(slab, far, bits):
        which, begin, rows = slabs[slab][:3]
        return owns[which].at[
            here.z + far, jnp.bitwise_xor(here.i, bits), pl.ds(begin, rows)
        ]

    def slot(slab, number):
        which, _, rows, _, _, first = slabs[slab]
        return gots[which].at[pl.ds(pl.multiple_of(first + number * rows, 16), rows)]

    def number_at(order, z, key):
        constant, counts = tables[order][key]
        return constant + z if counts else constant

    def copy_of(slab, far, bits):
        order = slabs[slab][3]
        dim = arrival(order, far, bits)
        step = 0 if dim else (1 if far > 0 else -1)
        number = number_at(order, here.z + step, (far - step, bits ^ dim, dim, -step))
        return pltpu.make_async_remote_copy(
            src_ref=own(slab, far, bits),
            dst_ref=slot(slab, number),
            send_sem=send_sem.at[slab, (here.z + far) * 4 + bits],
            recv_sem=recv_sem.at[slab, number],
            device_id=here.device(dim, step),
            device_id_type=MESH,
        )

    events = sorted(
        (slabs[slab][4] + n + 1 - hops(far, bits), slab, far, bits)
        for slab in range(len(slabs))
        for far, bits in sources(n)
    )

    def add_up(slab, far, bits, parts):
        which, begin, rows, order = slabs[slab][:4]
        numbers = [number_at(order, here.z, (far, bits) + part) for part in parts]
        for number in numbers:
            landed = slot(slab, number)
            pltpu.make_async_remote_copy(
                src_ref=landed,
                dst_ref=landed,
                send_sem=send_sem.at[slab, 0],
                recv_sem=recv_sem.at[slab, number],
                device_id=here.device(1, 0),
                device_id_type=MESH,
            ).wait_recv()
        root = far == 0 and bits == 0
        if not parts and not root:
            return
        mine = own(slab, far, bits)
        landed = [slot(slab, number) for number in numbers]

        @pl.loop(0, rows // 16)
        def _(row):
            at = pl.ds(pl.multiple_of(row * 16, 16), 16)
            added = mine[at].astype(jnp.float32)
            for part in landed:
                added = added + part[at].astype(jnp.float32)
            if root:
                outs[which][pl.ds(pl.multiple_of(begin + row * 16, 16), 16)] = added
            else:
                mine[at] = added.astype(jnp.bfloat16)

    for _, slab, far, bits in events:

        def act(slab=slab, far=far, bits=bits):
            parts = passes(slabs[slab][3], far, bits)
            fixed = [p for p in parts if p[0]]
            line = [p for p in parts if not p[0]]
            if not line:
                add_up(slab, far, bits, fixed)
            elif len(line) == 1:
                there = here.side(line[0][1])
                pl.when(there)(lambda: add_up(slab, far, bits, line + fixed))
                pl.when(jnp.logical_not(there))(lambda: add_up(slab, far, bits, fixed))
            else:
                low, high = here.below(), here.above()
                up, down = line
                pl.when(jnp.logical_and(low, high))(
                    lambda: add_up(slab, far, bits, line + fixed)
                )
                pl.when(jnp.logical_not(low))(lambda: add_up(slab, far, bits, [up] + fixed))
                pl.when(jnp.logical_not(high))(lambda: add_up(slab, far, bits, [down] + fixed))
            if far or bits:
                copy_of(slab, far, bits).start()

        guarded(here.exists(far), act)
    for _, slab, far, bits in events:
        if far or bits:
            guarded(
                here.exists(far),
                lambda at=(slab, far, bits): copy_of(*at).wait_send(),
            )


def scatter(groups, shapes, n, gap, collective_id):
    members = [len(group) for group in groups]
    slabs = []
    totals = [0] * len(groups)
    most = 0
    sizes = [(m * rows, columns) for m, (rows, columns) in zip(members, shapes)]
    for which, begin, rows, order, base in cut_slabs(sizes, gap):
        used = places(n, order)[1]
        slabs.append((which, begin, rows, order, base, totals[which]))
        totals[which] += rows * used
        most = max(most, used)
    size = sum(rows * columns for rows, columns in sizes) * 8 * n
    return pl.pallas_call(
        partial(scatter_kernel, n, slabs, members),
        out_shape=[jax.ShapeDtypeStruct(size, jnp.float32) for size in sizes],
        in_specs=[pl.BlockSpec(memory_space=pl.ANY)] * sum(members),
        out_specs=[pl.BlockSpec(memory_space=pltpu.VMEM)] * len(groups),
        scratch_shapes=[pltpu.VMEM((n, 4) + size, jnp.bfloat16) for size in sizes]
        + [pltpu.VMEM((total, size[1]), jnp.bfloat16) for size, total in zip(sizes, totals)]
        + [
            pltpu.SemaphoreType.DMA((len(slabs), 4 * n)),
            pltpu.SemaphoreType.DMA((len(slabs), most)),
            pltpu.SemaphoreType.DMA((4 * n * sum(members),)),
        ],
        compiler_params=pltpu.CompilerParams(
            collective_id=collective_id, has_side_effects=True, vmem_limit_bytes=58 * 2**20
        ),
        cost_estimate=pl.CostEstimate(flops=0, bytes_accessed=size * 16, transcendentals=0),
        name="scatter",
    )(*[matrix for group in groups for matrix in group])


class Row:
    def __init__(self, size):
        self.size = size
        self.parts = size // 4
        self.me = lax.axis_index("img") * self.parts + lax.axis_index("t")

    def other(self, step):
        return lax.rem(self.me + step, self.size)

    def device(self, index):
        return (lax.axis_index("dp"), index // self.parts, lax.rem(index, self.parts))


class Column:
    def __init__(self, size):
        self.size = size
        self.me = lax.axis_index("dp")

    def other(self, step):
        return lax.rem(self.me + step, self.size)

    def device(self, index):
        return (index, lax.axis_index("img"), lax.axis_index("t"))


def greet(*groups):
    barrier = pltpu.get_barrier_semaphore()
    for group in groups:
        for step in range(1, group.size):
            pl.semaphore_signal(
                barrier, inc=1, device_id=group.device(group.other(step)), device_id_type=MESH
            )
    pl.semaphore_wait(barrier, sum(group.size - 1 for group in groups))


class Exchange:
    def __init__(self, group, source, target, send_sem, recv_sem):
        self.group, self.source, self.target = group, source, target
        self.send_sem, self.recv_sem = send_sem, recv_sem

    def copy_of(self, step):
        index = self.group.other(step)
        return pltpu.make_async_remote_copy(
            src_ref=self.source(index),
            dst_ref=self.target(self.group.me),
            send_sem=self.send_sem.at[step],
            recv_sem=self.recv_sem.at[self.group.me],
            device_id=self.group.device(index),
            device_id_type=MESH,
        )

    def start(self):
        for step in range(1, self.group.size):
            self.copy_of(step).start()
        return self

    def finish(self):
        for step in range(1, self.group.size):
            index = self.group.other(step)
            pltpu.make_async_remote_copy(
                src_ref=self.target(index),
                dst_ref=self.target(index),
                send_sem=self.send_sem.at[step],
                recv_sem=self.recv_sem.at[index],
                device_id=self.group.device(index),
                device_id_type=MESH,
            ).wait_recv()
        for step in range(1, self.group.size):
            self.copy_of(step).wait_send()


def exchange(*parts):
    Exchange(*parts).start().finish()


def row_block(ref, rows, index):
    return ref.at[pl.ds(pl.multiple_of(index * rows, 16), rows)]


def small_call(kernel, out_shape, scratch, operands, collective_id, name):
    vmem = pl.BlockSpec(memory_space=pltpu.VMEM)
    return pl.pallas_call(
        kernel,
        out_shape=out_shape,
        in_specs=[vmem] * len(operands),
        out_specs=[vmem] * len(out_shape) if isinstance(out_shape, list) else vmem,
        scratch_shapes=scratch,
        compiler_params=pltpu.CompilerParams(
            collective_id=collective_id, has_side_effects=True
        ),
        cost_estimate=pl.CostEstimate(flops=0, bytes_accessed=2**24, transcendentals=0),
        name=name,
    )(*operands)


def semaphores(size):
    return [pltpu.SemaphoreType.DMA((size,)), pltpu.SemaphoreType.DMA((size,))]


class RowSpread:
    def __init__(self, row, mine, every, *sems):
        self.mine, self.every, self.rows, self.me = mine, every, mine.shape[0], row.me
        self.work = Exchange(row, lambda _: mine, self.block, *sems)

    def block(self, index):
        return row_block(self.every, self.rows, index)

    def start(self, values):
        self.mine[...] = values
        self.block(self.me)[...] = values
        self.work.start()

    def finish(self):
        self.work.finish()
        return self.every[...]


class RowSum:
    def __init__(self, row, short, got, rows, *sems):
        self.short, self.got, self.rows, self.row = short, got, rows, row
        self.work = Exchange(
            row,
            lambda index: row_block(short, rows, index),
            lambda index: row_block(got, rows, index),
            *sems,
        )

    def start(self, values=None):
        if values is not None:
            self.short[...] = values.astype(jnp.bfloat16)
        mine = row_block(self.short, self.rows, self.row.me)
        row_block(self.got, self.rows, self.row.me)[...] = mine[...]
        self.work.start()

    def finish(self):
        self.work.finish()
        total = self.got[pl.ds(0, self.rows)].astype(jnp.float32)
        for index in range(1, self.row.size):
            total = total + self.got[pl.ds(index * self.rows, self.rows)].astype(jnp.float32)
        return total


def head_lanes(width):
    lanes = lax.broadcasted_iota(jnp.int32, (1, width), 1) // HEAD_DIM
    return [lanes == head for head in range(width // HEAD_DIM)]


def only(lanes, values):
    return jnp.where(lanes, values, jnp.zeros_like(values))


def full_shares(query, key, allowed, lanes):
    scores = product(only(lanes, query), key, LAST) * HEAD_DIM ** (-0.5)
    scores = jnp.where(allowed > 0, scores, NEGATIVE)
    weight = jnp.exp(scores - jnp.max(scores, axis=-1, keepdims=True))
    return weight / jnp.sum(weight, axis=-1, keepdims=True)


def encoder_kernel(
    n, size, picked, gains, attention, dense, allowed,
    encoded, first, middle, top, inputs, query, key, value, mixed, dense_in, hidden, active,
    short, mine, got_text, got_mixed, got_dense, *sems,
):
    row, column = Row(size), Column(n)
    rows, width = first.shape[0], picked.shape[2]
    greet(row, column)

    def columns(index):
        return short.at[:, pl.ds(pl.multiple_of(index * width, 128), width)]

    columns(column.me)[...] = picked[column.me]
    exchange(column, lambda index: picked.at[index], columns, *sems[:2])
    text = RowSum(row, short, got_text, rows, *sems[2:4])
    text.start()
    values = text.finish()
    first[...] = values
    spread_one = RowSpread(row, mine, inputs, *sems[4:6])
    spread_one.start(rms_norm(values, gains[0:1]).astype(jnp.bfloat16))
    every = spread_one.finish()
    query[...] = jnp.dot(
        every, attention[0], preferred_element_type=jnp.float32
    ).astype(jnp.bfloat16)
    key[...] = jnp.dot(every, attention[1], preferred_element_type=jnp.float32).astype(jnp.bfloat16)
    value[...] = jnp.dot(
        every, attention[2], preferred_element_type=jnp.float32
    ).astype(jnp.bfloat16)
    out = jnp.zeros(query.shape, jnp.float32)
    for lanes in head_lanes(query.shape[1]):
        shares = full_shares(query[...], key[...], allowed[...], lanes).astype(jnp.bfloat16)
        out = out + jnp.dot(shares, only(lanes, value[...]), preferred_element_type=jnp.float32)
    mixed[...] = out.astype(jnp.bfloat16)
    branch = RowSum(row, short, got_mixed, rows, *sems[6:8])
    branch.start(product(mixed[...], attention[3], LAST))
    values = values + branch.finish()
    middle[...] = values
    spread_two = RowSpread(row, mine, dense_in, *sems[8:10])
    spread_two.start(rms_norm(values, gains[1:2]).astype(jnp.bfloat16))
    every = spread_two.finish()
    hidden[...] = jnp.dot(every, dense[0], preferred_element_type=jnp.float32)
    inner = hidden[...]
    active[...] = (0.5 * inner * (1.0 + lax.erf(inner * math.sqrt(0.5)))).astype(jnp.bfloat16)
    branch = RowSum(row, short, got_dense, rows, *sems[10:12])
    branch.start(product(active[...], dense[1], LAST))
    values = values + branch.finish()
    top[...] = values
    spread_three = RowSpread(row, mine, encoded, *sems[12:14])
    spread_three.start(rms_norm(values, gains[2:3]).astype(jnp.bfloat16))
    spread_three.finish()


def encoder_call(kernel, out_shape, scratch, operands, collective_id, name):
    vmem = pl.BlockSpec(memory_space=pltpu.VMEM)
    return pl.pallas_call(
        kernel,
        out_shape=out_shape,
        in_specs=[vmem] * len(operands),
        out_specs=[vmem] * len(out_shape),
        scratch_shapes=scratch,
        compiler_params=pltpu.CompilerParams(
            collective_id=collective_id, has_side_effects=True, vmem_limit_bytes=48 * 2**20
        ),
        cost_estimate=pl.CostEstimate(flops=0, bytes_accessed=2**27, transcendentals=0),
        name=name,
    )(*operands)


def encoder_forward(picked, gains, attention, dense, allowed):
    n, tokens, _ = picked.shape
    size = lax.axis_size("img") * lax.axis_size("t")
    width, inner = attention.shape[2], dense.shape[2]
    own = jax.ShapeDtypeStruct((tokens // size, D), jnp.float32)
    every = jax.ShapeDtypeStruct((tokens, D), jnp.bfloat16)
    head = jax.ShapeDtypeStruct((tokens, width), jnp.bfloat16)
    wide_out = [jax.ShapeDtypeStruct((tokens, inner), kind) for kind in (jnp.float32, jnp.bfloat16)]
    whole = pltpu.VMEM((tokens, D), jnp.bfloat16)
    outs = encoder_call(
        partial(encoder_kernel, n, size),
        [every, own, own, own, every, head, head, head, head, every] + wide_out,
        [whole, pltpu.VMEM((tokens // size, D), jnp.bfloat16), whole, whole, whole]
        + semaphores(n)
        + semaphores(size) * 6,
        [picked, gains, attention, dense, allowed],
        3,
        "encoder",
    )
    return outs[0], outs[1:]


def norm_back_sums(values, gain, upstream):
    scale = lax.rsqrt(jnp.mean(values * values, axis=-1, keepdims=True) + EPS)
    unit = values * scale
    inner = upstream * gain
    grad = scale * (inner - unit * jnp.mean(inner * unit, axis=-1, keepdims=True))
    return grad, jnp.sum(upstream * unit, axis=0, keepdims=True)


def encoder_back_kernel(
    n, size, grad_encoded, gains, attention, dense, allowed,
    first, middle, top, inputs, query, key, value, mixed, dense_in, hidden, active,
    text_rows, gain_grads, attention_grads, dense_grads,
    short, mine, got_encoded, got_dense, got_mixed, every_dense, every_mixed, every_text, *sems,
):
    row, column = Row(size), Column(n)
    rows, width = first.shape[0], text_rows.shape[2]
    short[...] = grad_encoded[...].astype(jnp.bfloat16)
    greet(row, column)
    gain_grads[...] = jnp.zeros(gain_grads.shape, jnp.float32)
    work = RowSum(row, short, got_encoded, rows, *sems[:2])
    work.start()
    grad, gain = norm_back_sums(top[...], gains[2:3], work.finish())
    gain_grads[2:3] = gain
    work = RowSpread(row, mine, every_dense, *sems[2:4])
    work.start(grad.astype(jnp.bfloat16))
    upstream = work.finish()
    inner = hidden[...]
    share = 0.5 * (1.0 + lax.erf(inner * math.sqrt(0.5)))
    slope = share + inner * jnp.exp(-0.5 * inner * inner) * (1.0 / math.sqrt(2.0 * math.pi))
    grad_hidden = (
        slope * jnp.dot(upstream, dense[1], preferred_element_type=jnp.float32)
    ).astype(jnp.bfloat16)
    work = RowSum(row, short, got_dense, rows, *sems[4:6])
    work.start(product(grad_hidden, dense[0], LAST))
    dense_grads[0] = product(dense_in[...], grad_hidden, FIRST).astype(jnp.bfloat16)
    dense_grads[1] = product(upstream, active[...], FIRST).astype(jnp.bfloat16)
    part, gain = norm_back_sums(middle[...], gains[1:2], work.finish())
    gain_grads[1:2] = gain
    grad = grad + part
    work = RowSpread(row, mine, every_mixed, *sems[6:8])
    work.start(grad.astype(jnp.bfloat16))
    upstream = work.finish()
    grad_mixed = jnp.dot(upstream, attention[3], preferred_element_type=jnp.float32).astype(
        jnp.bfloat16
    )
    scale = HEAD_DIM ** (-0.5)
    grad_query = grad_key = grad_value = jnp.zeros(query.shape, jnp.float32)
    for lanes in head_lanes(query.shape[1]):
        shares = full_shares(query[...], key[...], allowed[...], lanes)
        head_up = only(lanes, grad_mixed)
        grad_value = grad_value + product(shares.astype(jnp.bfloat16), head_up, FIRST)
        grad_shares = product(head_up, value[...], LAST)
        delta = jnp.sum(shares * grad_shares, axis=-1, keepdims=True)
        grad_scores = (shares * (grad_shares - delta)).astype(jnp.bfloat16)
        grad_query = grad_query + scale * jnp.dot(
            grad_scores, only(lanes, key[...]), preferred_element_type=jnp.float32
        )
        grad_key = grad_key + scale * product(grad_scores, only(lanes, query[...]), FIRST)
    grad_query = grad_query.astype(jnp.bfloat16)
    grad_key = grad_key.astype(jnp.bfloat16)
    grad_value = grad_value.astype(jnp.bfloat16)
    work = RowSum(row, short, got_mixed, rows, *sems[8:10])
    work.start(
        product(grad_query, attention[0], LAST)
        + product(grad_key, attention[1], LAST)
        + product(grad_value, attention[2], LAST)
    )
    for which, part in enumerate((grad_query, grad_key, grad_value)):
        attention_grads[which] = product(inputs[...], part, FIRST).astype(jnp.bfloat16)
    attention_grads[3] = product(upstream, mixed[...], FIRST).astype(jnp.bfloat16)
    part, gain = norm_back_sums(first[...], gains[0:1], work.finish())
    gain_grads[0:1] = gain
    work = RowSpread(row, mine, every_text, *sems[10:12])
    work.start((grad + part).astype(jnp.bfloat16))
    work.finish()

    def columns(index):
        return every_text.at[:, pl.ds(pl.multiple_of(index * width, 128), width)]

    text_rows[column.me] = columns(column.me)[...]
    exchange(column, columns, lambda index: text_rows.at[index], *sems[12:14])


def encoder_backward(grad_encoded, gains, attention, dense, allowed, kept):
    n = lax.axis_size("dp")
    tokens = grad_encoded.shape[0]
    size = lax.axis_size("img") * lax.axis_size("t")
    whole = pltpu.VMEM((tokens, D), jnp.bfloat16)
    return encoder_call(
        partial(encoder_back_kernel, n, size),
        [
            jax.ShapeDtypeStruct((n, tokens, D // n), jnp.bfloat16),
            jax.ShapeDtypeStruct((8, D), jnp.float32),
            jax.ShapeDtypeStruct(attention.shape, jnp.bfloat16),
            jax.ShapeDtypeStruct(dense.shape, jnp.bfloat16),
        ],
        [whole, pltpu.VMEM((tokens // size, D), jnp.bfloat16)]
        + [whole] * 6
        + semaphores(size) * 6
        + semaphores(n),
        [grad_encoded, gains, attention, dense, allowed, *kept],
        4,
        "encoder_back",
    )


def causal_kernel(query, key, value, mixed, partition):
    length = query.shape[0]
    block = min(256, length)
    scale = HEAD_DIM ** (-0.5)
    halves = head_lanes(query.shape[1])
    for begin in range(0, length, block):
        at, end = pl.ds(begin, block), begin + block
        ahead = lax.broadcasted_iota(jnp.int32, (block, end), 1) > begin + (
            lax.broadcasted_iota(jnp.int32, (block, end), 0)
        )
        out = jnp.zeros((block, query.shape[1]), jnp.float32)
        logs = jnp.zeros((block, query.shape[1]), jnp.float32)
        for lanes in halves:
            scores = product(only(lanes, query[at]), key[:end], LAST) * scale
            scores = jnp.where(ahead, NEGATIVE, scores)
            highest = jnp.max(scores, axis=-1, keepdims=True)
            weight = jnp.exp(scores - highest)
            total = jnp.sum(weight, axis=-1, keepdims=True)
            shares = (weight * (1.0 / total)).astype(jnp.bfloat16)
            out = out + jnp.dot(
                shares, only(lanes, value[:end]), preferred_element_type=jnp.float32
            )
            logs = jnp.where(lanes, highest + jnp.log(total), logs)
        mixed[at] = out.astype(jnp.bfloat16)
        partition[at] = logs


def causal_back_kernel(
    query, key, value, upstream, partition, out_query, out_key, out_value, grad_key, grad_value
):
    length = query.shape[0]
    block = min(256, length)
    scale = HEAD_DIM ** (-0.5)
    halves = head_lanes(query.shape[1])
    grad_key[...] = jnp.zeros(grad_key.shape, jnp.float32)
    grad_value[...] = jnp.zeros(grad_value.shape, jnp.float32)
    for begin in range(0, length, block):
        at, end = pl.ds(begin, block), begin + block
        ahead = lax.broadcasted_iota(jnp.int32, (block, end), 1) > begin + (
            lax.broadcasted_iota(jnp.int32, (block, end), 0)
        )
        grad_query = jnp.zeros((block, query.shape[1]), jnp.float32)
        for head, lanes in enumerate(halves):
            head_query, head_up = only(lanes, query[at]), only(lanes, upstream[at])
            log = partition[at, head * HEAD_DIM : head * HEAD_DIM + 1]
            scores = product(head_query, key[:end], LAST) * scale
            shares = jnp.exp(jnp.where(ahead, NEGATIVE, scores) - log)
            grad_value[:end] += product(shares.astype(jnp.bfloat16), head_up, FIRST)
            grad_shares = product(head_up, value[:end], LAST)
            delta = jnp.sum(shares * grad_shares, axis=-1, keepdims=True)
            grad_scores = (shares * (grad_shares - delta)).astype(jnp.bfloat16)
            grad_query = grad_query + jnp.dot(
                grad_scores, only(lanes, key[:end]), preferred_element_type=jnp.float32
            )
            grad_key[:end] += product(grad_scores, head_query, FIRST)
        out_query[at] = (grad_query * scale).astype(jnp.bfloat16)
    out_key[...] = (grad_key[...] * scale).astype(jnp.bfloat16)
    out_value[...] = grad_value[...].astype(jnp.bfloat16)


def by_heads(kernel, operands, kinds, scratch):
    length, width = operands[0].shape
    lanes = min(128, width)
    spec = pl.BlockSpec((length, lanes), lambda pair: (0, pair))
    return pl.pallas_call(
        kernel,
        grid=(width // lanes,),
        out_shape=[jax.ShapeDtypeStruct((length, width), kind) for kind in kinds],
        in_specs=[spec] * len(operands),
        out_specs=[spec] * len(kinds),
        scratch_shapes=[pltpu.VMEM((length, lanes), jnp.float32)] * scratch,
        compiler_params=pltpu.CompilerParams(vmem_limit_bytes=40 * 2**20),
        cost_estimate=pl.CostEstimate(
            flops=4 * length * length * width, bytes_accessed=2**25, transcendentals=length * length
        ),
        name="causal",
    )(*operands)


def causal_forward(query, key, value):
    return by_heads(causal_kernel, (query, key, value), (jnp.bfloat16, jnp.float32), 0)


def causal_backward(query, key, value, partition, upstream):
    return by_heads(
        causal_back_kernel, (query, key, value, upstream, partition), (jnp.bfloat16,) * 3, 2
    )


def share_kernel(n, size, mine, every, *sems):
    row, column = Row(size), Column(n)
    greet(row, column)
    every[column.me, row.me] = mine[...]
    exchange(row, lambda _: mine, lambda index: every.at[column.me, index], *sems[:2])
    exchange(
        column, lambda _: every.at[column.me], lambda index: every.at[index], *sems[2:]
    )


def share(values):
    n = lax.axis_size("dp")
    size = lax.axis_size("img") * lax.axis_size("t")
    return small_call(
        partial(share_kernel, n, size),
        jax.ShapeDtypeStruct((n, size) + values.shape, values.dtype),
        semaphores(size) + semaphores(n),
        [values],
        7,
        "share",
    )


def total_kernel(n, size, mine, result, row_result, row_got, column_got, part, *sems):
    row, column = Row(size), Column(n)
    greet(row, column)
    row_got[row.me] = mine[...]
    exchange(row, lambda _: mine, lambda index: row_got.at[index], *sems[:2])
    added = row_got[0]
    for index in range(1, size):
        added = added + row_got[index]
    part[...] = added
    column_got[column.me] = added
    exchange(column, lambda _: part, lambda index: column_got.at[index], *sems[2:])
    added = column_got[0]
    for index in range(1, n):
        added = added + column_got[index]
    result[...] = added
    row_result[...] = part[...]


def total_of(values):
    n = lax.axis_size("dp")
    size = lax.axis_size("img") * lax.axis_size("t")
    return small_call(
        partial(total_kernel, n, size),
        [jax.ShapeDtypeStruct(values.shape, values.dtype)] * 2,
        [
            pltpu.VMEM((size,) + values.shape, values.dtype),
            pltpu.VMEM((n,) + values.shape, values.dtype),
            pltpu.VMEM(values.shape, values.dtype),
        ]
        + semaphores(size)
        + semaphores(n),
        [values],
        8,
        "total",
    )


def rms_norm(values, gain):
    return values * lax.rsqrt(jnp.mean(values * values, axis=-1, keepdims=True) + EPS) * gain


def norm_back(values, gain, upstream):
    _, pull = jax.vjp(rms_norm, values, gain)
    return pull(upstream)


def gelu_exact(values):
    return jax.nn.gelu(values, approximate=False)


ROW = ("img", "t")


def spread(values, axis):
    if axis == "t" and lax.axis_size("t") == 2:
        other = lax.ppermute(values, "t", [(0, 1), (1, 0)])
        first = lax.axis_index("t") == 0
        return jnp.concatenate(
            [jnp.where(first, values, other), jnp.where(first, other, values)], axis=0
        )
    return lax.all_gather(values, axis, axis=0, tiled=True)


def collect(values, axis):
    if axis == "t" and lax.axis_size("t") == 2:
        half = values.shape[0] // 2
        place = lax.axis_index("t")
        away = lax.dynamic_slice_in_dim(values, (1 - place) * half, half, 0)
        came = lax.ppermute(away.astype(jnp.bfloat16), "t", [(0, 1), (1, 0)])
        return lax.dynamic_slice_in_dim(values, place * half, half, 0) + came.astype(jnp.float32)
    return lax.psum_scatter(
        values.astype(jnp.bfloat16), axis, scatter_dimension=0, tiled=True
    ).astype(jnp.float32)


def product(left, right, dims):
    return lax.dot_general(left, right, dims, preferred_element_type=jnp.float32)


def split_heads(values, groups):
    return values.reshape(groups, values.shape[0] // groups, values.shape[1] // HEAD_DIM, HEAD_DIM)


def core_forward(query, key, value, allowed, scale):
    scores = jnp.einsum("bqhe,bkhe->bhqk", query, key, preferred_element_type=jnp.float32) * scale
    scores = jnp.where(allowed[:, None], scores, NEGATIVE)
    highest = jnp.max(scores, axis=-1, keepdims=True)
    weight = jnp.exp(scores - highest)
    totals = jnp.sum(weight, axis=-1, keepdims=True)
    shares = (weight / totals).astype(jnp.bfloat16)
    mixed = jnp.einsum("bhqk,bkhe->bqhe", shares, value, preferred_element_type=jnp.float32)
    return (mixed.astype(jnp.bfloat16), highest + jnp.log(totals))


def core_backward(query, key, value, allowed, scale, partition, upstream):
    scores = jnp.einsum("bqhe,bkhe->bhqk", query, key, preferred_element_type=jnp.float32) * scale
    scores = jnp.where(allowed[:, None], scores, NEGATIVE)
    shares = jnp.exp(scores - partition)
    grad_value = jnp.einsum(
        "bhqk,bqhe->bkhe", shares.astype(jnp.bfloat16), upstream, preferred_element_type=jnp.float32
    )
    grad_shares = jnp.einsum("bqhe,bkhe->bhqk", upstream, value, preferred_element_type=jnp.float32)
    inner = jnp.sum(shares * grad_shares, axis=-1, keepdims=True)
    grad_scores = (shares * (grad_shares - inner)).astype(jnp.bfloat16)
    grad_query = (
        jnp.einsum("bhqk,bkhe->bqhe", grad_scores, key, preferred_element_type=jnp.float32) * scale
    )
    grad_key = (
        jnp.einsum("bhqk,bqhe->bkhe", grad_scores, query, preferred_element_type=jnp.float32)
        * scale
    )
    return (grad_query, grad_key, grad_value)


def mix_forward(query, key, value, kind, context):
    scale = HEAD_DIM ** (-0.5)
    width = query.shape[1]
    if kind == "self":
        return causal_forward(query, key, value)
    query, key, value = (split_heads(part, 1) for part in (query, key, value))
    mixed, partition = core_forward(query, key, value, context["allowed"], scale)
    return (mixed.reshape(-1, width), partition)


def mix_backward(query, key, value, partition, upstream, kind, context):
    scale = HEAD_DIM ** (-0.5)
    width = query.shape[1]
    if kind == "self":
        return causal_backward(query, key, value, partition, upstream)
    query, key, value, upstream = (split_heads(part, 1) for part in (query, key, value, upstream))
    grads = core_backward(query, key, value, context["allowed"], scale, partition, upstream)
    return tuple(grad.reshape(-1, width).astype(jnp.bfloat16) for grad in grads)


def attention_forward(values, gain, weights, kind, axis, context, source=None):
    normed = rms_norm(values, gain).astype(jnp.bfloat16)
    inputs = spread(normed, axis)
    if source is None:
        source = inputs
    query = jnp.dot(inputs, weights[0], preferred_element_type=jnp.float32).astype(jnp.bfloat16)
    key = jnp.dot(source, weights[1], preferred_element_type=jnp.float32).astype(jnp.bfloat16)
    value = jnp.dot(source, weights[2], preferred_element_type=jnp.float32).astype(jnp.bfloat16)
    mixed, partition = mix_forward(query, key, value, kind, context)
    output = collect(product(mixed, weights[3], LAST), axis)
    return (output, (inputs, source, query, key, value, mixed, partition))


def attention_backward(upstream, values, gain, weights, kind, axis, context, kept):
    inputs, source, query, key, value, mixed, partition = kept
    grad_rows = spread(upstream.astype(jnp.bfloat16), axis)
    grad_out = product(grad_rows, mixed, FIRST)
    grad_mixed = jnp.dot(grad_rows, weights[3], preferred_element_type=jnp.float32).astype(
        jnp.bfloat16
    )
    grad_query, grad_key, grad_value = mix_backward(
        query, key, value, partition, grad_mixed, kind, context
    )
    grads = [
        product(inputs, grad_query, FIRST).astype(jnp.bfloat16),
        product(source, grad_key, FIRST).astype(jnp.bfloat16),
        product(source, grad_value, FIRST).astype(jnp.bfloat16),
        grad_out.astype(jnp.bfloat16),
    ]
    from_query = product(grad_query, weights[0], LAST)
    from_source = product(grad_key, weights[1], LAST) + product(grad_value, weights[2], LAST)
    if kind == "cross":
        grad_normed = collect(from_query, axis)
    else:
        grad_normed = collect(from_query + from_source, axis)
    grad_values, grad_gain = norm_back(values, gain, grad_normed)
    return (grad_values, grad_gain, grads, from_source)


def dense_forward(values, gain, weights, axis):
    normed = rms_norm(values, gain).astype(jnp.bfloat16)
    inputs = spread(normed, axis)
    hidden = jnp.dot(inputs, weights[0], preferred_element_type=jnp.float32)
    active = gelu_exact(hidden).astype(jnp.bfloat16)
    output = collect(product(active, weights[1], LAST), axis)
    return (output, (inputs, weights, hidden, active))


def dense_backward(upstream, values, gain, axis, kept):
    inputs, matrices, hidden, active = kept
    grad_rows = spread(upstream.astype(jnp.bfloat16), axis)
    grad_active = jnp.dot(grad_rows, matrices[1], preferred_element_type=jnp.float32)
    _, pull = jax.vjp(gelu_exact, hidden)
    grad_hidden = pull(grad_active)[0].astype(jnp.bfloat16)
    grads = [
        product(inputs, grad_hidden, FIRST).astype(jnp.bfloat16),
        product(grad_rows, active, FIRST).astype(jnp.bfloat16),
    ]
    grad_normed = collect(product(grad_hidden, matrices[0], LAST), axis)
    grad_values, grad_gain = norm_back(values, gain, grad_normed)
    return (grad_values, grad_gain, grads)


def code_hits(token_ids, usable, vocab):
    local = token_ids - lax.axis_index(ROW) * vocab
    places = jnp.arange(vocab, dtype=jnp.int32)
    return ((local[:, None] == places[None, :]) & usable[:, None]).astype(jnp.bfloat16)


def code_forward(token_ids, usable, table):
    hits = code_hits(token_ids, usable, table.shape[0])
    picked = jnp.dot(hits, table, preferred_element_type=jnp.float32).astype(jnp.bfloat16)
    return lax.psum_scatter(picked, ROW, scatter_dimension=0, tiled=True).astype(jnp.float32)


def code_backward(upstream, token_ids, usable, vocab):
    rows = lax.all_gather(upstream.astype(jnp.bfloat16), ROW, axis=0, tiled=True)
    return product(code_hits(token_ids, usable, vocab), rows, FIRST)


def merge_stats(first, second):
    highest = jnp.maximum(first[0], second[0])
    mass = first[1] * jnp.exp(first[0] - highest) + second[1] * jnp.exp(second[0] - highest)
    return (highest, mass, first[2] + second[2], first[3] + second[3])


def joined(stats):
    if lax.axis_size("t") == 2:
        other = lax.ppermute(jnp.stack(stats), "t", [(0, 1), (1, 0)])
        return merge_stats(stats, tuple(other))
    every = lax.all_gather(jnp.stack(stats), "t")
    state = tuple(every[0])
    for place in range(1, every.shape[0]):
        state = merge_stats(state, tuple(every[place]))
    return state


def matrices_of(gathered, n):
    count, rows, columns = gathered.shape
    if rows <= D:
        return gathered
    parts = gathered.reshape(count, n, 4, rows // n // 4, columns)
    return jnp.transpose(parts, (0, 1, 3, 2, 4)).reshape(count, rows // 4, 4 * columns)


def blocks_of(matrix, columns, n):
    if columns % 128 == 0:
        return matrix
    rows = matrix.shape[0]
    parts = matrix.reshape(n, rows // n, 4, columns)
    return jnp.transpose(parts, (0, 2, 1, 3)).reshape(4 * rows, columns)


def update(master, moment, average, gradient, factor, rate):
    clipped = gradient * factor
    moment_new = MOMENT * moment + clipped
    master_new = master - rate * (clipped + MOMENT * moment_new)
    average_new = DECAY * average + (1.0 - DECAY) * master_new
    return (master_new, moment_new, average_new, master_new.astype(jnp.bfloat16))


def per_device(
    code_ids,
    code_mask,
    caption_ids,
    caption_segments,
    image_row,
    attention_master,
    attention_momentum,
    attention_average,
    dense_master,
    dense_momentum,
    dense_average,
    text_master,
    text_momentum,
    text_average,
    code_master,
    code_momentum,
    code_average,
    gain_master,
    gain_momentum,
    gain_average,
):
    n = lax.axis_size("dp")
    z, image, part = lax.axis_index("dp"), lax.axis_index("img"), lax.axis_index("t")
    attention_shape = attention_master.shape[1:]
    dense_shape = dense_master.shape[1:]
    code_shape = code_master.shape[1:]
    images, length = code_ids.shape
    caption_rows, caption_length = caption_ids.shape
    text_rows, text_width = text_master.shape
    text_count = caption_ids.size
    mask = code_mask.astype(jnp.float32)
    encoder_attention, encoder_dense, code_table = (
        lax.all_gather(attention_master[0].astype(jnp.bfloat16), "dp", axis=1, tiled=True),
        lax.all_gather(dense_master[0].astype(jnp.bfloat16), "dp", axis=1, tiled=True),
        lax.all_gather(code_master[0].astype(jnp.bfloat16), "dp", axis=1, tiled=True),
    )
    self_weights, cross_weights, dense_weights, out_table = gather(
        [
            attention_master[1].astype(jnp.bfloat16),
            attention_master[2].astype(jnp.bfloat16),
            dense_master[1].astype(jnp.bfloat16),
            code_master[1:2].astype(jnp.bfloat16),
        ],
        [False, False, False, True],
        n,
        1.0,
        0,
    )
    out_table = out_table[0]
    self_weights, cross_weights, dense_weights = (
        matrices_of(weights, n) for weights in (self_weights, cross_weights, dense_weights)
    )
    previous = jnp.concatenate(
        [jnp.zeros((images, 1), jnp.int32), code_ids[:, :-1]], axis=1
    ).reshape(-1)
    starting = jnp.broadcast_to(jnp.arange(length) > 0, (images, length)).reshape(-1)
    code_table, self_weights, mask, encoder_attention, encoder_dense = lax.optimization_barrier(
        (code_table, self_weights, mask, encoder_attention, encoder_dense)
    )
    decoder_in = code_forward(previous, starting, code_table)
    gain_width = gain_master.shape[1]
    note = jnp.zeros((16, 128), jnp.float32)
    note = note.at[:7, :gain_width].set(gain_master)
    note = note.at[7, 0].set(jnp.sum(mask))
    note = note.at[8 : 8 + text_count // 128].set(
        caption_ids.astype(jnp.float32).reshape(-1, 128)
    )
    notes = share(note)
    gain_set = (
        jnp.transpose(notes[:, :, :7, :gain_width], (2, 0, 1, 3))
        .reshape(7, D)
    )
    gain_set = lax.reduce_precision(gain_set, exponent_bits=8, mantissa_bits=7)
    count = jnp.sum(notes[:, 0, 7, 0])
    all_text = notes[:, 0, 8 : 8 + text_count // 128].reshape(-1).astype(jnp.int32)
    segments = caption_segments.reshape(-1)
    same = (segments[:, None] == segments[None, :]).astype(jnp.float32)
    row = jnp.sum(jnp.where(jnp.arange(images) == image, image_row, 0)) - z * caption_rows
    owners = lax.dynamic_index_in_dim(caption_segments, row, 0, False)
    cross_context = {"allowed": (owners == z * images + image)[None, None, :]}
    text_local = all_text - lax.axis_index(ROW) * text_rows
    text_inside = (text_local >= 0) & (text_local < text_rows)
    picked = jnp.take(text_master, jnp.clip(text_local, 0, text_rows - 1), axis=0)
    picked = jnp.where(text_inside[:, None], picked, 0.0).astype(jnp.bfloat16)
    encoder_gains = jnp.concatenate([gain_set, jnp.zeros((1, D), jnp.float32)])
    encoded, encoder_keep = encoder_forward(
        picked.reshape(n, text_count, text_width),
        encoder_gains,
        encoder_attention,
        encoder_dense,
        same,
    )
    decoder_in, encoded = lax.optimization_barrier((decoder_in, encoded))
    caption = lax.dynamic_slice_in_dim(encoded, row * caption_length, caption_length, 0)
    branch, self_keep = attention_forward(
        decoder_in, gain_set[3], self_weights, "self", "t", None
    )
    decoder_one = decoder_in + branch
    branch, cross_keep = attention_forward(
        decoder_one, gain_set[4], cross_weights, "cross", "t", cross_context, caption
    )
    decoder_two = decoder_one + branch
    branch, decoder_dense_keep = dense_forward(decoder_two, gain_set[5], dense_weights, "t")
    decoder_top = decoder_two + branch
    final = spread(rms_norm(decoder_top, gain_set[6]).astype(jnp.bfloat16), "t")
    logits = product(final, out_table, LAST)
    rows = code_shape[0]
    codes = lax.dynamic_index_in_dim(code_ids, image, 0, False)
    held = codes // rows
    local_target = jnp.where(
        held % lax.axis_size("t") == part, held // lax.axis_size("t") * rows + codes % rows, -1
    )
    hits = jnp.arange(logits.shape[1], dtype=jnp.int32)[None, :] == local_target[:, None]
    highest = jnp.max(logits, axis=-1)
    highest, mass, target_logit, logit_total = joined(
        (
            highest,
            jnp.sum(jnp.exp(logits - highest[:, None]), axis=-1),
            jnp.sum(jnp.where(hits, logits, 0.0), axis=-1),
            jnp.sum(logits, axis=-1),
        )
    )
    partition = highest + jnp.log(mass)
    valid = lax.dynamic_index_in_dim(mask, image, 0, False)
    per_token = (
        partition
        - (1.0 - SMOOTH) * target_logit
        - SMOOTH * logit_total / VC
        + Z_WEIGHT * partition * partition
    )
    own_tokens = jnp.where(
        (jnp.arange(images)[:, None] == image) & (part == 0), per_token[None, :], 0.0
    )
    loss_part = jnp.sum(per_token * valid) / lax.axis_size("t")
    weighting = valid / count
    grad_logits = weighting[:, None] * (
        (1.0 + 2.0 * Z_WEIGHT * partition)[:, None] * jnp.exp(logits - partition[:, None])
        - (1.0 - SMOOTH) * hits.astype(jnp.float32)
        - SMOOTH / VC
    )
    grad_logits = grad_logits.astype(jnp.bfloat16)
    grad_out_table = product(grad_logits, final, FIRST).astype(jnp.bfloat16)
    out_grads = lax.psum_scatter(
        lax.psum_scatter(grad_out_table, "img", scatter_dimension=0, tiled=True),
        "dp",
        scatter_dimension=1,
        tiled=True,
    ).astype(jnp.float32)
    grad_final = collect(
        jnp.dot(grad_logits, out_table, preferred_element_type=jnp.float32), "t"
    )
    grad_top, gain_six = norm_back(decoder_top, gain_set[6], grad_final)
    grad_branch, gain_five, dense_one = dense_backward(
        grad_top, decoder_two, gain_set[5], "t", decoder_dense_keep
    )
    grad_two = grad_top + grad_branch
    grad_branch, gain_four, attention_two, grad_caption = attention_backward(
        grad_two, decoder_one, gain_set[4], cross_weights, "cross", "t", cross_context, cross_keep
    )
    grad_one = grad_two + grad_branch
    grad_branch, gain_three, attention_one, _ = attention_backward(
        grad_one, decoder_in, gain_set[3], self_weights, "self", "t", None, self_keep
    )
    grad_start = grad_one + grad_branch
    narrow = attention_shape[2]
    one_grads, two_grads, dense_one_grads = scatter(
        [
            [blocks_of(matrix, narrow, n) for matrix in attention_one],
            [blocks_of(matrix, narrow, n) for matrix in attention_two],
            dense_one,
        ],
        [attention_shape[1:], attention_shape[1:], dense_shape[1:]],
        n,
        1.0,
        2,
    )
    grad_code_in = code_backward(grad_start, previous, starting, code_shape[0])
    grad_encoded = lax.dynamic_update_slice_in_dim(
        jnp.zeros(encoded.shape, jnp.float32), grad_caption, row * caption_length, 0
    )
    text_rows_back, encoder_gain_grads, attention_zero, dense_zero = encoder_backward(
        grad_encoded, encoder_gains, encoder_attention, encoder_dense, same, encoder_keep
    )
    text_hits = jnp.arange(text_rows, dtype=jnp.int32)[:, None] == text_local[None, :]
    text_grads = jnp.dot(
        text_hits.astype(jnp.bfloat16),
        text_rows_back.reshape(-1, text_width),
        preferred_element_type=jnp.float32,
    )

    def owned(values, axis):
        return lax.psum_scatter(
            values.astype(jnp.bfloat16), "dp", scatter_dimension=axis, tiled=True
        ).astype(jnp.float32)

    attention_grads = jnp.stack(
        [
            owned(attention_zero, 1),
            one_grads.reshape(attention_shape),
            two_grads.reshape(attention_shape),
        ]
    )
    dense_grads = jnp.stack([owned(dense_zero, 1), dense_one_grads.reshape(dense_shape)])
    code_grads = jnp.stack([owned(grad_code_in, 1), out_grads.reshape(code_shape)])
    squares = (
        jnp.sum(attention_grads * attention_grads)
        + jnp.sum(dense_grads * dense_grads)
        + jnp.sum(text_grads * text_grads)
        + jnp.sum(code_grads * code_grads)
    )
    sums = jnp.concatenate(
        [
            encoder_gain_grads[:3],
            jnp.stack([gain_three, gain_four, gain_five, gain_six]),
        ]
    )
    tail = jnp.zeros((1, D), jnp.float32).at[0, 0].set(squares).at[0, 1].set(loss_part)
    own_tokens = jnp.concatenate([own_tokens, jnp.zeros((8 - images, D), jnp.float32)])
    sums, row_sums = total_of(jnp.concatenate([sums, tail, own_tokens], axis=0))
    per_image = row_sums[8 : 8 + images]
    gain_sums = sums[:7]
    loss = sums[7, 1] / count
    norm = jnp.sqrt(sums[7, 0] + jnp.sum(gain_sums * gain_sums))
    gain_grads = lax.dynamic_slice_in_dim(
        gain_sums, lax.axis_index(("dp",) + ROW) * gain_width, gain_width, 1
    )
    factor = jnp.minimum(1.0, CLIP / norm)
    rate = 0.012 * math.sqrt(12 * D * D + 4 * D * FF + VT * D + 2 * VC * D + 7 * D) / CLIP
    attention_out = update(
        attention_master, attention_momentum, attention_average, attention_grads, factor, rate
    )
    dense_out = update(dense_master, dense_momentum, dense_average, dense_grads, factor, rate)
    text_out = update(text_master, text_momentum, text_average, text_grads, factor, rate)
    code_out = update(code_master, code_momentum, code_average, code_grads, factor, rate)
    gain_out = update(gain_master, gain_momentum, gain_average, gain_grads, factor, rate)
    return (
        loss,
        norm,
        attention_out[0],
        attention_out[1],
        attention_out[2],
        attention_out[3],
        dense_out[0],
        dense_out[1],
        dense_out[2],
        dense_out[3],
        text_out[0],
        text_out[1],
        text_out[2],
        text_out[3],
        code_out[0],
        code_out[1],
        code_out[2],
        code_out[3],
        gain_out[0],
        gain_out[1],
        gain_out[2],
        gain_out[3],
        per_image,
    )


def solution(mesh):
    n, m = mesh.shape["dp"], mesh.shape["mp"]
    view = Mesh(mesh.devices.reshape(n, 4, m // 4), ("dp",) + ROW)
    return jax.shard_map(
        per_device,
        mesh=view,
        in_specs=(
            P("dp", None),
            P("dp", None),
            P("dp", None),
            P("dp", None),
            P("dp"),
            P(None, None, "dp", ROW),
            P(None, None, "dp", ROW),
            P(None, None, "dp", ROW),
            P(None, None, "dp", ROW),
            P(None, None, "dp", ROW),
            P(None, None, "dp", ROW),
            P(ROW, "dp"),
            P(ROW, "dp"),
            P(ROW, "dp"),
            P(None, ROW, "dp"),
            P(None, ROW, "dp"),
            P(None, ROW, "dp"),
            P(None, ("dp",) + ROW),
            P(None, ("dp",) + ROW),
            P(None, ("dp",) + ROW),
        ),
        out_specs=(
            P(),
            P(),
            P(None, None, "dp", ROW),
            P(None, None, "dp", ROW),
            P(None, None, "dp", ROW),
            P(None, None, "dp", ROW),
            P(None, None, "dp", ROW),
            P(None, None, "dp", ROW),
            P(None, None, "dp", ROW),
            P(None, None, "dp", ROW),
            P(ROW, "dp"),
            P(ROW, "dp"),
            P(ROW, "dp"),
            P(ROW, "dp"),
            P(None, ROW, "dp"),
            P(None, ROW, "dp"),
            P(None, ROW, "dp"),
            P(None, ROW, "dp"),
            P(None, ("dp",) + ROW),
            P(None, ("dp",) + ROW),
            P(None, ("dp",) + ROW),
            P(None, ("dp",) + ROW),
            P("dp", None),
        ),
        check_vma=False,
    )
```

```python
from functools import partial
import math

import jax
import jax.numpy as jnp
from jax import lax
from jax.experimental import pallas as pl
from jax.experimental.pallas import tpu as pltpu
from jax.sharding import Mesh, PartitionSpec as P

D = 1024
HEAD_DIM = 64
FF = 4096
VC = 8192
VT = 16000


EPS = 1e-06
CLIP = 0.01
MOMENT = 0.9
DECAY = 0.75
SMOOTH = 0.1
Z_WEIGHT = 0.01
NEGATIVE = -1e30
LAST = (((1,), (1,)), ((), ()))
FIRST = (((0,), (0,)), ((), ()))


MESH = pl.DeviceIdType.MESH
ORDERS = ((0, 1, 2), (0, 2, 1))


def sources(n):
    return [(far, bits) for far in range(1 - n, n) for bits in range(4)]


def hops(far, bits):
    return abs(far) + (bits & 1) + (bits >> 1)


def arrival(order, far, bits):
    last = None
    for dim in order:
        if (dim == 0 and far != 0) or (dim > 0 and bits & dim):
            last = dim
    return last


def passes(order, far, bits):
    came = arrival(order, far, bits)
    place = -1 if came is None else order.index(came)
    found = [(0, -1 if far > 0 else 1)] if came == 0 else []
    for dim in order[place + 1 :]:
        found += [(0, 1), (0, -1)] if dim == 0 else [(dim, 0)]
    return found


def cut_slabs(shapes, gap):
    slabs = []
    base = 0.0
    for which, (rows, _) in enumerate(shapes):
        count = 4 if rows % 64 == 0 else 2
        for part in range(count):
            size = rows // count
            order = ORDERS[part % len(ORDERS)]
            slabs.append((which, part * size, size, order, base + gap * (part // 2)))
        base += gap * (count // 2)
    return slabs


def wide(shape, table, n):
    _, rows, columns = shape
    if table:
        return (4 * rows, n * columns)
    return (n * rows, 4 * columns) if columns % 128 == 0 else (4 * n * rows, columns)


def placed(whole, shape, table, z, i, begin, rows):
    if table or shape[2] % 128 == 0:
        down, right = (i, z) if table else (z, i)
        return whole.at[
            :,
            pl.ds(pl.multiple_of(down * shape[1] + begin, 16), rows),
            pl.ds(pl.multiple_of(right * shape[2], 128), shape[2]),
        ]
    return whole.at[:, pl.ds(pl.multiple_of((z * 4 + i) * shape[1] + begin, 16), rows)]


class Here:
    def __init__(self, n):
        self.n = n
        self.z = lax.axis_index("dp")
        self.i = lax.axis_index("img")
        self.t = lax.axis_index("t")

    def device(self, dim, step):
        if dim == 0:
            return (self.z + step, self.i, self.t)
        return (self.z, jnp.bitwise_xor(self.i, dim), self.t)

    def below(self):
        return self.z > 0

    def above(self):
        return self.z < self.n - 1

    def side(self, step):
        return self.above() if step > 0 else self.below()

    def greet(self):
        barrier = pltpu.get_barrier_semaphore()

        def tell(device):
            pl.semaphore_signal(barrier, inc=1, device_id=device, device_id_type=MESH)

        pl.when(self.below())(lambda: tell(self.device(0, -1)))
        pl.when(self.above())(lambda: tell(self.device(0, 1)))
        tell(self.device(1, 0))
        tell(self.device(2, 0))
        pl.semaphore_wait(
            barrier, 2 + jnp.where(self.below(), 1, 0) + jnp.where(self.above(), 1, 0)
        )

    def exists(self, far):
        if far == 0:
            return None
        return (self.z + far >= 0) if far < 0 else (self.z + far < self.n)


def guarded(condition, action):
    if condition is None:
        action()
    else:
        pl.when(condition)(action)


def both(first, second):
    if first is None or second is None:
        return second if first is None else first
    return jnp.logical_and(first, second)


def gather_kernel(n, slabs, tables, *refs):
    count = len(tables)
    ins, outs = refs[:count], refs[count : 2 * count]
    send_sem, recv_sem, local_sem = refs[2 * count :]
    here = Here(n)
    here.greet()
    local = []
    for which in range(count):
        shape = ins[which].shape
        copy = pltpu.make_async_copy(
            ins[which],
            placed(outs[which], shape, tables[which], here.z, here.i, 0, shape[1]),
            local_sem.at[which],
        )
        copy.start()
        local.append(copy)

    def block(slab, far, bits):
        which, begin, rows = slabs[slab][:3]
        z, i = here.z + far, jnp.bitwise_xor(here.i, bits)
        return placed(outs[which], ins[which].shape, tables[which], z, i, begin, rows)

    def name(far, bits):
        return (here.z + far) * 4 + jnp.bitwise_xor(here.i, bits)

    def copy_of(slab, far, bits, dim, step):
        which, begin, rows = slabs[slab][:3]
        target = block(slab, far, bits)
        own = far == 0 and bits == 0
        return pltpu.make_async_remote_copy(
            src_ref=ins[which].at[:, pl.ds(begin, rows)] if own else target,
            dst_ref=target,
            send_sem=send_sem.at[slab, name(far, bits), (1 + step) // 2 if dim == 0 else 1 + dim],
            recv_sem=recv_sem.at[slab, name(far, bits)],
            device_id=here.device(dim, step),
            device_id_type=MESH,
        )

    def arrive(slab, far, bits):
        target = block(slab, far, bits)
        pltpu.make_async_remote_copy(
            src_ref=target,
            dst_ref=target,
            send_sem=send_sem.at[slab, 0, 0],
            recv_sem=recv_sem.at[slab, name(far, bits)],
            device_id=here.device(1, 0),
            device_id_type=MESH,
        ).wait_recv()

    events = sorted(
        (slabs[slab][4] + hops(far, bits), slab, far, bits)
        for slab in range(len(slabs))
        for far, bits in sources(n)
    )
    sent = []
    final = []
    for _, slab, far, bits in events:
        onward = passes(slabs[slab][3], far, bits)
        own = far == 0 and bits == 0
        if not onward:
            final.append((slab, far, bits))
            continue

        def act(slab=slab, far=far, bits=bits, onward=onward, own=own):
            if not own:
                arrive(slab, far, bits)
            for dim, step in onward:
                guarded(
                    here.side(step) if dim == 0 else None,
                    lambda dim=dim, step=step: copy_of(slab, far, bits, dim, step).start(),
                )

        guarded(here.exists(far), act)
        sent += [(slab, far, bits, dim, step) for dim, step in onward]
    for slab, far, bits in final:
        guarded(here.exists(far), lambda at=(slab, far, bits): arrive(*at))
    for slab, far, bits, dim, step in sent:
        guarded(
            both(here.exists(far), here.side(step) if dim == 0 else None),
            lambda at=(slab, far, bits, dim, step): copy_of(*at).wait_send(),
        )
    for copy in local:
        copy.wait()


def gather(arrays, tables, n, gap, collective_id):
    count = len(arrays)
    slabs = cut_slabs([a.shape[1:] for a in arrays], gap)
    size = sum(a.size * a.dtype.itemsize for a in arrays) * 4 * n
    return pl.pallas_call(
        partial(gather_kernel, n, slabs, tables),
        out_shape=[
            jax.ShapeDtypeStruct((a.shape[0],) + wide(a.shape, table, n), a.dtype)
            for a, table in zip(arrays, tables)
        ],
        in_specs=[pl.BlockSpec(memory_space=pl.ANY)] * count,
        out_specs=[pl.BlockSpec(memory_space=pl.ANY)] * count,
        scratch_shapes=[
            pltpu.SemaphoreType.DMA((len(slabs), 4 * n, 4)),
            pltpu.SemaphoreType.DMA((len(slabs), 4 * n)),
            pltpu.SemaphoreType.DMA((count,)),
        ],
        compiler_params=pltpu.CompilerParams(
            collective_id=collective_id, has_side_effects=True
        ),
        cost_estimate=pl.CostEstimate(flops=0, bytes_accessed=size * 16, transcendentals=0),
        name="gather",
    )(*arrays)


def places(n, order):
    table = {}
    used = 0
    line = [b for b in range(4) if any(dim == 0 for dim, _ in passes(order, 0, b))]
    for rank, bits in enumerate(line):
        for far in range(1 - n, n):
            for dim, step in passes(order, far, bits):
                if dim == 0:
                    second = far == 0 and step < 0
                    table[far, bits, dim, step] = (
                        (used + n, False) if second else (used + far, True)
                    )
        used += n + 1
    for flip in (1, 2):
        pairs = [p for p in sources(n) if (flip, 0) in passes(order, *p)]
        spread = any(far for far, _ in pairs)
        for bits in sorted({b for _, b in pairs}):
            for far, other in pairs:
                if other == bits:
                    table[far, bits, flip, 0] = (used + far, True) if spread else (used, False)
            used += n if spread else 1
    return table, used


def scatter_kernel(n, slabs, members, *refs):
    total = sum(members)
    count = len(members)
    ins, refs = refs[:total], refs[total:]
    outs, owns, gots = refs[:count], refs[count : 2 * count], refs[2 * count : 3 * count]
    send_sem, recv_sem, local_sem = refs[3 * count :]
    here = Here(n)
    tables = {order: places(n, order)[0] for order in ORDERS}
    loads = []
    for which in range(count):
        for member in range(members[which]):
            matrix = ins[sum(members[:which]) + member]
            rows = owns[which].shape[2] // members[which]
            columns = owns[which].shape[3]
            for z in range(n):
                for i in range(4):
                    copy = pltpu.make_async_copy(
                        matrix.at[pl.ds(z * rows, rows), pl.ds(i * columns, columns)]
                        if matrix.shape[0] == n * rows
                        else matrix.at[pl.ds((z * 4 + i) * rows, rows)],
                        owns[which].at[z, i, pl.ds(member * rows, rows)],
                        local_sem.at[len(loads)],
                    )
                    copy.start()
                    loads.append(copy)
    here.greet()
    for copy in loads:
        copy.wait()

    def own(slab, far, bits):
        which, begin, rows = slabs[slab][:3]
        return owns[which].at[
            here.z + far, jnp.bitwise_xor(here.i, bits), pl.ds(begin, rows)
        ]

    def slot(slab, number):
        which, _, rows, _, _, first = slabs[slab]
        return gots[which].at[pl.ds(pl.multiple_of(first + number * rows, 16), rows)]

    def number_at(order, z, key):
        constant, counts = tables[order][key]
        return constant + z if counts else constant

    def copy_of(slab, far, bits):
        order = slabs[slab][3]
        dim = arrival(order, far, bits)
        step = 0 if dim else (1 if far > 0 else -1)
        number = number_at(order, here.z + step, (far - step, bits ^ dim, dim, -step))
        return pltpu.make_async_remote_copy(
            src_ref=own(slab, far, bits),
            dst_ref=slot(slab, number),
            send_sem=send_sem.at[slab, (here.z + far) * 4 + bits],
            recv_sem=recv_sem.at[slab, number],
            device_id=here.device(dim, step),
            device_id_type=MESH,
        )

    events = sorted(
        (slabs[slab][4] + n + 1 - hops(far, bits), slab, far, bits)
        for slab in range(len(slabs))
        for far, bits in sources(n)
    )

    def add_up(slab, far, bits, parts):
        which, begin, rows, order = slabs[slab][:4]
        numbers = [number_at(order, here.z, (far, bits) + part) for part in parts]
        for number in numbers:
            landed = slot(slab, number)
            pltpu.make_async_remote_copy(
                src_ref=landed,
                dst_ref=landed,
                send_sem=send_sem.at[slab, 0],
                recv_sem=recv_sem.at[slab, number],
                device_id=here.device(1, 0),
                device_id_type=MESH,
            ).wait_recv()
        root = far == 0 and bits == 0
        if not parts and not root:
            return
        mine = own(slab, far, bits)
        landed = [slot(slab, number) for number in numbers]

        @pl.loop(0, rows // 16)
        def _(row):
            at = pl.ds(pl.multiple_of(row * 16, 16), 16)
            added = mine[at].astype(jnp.float32)
            for part in landed:
                added = added + part[at].astype(jnp.float32)
            if root:
                outs[which][pl.ds(pl.multiple_of(begin + row * 16, 16), 16)] = added
            else:
                mine[at] = added.astype(jnp.bfloat16)

    for _, slab, far, bits in events:

        def act(slab=slab, far=far, bits=bits):
            parts = passes(slabs[slab][3], far, bits)
            fixed = [p for p in parts if p[0]]
            line = [p for p in parts if not p[0]]
            if not line:
                add_up(slab, far, bits, fixed)
            elif len(line) == 1:
                there = here.side(line[0][1])
                pl.when(there)(lambda: add_up(slab, far, bits, line + fixed))
                pl.when(jnp.logical_not(there))(lambda: add_up(slab, far, bits, fixed))
            else:
                low, high = here.below(), here.above()
                up, down = line
                pl.when(jnp.logical_and(low, high))(
                    lambda: add_up(slab, far, bits, line + fixed)
                )
                pl.when(jnp.logical_not(low))(lambda: add_up(slab, far, bits, [up] + fixed))
                pl.when(jnp.logical_not(high))(lambda: add_up(slab, far, bits, [down] + fixed))
            if far or bits:
                copy_of(slab, far, bits).start()

        guarded(here.exists(far), act)
    for _, slab, far, bits in events:
        if far or bits:
            guarded(
                here.exists(far),
                lambda at=(slab, far, bits): copy_of(*at).wait_send(),
            )


def scatter(groups, shapes, n, gap, collective_id):
    members = [len(group) for group in groups]
    slabs = []
    totals = [0] * len(groups)
    most = 0
    sizes = [(m * rows, columns) for m, (rows, columns) in zip(members, shapes)]
    for which, begin, rows, order, base in cut_slabs(sizes, gap):
        used = places(n, order)[1]
        slabs.append((which, begin, rows, order, base, totals[which]))
        totals[which] += rows * used
        most = max(most, used)
    size = sum(rows * columns for rows, columns in sizes) * 8 * n
    return pl.pallas_call(
        partial(scatter_kernel, n, slabs, members),
        out_shape=[jax.ShapeDtypeStruct(size, jnp.float32) for size in sizes],
        in_specs=[pl.BlockSpec(memory_space=pl.ANY)] * sum(members),
        out_specs=[pl.BlockSpec(memory_space=pltpu.VMEM)] * len(groups),
        scratch_shapes=[pltpu.VMEM((n, 4) + size, jnp.bfloat16) for size in sizes]
        + [pltpu.VMEM((total, size[1]), jnp.bfloat16) for size, total in zip(sizes, totals)]
        + [
            pltpu.SemaphoreType.DMA((len(slabs), 4 * n)),
            pltpu.SemaphoreType.DMA((len(slabs), most)),
            pltpu.SemaphoreType.DMA((4 * n * sum(members),)),
        ],
        compiler_params=pltpu.CompilerParams(
            collective_id=collective_id, has_side_effects=True, vmem_limit_bytes=58 * 2**20
        ),
        cost_estimate=pl.CostEstimate(flops=0, bytes_accessed=size * 16, transcendentals=0),
        name="scatter",
    )(*[matrix for group in groups for matrix in group])


class Row:
    def __init__(self, size):
        self.size = size
        self.parts = size // 4
        self.me = lax.axis_index("img") * self.parts + lax.axis_index("t")

    def other(self, step):
        return lax.rem(self.me + step, self.size)

    def device(self, index):
        return (lax.axis_index("dp"), index // self.parts, lax.rem(index, self.parts))


class Along:
    def __init__(self, axis, size):
        self.axis, self.size = axis, size
        self.me = lax.axis_index(axis)

    def other(self, step):
        return lax.rem(self.me + step, self.size)

    def device(self, index):
        return tuple(
            index if axis == self.axis else lax.axis_index(axis) for axis in ("dp",) + ROW
        )


def Column(size):
    return Along("dp", size)


def greet(*groups):
    barrier = pltpu.get_barrier_semaphore()
    for group in groups:
        for step in range(1, group.size):
            pl.semaphore_signal(
                barrier, inc=1, device_id=group.device(group.other(step)), device_id_type=MESH
            )
    pl.semaphore_wait(barrier, sum(group.size - 1 for group in groups))


class Exchange:
    def __init__(self, group, source, target, send_sem, recv_sem):
        self.group, self.source, self.target = group, source, target
        self.send_sem, self.recv_sem = send_sem, recv_sem

    def copy_of(self, step):
        index = self.group.other(step)
        return pltpu.make_async_remote_copy(
            src_ref=self.source(index),
            dst_ref=self.target(self.group.me),
            send_sem=self.send_sem.at[step],
            recv_sem=self.recv_sem.at[self.group.me],
            device_id=self.group.device(index),
            device_id_type=MESH,
        )

    def start(self):
        for step in range(1, self.group.size):
            self.copy_of(step).start()
        return self

    def finish(self):
        for step in range(1, self.group.size):
            index = self.group.other(step)
            pltpu.make_async_remote_copy(
                src_ref=self.target(index),
                dst_ref=self.target(index),
                send_sem=self.send_sem.at[step],
                recv_sem=self.recv_sem.at[index],
                device_id=self.group.device(index),
                device_id_type=MESH,
            ).wait_recv()
        for step in range(1, self.group.size):
            self.copy_of(step).wait_send()


def exchange(*parts):
    Exchange(*parts).start().finish()


def row_block(ref, rows, index):
    return ref.at[pl.ds(pl.multiple_of(index * rows, 16), rows)]


def small_call(kernel, out_shape, scratch, operands, collective_id, name):
    vmem = pl.BlockSpec(memory_space=pltpu.VMEM)
    return pl.pallas_call(
        kernel,
        out_shape=out_shape,
        in_specs=[vmem] * len(operands),
        out_specs=[vmem] * len(out_shape) if isinstance(out_shape, list) else vmem,
        scratch_shapes=scratch,
        compiler_params=pltpu.CompilerParams(
            collective_id=collective_id, has_side_effects=True
        ),
        cost_estimate=pl.CostEstimate(flops=0, bytes_accessed=2**24, transcendentals=0),
        name=name,
    )(*operands)


def semaphores(size):
    return [pltpu.SemaphoreType.DMA((size,)), pltpu.SemaphoreType.DMA((size,))]


class RowSpread:
    def __init__(self, row, mine, every, *sems):
        self.mine, self.every, self.rows, self.me = mine, every, mine.shape[0], row.me
        self.work = Exchange(row, lambda _: mine, self.block, *sems)

    def block(self, index):
        return row_block(self.every, self.rows, index)

    def start(self, values):
        self.mine[...] = values
        self.block(self.me)[...] = values
        self.work.start()

    def finish(self):
        self.work.finish()
        return self.every[...]


class RowSum:
    def __init__(self, row, short, got, rows, *sems):
        self.short, self.got, self.rows, self.row = short, got, rows, row
        self.work = Exchange(
            row,
            lambda index: row_block(short, rows, index),
            lambda index: row_block(got, rows, index),
            *sems,
        )

    def start(self, values=None):
        if values is not None:
            self.short[...] = values.astype(jnp.bfloat16)
        mine = row_block(self.short, self.rows, self.row.me)
        row_block(self.got, self.rows, self.row.me)[...] = mine[...]
        self.work.start()

    def finish(self):
        self.work.finish()
        total = self.got[pl.ds(0, self.rows)].astype(jnp.float32)
        for index in range(1, self.row.size):
            total = total + self.got[pl.ds(index * self.rows, self.rows)].astype(jnp.float32)
        return total


def head_lanes(width):
    lanes = lax.broadcasted_iota(jnp.int32, (1, width), 1) // HEAD_DIM
    return [lanes == head for head in range(width // HEAD_DIM)]


def only(lanes, values):
    return jnp.where(lanes, values, jnp.zeros_like(values))


def full_shares(query, key, allowed, lanes):
    scores = product(only(lanes, query), key, LAST) * HEAD_DIM ** (-0.5)
    scores = jnp.where(allowed > 0, scores, NEGATIVE)
    weight = jnp.exp(scores - jnp.max(scores, axis=-1, keepdims=True))
    return weight / jnp.sum(weight, axis=-1, keepdims=True)


def encoder_kernel(
    n, size, picked, gains, attention, dense, allowed,
    encoded, first, middle, top, inputs, query, key, value, mixed, dense_in, hidden, active,
    short, mine, got_text, got_mixed, got_dense, *sems,
):
    row, column = Row(size), Column(n)
    rows, width = first.shape[0], picked.shape[2]
    greet(row, column)

    def columns(index):
        return short.at[:, pl.ds(pl.multiple_of(index * width, 128), width)]

    columns(column.me)[...] = picked[column.me]
    exchange(column, lambda index: picked.at[index], columns, *sems[:2])
    text = RowSum(row, short, got_text, rows, *sems[2:4])
    text.start()
    values = text.finish()
    first[...] = values
    spread_one = RowSpread(row, mine, inputs, *sems[4:6])
    spread_one.start(rms_norm(values, gains[0:1]).astype(jnp.bfloat16))
    every = spread_one.finish()
    query[...] = jnp.dot(
        every, attention[0], preferred_element_type=jnp.float32
    ).astype(jnp.bfloat16)
    key[...] = jnp.dot(every, attention[1], preferred_element_type=jnp.float32).astype(jnp.bfloat16)
    value[...] = jnp.dot(
        every, attention[2], preferred_element_type=jnp.float32
    ).astype(jnp.bfloat16)
    out = jnp.zeros(query.shape, jnp.float32)
    for lanes in head_lanes(query.shape[1]):
        shares = full_shares(query[...], key[...], allowed[...], lanes).astype(jnp.bfloat16)
        out = out + jnp.dot(shares, only(lanes, value[...]), preferred_element_type=jnp.float32)
    mixed[...] = out.astype(jnp.bfloat16)
    branch = RowSum(row, short, got_mixed, rows, *sems[6:8])
    branch.start(product(mixed[...], attention[3], LAST))
    values = values + branch.finish()
    middle[...] = values
    spread_two = RowSpread(row, mine, dense_in, *sems[8:10])
    spread_two.start(rms_norm(values, gains[1:2]).astype(jnp.bfloat16))
    every = spread_two.finish()
    hidden[...] = jnp.dot(every, dense[0], preferred_element_type=jnp.float32)
    inner = hidden[...]
    active[...] = (0.5 * inner * (1.0 + lax.erf(inner * math.sqrt(0.5)))).astype(jnp.bfloat16)
    branch = RowSum(row, short, got_dense, rows, *sems[10:12])
    branch.start(product(active[...], dense[1], LAST))
    values = values + branch.finish()
    top[...] = values
    spread_three = RowSpread(row, mine, encoded, *sems[12:14])
    spread_three.start(rms_norm(values, gains[2:3]).astype(jnp.bfloat16))
    spread_three.finish()


def encoder_call(kernel, out_shape, scratch, operands, collective_id, name):
    vmem = pl.BlockSpec(memory_space=pltpu.VMEM)
    return pl.pallas_call(
        kernel,
        out_shape=out_shape,
        in_specs=[vmem] * len(operands),
        out_specs=[vmem] * len(out_shape),
        scratch_shapes=scratch,
        compiler_params=pltpu.CompilerParams(
            collective_id=collective_id, has_side_effects=True, vmem_limit_bytes=48 * 2**20
        ),
        cost_estimate=pl.CostEstimate(flops=0, bytes_accessed=2**27, transcendentals=0),
        name=name,
    )(*operands)


def encoder_forward(picked, gains, attention, dense, allowed):
    n, tokens, _ = picked.shape
    size = lax.axis_size("img") * lax.axis_size("t")
    width, inner = attention.shape[2], dense.shape[2]
    own = jax.ShapeDtypeStruct((tokens // size, D), jnp.float32)
    every = jax.ShapeDtypeStruct((tokens, D), jnp.bfloat16)
    head = jax.ShapeDtypeStruct((tokens, width), jnp.bfloat16)
    wide_out = [jax.ShapeDtypeStruct((tokens, inner), kind) for kind in (jnp.float32, jnp.bfloat16)]
    whole = pltpu.VMEM((tokens, D), jnp.bfloat16)
    outs = encoder_call(
        partial(encoder_kernel, n, size),
        [every, own, own, own, every, head, head, head, head, every] + wide_out,
        [whole, pltpu.VMEM((tokens // size, D), jnp.bfloat16), whole, whole, whole]
        + semaphores(n)
        + semaphores(size) * 6,
        [picked, gains, attention, dense, allowed],
        3,
        "encoder",
    )
    return outs[0], outs[1:]


def norm_back_sums(values, gain, upstream):
    scale = lax.rsqrt(jnp.mean(values * values, axis=-1, keepdims=True) + EPS)
    unit = values * scale
    inner = upstream * gain
    grad = scale * (inner - unit * jnp.mean(inner * unit, axis=-1, keepdims=True))
    return grad, jnp.sum(upstream * unit, axis=0, keepdims=True)


def encoder_back_kernel(
    n, size, grad_encoded, gains, attention, dense, allowed,
    first, middle, top, inputs, query, key, value, mixed, dense_in, hidden, active,
    text_rows, gain_grads, attention_grads, dense_grads,
    short, mine, got_encoded, got_dense, got_mixed, every_dense, every_mixed, every_text, *sems,
):
    row, column = Row(size), Column(n)
    rows, width = first.shape[0], text_rows.shape[2]
    short[...] = grad_encoded[...].astype(jnp.bfloat16)
    greet(row, column)
    gain_grads[...] = jnp.zeros(gain_grads.shape, jnp.float32)
    work = RowSum(row, short, got_encoded, rows, *sems[:2])
    work.start()
    grad, gain = norm_back_sums(top[...], gains[2:3], work.finish())
    gain_grads[2:3] = gain
    work = RowSpread(row, mine, every_dense, *sems[2:4])
    work.start(grad.astype(jnp.bfloat16))
    upstream = work.finish()
    inner = hidden[...]
    share = 0.5 * (1.0 + lax.erf(inner * math.sqrt(0.5)))
    slope = share + inner * jnp.exp(-0.5 * inner * inner) * (1.0 / math.sqrt(2.0 * math.pi))
    grad_hidden = (
        slope * jnp.dot(upstream, dense[1], preferred_element_type=jnp.float32)
    ).astype(jnp.bfloat16)
    work = RowSum(row, short, got_dense, rows, *sems[4:6])
    work.start(product(grad_hidden, dense[0], LAST))
    dense_grads[0] = product(dense_in[...], grad_hidden, FIRST).astype(jnp.bfloat16)
    dense_grads[1] = product(upstream, active[...], FIRST).astype(jnp.bfloat16)
    part, gain = norm_back_sums(middle[...], gains[1:2], work.finish())
    gain_grads[1:2] = gain
    grad = grad + part
    work = RowSpread(row, mine, every_mixed, *sems[6:8])
    work.start(grad.astype(jnp.bfloat16))
    upstream = work.finish()
    grad_mixed = jnp.dot(upstream, attention[3], preferred_element_type=jnp.float32).astype(
        jnp.bfloat16
    )
    scale = HEAD_DIM ** (-0.5)
    grad_query = grad_key = grad_value = jnp.zeros(query.shape, jnp.float32)
    for lanes in head_lanes(query.shape[1]):
        shares = full_shares(query[...], key[...], allowed[...], lanes)
        head_up = only(lanes, grad_mixed)
        grad_value = grad_value + product(shares.astype(jnp.bfloat16), head_up, FIRST)
        grad_shares = product(head_up, value[...], LAST)
        delta = jnp.sum(shares * grad_shares, axis=-1, keepdims=True)
        grad_scores = (shares * (grad_shares - delta)).astype(jnp.bfloat16)
        grad_query = grad_query + scale * jnp.dot(
            grad_scores, only(lanes, key[...]), preferred_element_type=jnp.float32
        )
        grad_key = grad_key + scale * product(grad_scores, only(lanes, query[...]), FIRST)
    grad_query = grad_query.astype(jnp.bfloat16)
    grad_key = grad_key.astype(jnp.bfloat16)
    grad_value = grad_value.astype(jnp.bfloat16)
    work = RowSum(row, short, got_mixed, rows, *sems[8:10])
    work.start(
        product(grad_query, attention[0], LAST)
        + product(grad_key, attention[1], LAST)
        + product(grad_value, attention[2], LAST)
    )
    for which, part in enumerate((grad_query, grad_key, grad_value)):
        attention_grads[which] = product(inputs[...], part, FIRST).astype(jnp.bfloat16)
    attention_grads[3] = product(upstream, mixed[...], FIRST).astype(jnp.bfloat16)
    part, gain = norm_back_sums(first[...], gains[0:1], work.finish())
    gain_grads[0:1] = gain
    work = RowSpread(row, mine, every_text, *sems[10:12])
    work.start((grad + part).astype(jnp.bfloat16))
    work.finish()

    def columns(index):
        return every_text.at[:, pl.ds(pl.multiple_of(index * width, 128), width)]

    text_rows[column.me] = columns(column.me)[...]
    exchange(column, columns, lambda index: text_rows.at[index], *sems[12:14])


def encoder_backward(grad_encoded, gains, attention, dense, allowed, kept):
    n = lax.axis_size("dp")
    tokens = grad_encoded.shape[0]
    size = lax.axis_size("img") * lax.axis_size("t")
    whole = pltpu.VMEM((tokens, D), jnp.bfloat16)
    return encoder_call(
        partial(encoder_back_kernel, n, size),
        [
            jax.ShapeDtypeStruct((n, tokens, D // n), jnp.bfloat16),
            jax.ShapeDtypeStruct((8, D), jnp.float32),
            jax.ShapeDtypeStruct(attention.shape, jnp.bfloat16),
            jax.ShapeDtypeStruct(dense.shape, jnp.bfloat16),
        ],
        [whole, pltpu.VMEM((tokens // size, D), jnp.bfloat16)]
        + [whole] * 6
        + semaphores(size) * 6
        + semaphores(n),
        [grad_encoded, gains, attention, dense, allowed, *kept],
        4,
        "encoder_back",
    )


def causal_kernel(query, key, value, mixed, partition):
    length = query.shape[0]
    block = min(256, length)
    scale = HEAD_DIM ** (-0.5)
    halves = head_lanes(query.shape[1])
    for begin in range(0, length, block):
        at, end = pl.ds(begin, block), begin + block
        ahead = lax.broadcasted_iota(jnp.int32, (block, end), 1) > begin + (
            lax.broadcasted_iota(jnp.int32, (block, end), 0)
        )
        out = jnp.zeros((block, query.shape[1]), jnp.float32)
        logs = jnp.zeros((block, query.shape[1]), jnp.float32)
        for lanes in halves:
            scores = product(only(lanes, query[at]), key[:end], LAST) * scale
            scores = jnp.where(ahead, NEGATIVE, scores)
            highest = jnp.max(scores, axis=-1, keepdims=True)
            weight = jnp.exp(scores - highest)
            total = jnp.sum(weight, axis=-1, keepdims=True)
            shares = (weight * (1.0 / total)).astype(jnp.bfloat16)
            out = out + jnp.dot(
                shares, only(lanes, value[:end]), preferred_element_type=jnp.float32
            )
            logs = jnp.where(lanes, highest + jnp.log(total), logs)
        mixed[at] = out.astype(jnp.bfloat16)
        partition[at] = logs


def causal_back_kernel(
    query, key, value, upstream, partition, out_query, out_key, out_value, grad_key, grad_value
):
    length = query.shape[0]
    block = min(256, length)
    scale = HEAD_DIM ** (-0.5)
    halves = head_lanes(query.shape[1])
    grad_key[...] = jnp.zeros(grad_key.shape, jnp.float32)
    grad_value[...] = jnp.zeros(grad_value.shape, jnp.float32)
    for begin in range(0, length, block):
        at, end = pl.ds(begin, block), begin + block
        ahead = lax.broadcasted_iota(jnp.int32, (block, end), 1) > begin + (
            lax.broadcasted_iota(jnp.int32, (block, end), 0)
        )
        grad_query = jnp.zeros((block, query.shape[1]), jnp.float32)
        for head, lanes in enumerate(halves):
            head_query, head_up = only(lanes, query[at]), only(lanes, upstream[at])
            log = partition[at, head * HEAD_DIM : head * HEAD_DIM + 1]
            scores = product(head_query, key[:end], LAST) * scale
            shares = jnp.exp(jnp.where(ahead, NEGATIVE, scores) - log)
            grad_value[:end] += product(shares.astype(jnp.bfloat16), head_up, FIRST)
            grad_shares = product(head_up, value[:end], LAST)
            delta = jnp.sum(shares * grad_shares, axis=-1, keepdims=True)
            grad_scores = (shares * (grad_shares - delta)).astype(jnp.bfloat16)
            grad_query = grad_query + jnp.dot(
                grad_scores, only(lanes, key[:end]), preferred_element_type=jnp.float32
            )
            grad_key[:end] += product(grad_scores, head_query, FIRST)
        out_query[at] = (grad_query * scale).astype(jnp.bfloat16)
    out_key[...] = (grad_key[...] * scale).astype(jnp.bfloat16)
    out_value[...] = grad_value[...].astype(jnp.bfloat16)


def by_heads(kernel, operands, kinds, scratch):
    length, width = operands[0].shape
    lanes = min(128, width)
    spec = pl.BlockSpec((length, lanes), lambda pair: (0, pair))
    return pl.pallas_call(
        kernel,
        grid=(width // lanes,),
        out_shape=[jax.ShapeDtypeStruct((length, width), kind) for kind in kinds],
        in_specs=[spec] * len(operands),
        out_specs=[spec] * len(kinds),
        scratch_shapes=[pltpu.VMEM((length, lanes), jnp.float32)] * scratch,
        compiler_params=pltpu.CompilerParams(vmem_limit_bytes=40 * 2**20),
        cost_estimate=pl.CostEstimate(
            flops=4 * length * length * width, bytes_accessed=2**25, transcendentals=length * length
        ),
        name="causal",
    )(*operands)


def causal_forward(query, key, value):
    return by_heads(causal_kernel, (query, key, value), (jnp.bfloat16, jnp.float32), 0)


def causal_backward(query, key, value, partition, upstream):
    return by_heads(
        causal_back_kernel, (query, key, value, upstream, partition), (jnp.bfloat16,) * 3, 2
    )


def share_kernel(n, size, mine, every, *sems):
    row, column = Row(size), Column(n)
    greet(row, column)
    every[column.me, row.me] = mine[...]
    exchange(row, lambda _: mine, lambda index: every.at[column.me, index], *sems[:2])
    exchange(
        column, lambda _: every.at[column.me], lambda index: every.at[index], *sems[2:]
    )


def share(values):
    n = lax.axis_size("dp")
    size = lax.axis_size("img") * lax.axis_size("t")
    return small_call(
        partial(share_kernel, n, size),
        jax.ShapeDtypeStruct((n, size) + values.shape, values.dtype),
        semaphores(size) + semaphores(n),
        [values],
        7,
        "share",
    )


def total_kernel(sizes, mine, result, row_result, *refs):
    groups = [Along(axis, size) for axis, size in sizes]
    parts, gots, sems = refs[:3], refs[3:6], refs[6:]
    greet(*groups)
    parts[0][...] = mine[...]
    for turn, group in enumerate(groups):
        rows = gots[turn].shape[1]
        source = parts[turn].at[pl.ds(0, rows)]
        got = gots[turn]
        got[group.me] = source[...]
        exchange(
            group,
            lambda _, source=source: source,
            lambda index, got=got: got.at[index],
            *sems[2 * turn : 2 * turn + 2],
        )
        added = got[0]
        for index in range(1, group.size):
            added = added + got[index]
        if turn < 2:
            parts[turn + 1][...] = added
        else:
            result[...] = added
    row_result[...] = parts[2][...]


def total_of(values, rows):
    sizes = [(axis, lax.axis_size(axis)) for axis in ("t", "img", "dp")]
    shape = values.shape
    short = (rows, shape[1])
    shapes = [shape, shape, short]
    return small_call(
        partial(total_kernel, sizes),
        [jax.ShapeDtypeStruct(short, values.dtype), jax.ShapeDtypeStruct(shape, values.dtype)],
        [pltpu.VMEM(shape, values.dtype)] * 3
        + [pltpu.VMEM((size,) + part, values.dtype) for (_, size), part in zip(sizes, shapes)]
        + [sem for _, size in sizes for sem in semaphores(size)],
        [values],
        8,
        "total",
    )


def rms_norm(values, gain):
    return values * lax.rsqrt(jnp.mean(values * values, axis=-1, keepdims=True) + EPS) * gain


def norm_back(values, gain, upstream):
    _, pull = jax.vjp(rms_norm, values, gain)
    return pull(upstream)


ROW = ("img", "t")


def spread(values, axis):
    if axis == "t" and lax.axis_size("t") == 2:
        other = lax.ppermute(values, "t", [(0, 1), (1, 0)])
        first = lax.axis_index("t") == 0
        return jnp.concatenate(
            [jnp.where(first, values, other), jnp.where(first, other, values)], axis=0
        )
    return lax.all_gather(values, axis, axis=0, tiled=True)


def collect(values, axis):
    if axis == "t" and lax.axis_size("t") == 2:
        half = values.shape[0] // 2
        place = lax.axis_index("t")
        away = lax.dynamic_slice_in_dim(values, (1 - place) * half, half, 0)
        came = lax.ppermute(away.astype(jnp.bfloat16), "t", [(0, 1), (1, 0)])
        return lax.dynamic_slice_in_dim(values, place * half, half, 0) + came.astype(jnp.float32)
    return lax.psum_scatter(
        values.astype(jnp.bfloat16), axis, scatter_dimension=0, tiled=True
    ).astype(jnp.float32)


def product(left, right, dims):
    return lax.dot_general(left, right, dims, preferred_element_type=jnp.float32)


def split_heads(values, groups):
    return values.reshape(groups, values.shape[0] // groups, values.shape[1] // HEAD_DIM, HEAD_DIM)


def core_forward(query, key, value, allowed, scale):
    scores = jnp.einsum("bqhe,bkhe->bhqk", query, key, preferred_element_type=jnp.float32) * scale
    scores = jnp.where(allowed[:, None], scores, NEGATIVE)
    highest = jnp.max(scores, axis=-1, keepdims=True)
    weight = jnp.exp(scores - highest)
    totals = jnp.sum(weight, axis=-1, keepdims=True)
    shares = (weight / totals).astype(jnp.bfloat16)
    mixed = jnp.einsum("bhqk,bkhe->bqhe", shares, value, preferred_element_type=jnp.float32)
    return (mixed.astype(jnp.bfloat16), highest + jnp.log(totals))


def core_backward(query, key, value, allowed, scale, partition, upstream):
    scores = jnp.einsum("bqhe,bkhe->bhqk", query, key, preferred_element_type=jnp.float32) * scale
    scores = jnp.where(allowed[:, None], scores, NEGATIVE)
    shares = jnp.exp(scores - partition)
    grad_value = jnp.einsum(
        "bhqk,bqhe->bkhe", shares.astype(jnp.bfloat16), upstream, preferred_element_type=jnp.float32
    )
    grad_shares = jnp.einsum("bqhe,bkhe->bhqk", upstream, value, preferred_element_type=jnp.float32)
    inner = jnp.sum(shares * grad_shares, axis=-1, keepdims=True)
    grad_scores = (shares * (grad_shares - inner)).astype(jnp.bfloat16)
    grad_query = (
        jnp.einsum("bhqk,bkhe->bqhe", grad_scores, key, preferred_element_type=jnp.float32) * scale
    )
    grad_key = (
        jnp.einsum("bhqk,bqhe->bkhe", grad_scores, query, preferred_element_type=jnp.float32)
        * scale
    )
    return (grad_query, grad_key, grad_value)


def mix_forward(query, key, value, kind, context):
    scale = HEAD_DIM ** (-0.5)
    width = query.shape[1]
    if kind == "self":
        return causal_forward(query, key, value)
    query, key, value = (split_heads(part, 1) for part in (query, key, value))
    mixed, partition = core_forward(query, key, value, context["allowed"], scale)
    return (mixed.reshape(-1, width), partition)


def mix_backward(query, key, value, partition, upstream, kind, context):
    scale = HEAD_DIM ** (-0.5)
    width = query.shape[1]
    if kind == "self":
        return causal_backward(query, key, value, partition, upstream)
    query, key, value, upstream = (split_heads(part, 1) for part in (query, key, value, upstream))
    grads = core_backward(query, key, value, context["allowed"], scale, partition, upstream)
    return tuple(grad.reshape(-1, width).astype(jnp.bfloat16) for grad in grads)


def attention_forward(values, gain, weights, kind, axis, context, source=None):
    normed = rms_norm(values, gain).astype(jnp.bfloat16)
    inputs = spread(normed, axis)
    if source is None:
        source = inputs
    query = jnp.dot(inputs, weights[0], preferred_element_type=jnp.float32).astype(jnp.bfloat16)
    key = jnp.dot(source, weights[1], preferred_element_type=jnp.float32).astype(jnp.bfloat16)
    value = jnp.dot(source, weights[2], preferred_element_type=jnp.float32).astype(jnp.bfloat16)
    mixed, partition = mix_forward(query, key, value, kind, context)
    output = collect(product(mixed, weights[3], LAST), axis)
    return (output, (inputs, source, query, key, value, mixed, partition))


def attention_backward(upstream, values, gain, weights, kind, axis, context, kept):
    inputs, source, query, key, value, mixed, partition = kept
    grad_rows = spread(upstream.astype(jnp.bfloat16), axis)
    grad_out = product(grad_rows, mixed, FIRST)
    grad_mixed = jnp.dot(grad_rows, weights[3], preferred_element_type=jnp.float32).astype(
        jnp.bfloat16
    )
    grad_query, grad_key, grad_value = mix_backward(
        query, key, value, partition, grad_mixed, kind, context
    )
    grads = [
        product(inputs, grad_query, FIRST).astype(jnp.bfloat16),
        product(source, grad_key, FIRST).astype(jnp.bfloat16),
        product(source, grad_value, FIRST).astype(jnp.bfloat16),
        grad_out.astype(jnp.bfloat16),
    ]
    from_query = product(grad_query, weights[0], LAST)
    from_source = product(grad_key, weights[1], LAST) + product(grad_value, weights[2], LAST)
    if kind == "cross":
        grad_normed = collect(from_query, axis)
    else:
        grad_normed = collect(from_query + from_source, axis)
    grad_values, grad_gain = norm_back(values, gain, grad_normed)
    return (grad_values, grad_gain, grads, from_source)


def dense_forward(values, gain, weights, axis):
    normed = rms_norm(values, gain).astype(jnp.bfloat16)
    inputs = spread(normed, axis)
    hidden = jnp.dot(inputs, weights[0], preferred_element_type=jnp.float32)
    share_below = 0.5 * (1.0 + lax.erf(hidden * math.sqrt(0.5)))
    active = (hidden * share_below).astype(jnp.bfloat16)
    slope = share_below + hidden * jnp.exp(-0.5 * hidden * hidden) * (
        1.0 / math.sqrt(2.0 * math.pi)
    )
    output = collect(product(active, weights[1], LAST), axis)
    return (output, (inputs, weights, slope, active))


def dense_backward(upstream, values, gain, axis, kept):
    inputs, matrices, slope, active = kept
    grad_rows = spread(upstream.astype(jnp.bfloat16), axis)
    grad_active = jnp.dot(grad_rows, matrices[1], preferred_element_type=jnp.float32)
    grad_hidden = (grad_active * slope).astype(jnp.bfloat16)
    grads = [
        product(inputs, grad_hidden, FIRST).astype(jnp.bfloat16),
        product(grad_rows, active, FIRST).astype(jnp.bfloat16),
    ]
    grad_normed = collect(product(grad_hidden, matrices[0], LAST), axis)
    grad_values, grad_gain = norm_back(values, gain, grad_normed)
    return (grad_values, grad_gain, grads)


def code_hits(token_ids, usable, vocab):
    local = token_ids - lax.axis_index(ROW) * vocab
    places = jnp.arange(vocab, dtype=jnp.int32)
    return ((local[:, None] == places[None, :]) & usable[:, None]).astype(jnp.bfloat16)


def code_forward(token_ids, usable, table):
    hits = code_hits(token_ids, usable, table.shape[0])
    picked = jnp.dot(hits, table, preferred_element_type=jnp.float32).astype(jnp.bfloat16)
    return lax.psum_scatter(picked, ROW, scatter_dimension=0, tiled=True).astype(jnp.float32)


def code_backward(upstream, token_ids, usable, vocab):
    rows = lax.all_gather(upstream.astype(jnp.bfloat16), ROW, axis=0, tiled=True)
    return product(code_hits(token_ids, usable, vocab), rows, FIRST)


def merge_stats(first, second):
    highest = jnp.maximum(first[0], second[0])
    mass = first[1] * jnp.exp(first[0] - highest) + second[1] * jnp.exp(second[0] - highest)
    return (highest, mass, first[2] + second[2], first[3] + second[3])


def joined(stats):
    if lax.axis_size("t") == 2:
        other = lax.ppermute(jnp.stack(stats), "t", [(0, 1), (1, 0)])
        return merge_stats(stats, tuple(other))
    every = lax.all_gather(jnp.stack(stats), "t")
    state = tuple(every[0])
    for place in range(1, every.shape[0]):
        state = merge_stats(state, tuple(every[place]))
    return state


def matrices_of(gathered, n):
    count, rows, columns = gathered.shape
    if rows <= D:
        return gathered
    parts = gathered.reshape(count, n, 4, rows // n // 4, columns)
    return jnp.transpose(parts, (0, 1, 3, 2, 4)).reshape(count, rows // 4, 4 * columns)


def blocks_of(matrix, columns, n):
    if columns % 128 == 0:
        return matrix
    rows = matrix.shape[0]
    parts = matrix.reshape(n, rows // n, 4, columns)
    return jnp.transpose(parts, (0, 2, 1, 3)).reshape(4 * rows, columns)


def update(master, moment, average, gradient, factor, rate):
    clipped = gradient * factor
    moment_new = MOMENT * moment + clipped
    master_new = master - rate * (clipped + MOMENT * moment_new)
    average_new = DECAY * average + (1.0 - DECAY) * master_new
    return (master_new, moment_new, average_new, master_new.astype(jnp.bfloat16))


def per_device(
    code_ids,
    code_mask,
    caption_ids,
    caption_segments,
    image_row,
    attention_master,
    attention_momentum,
    attention_average,
    dense_master,
    dense_momentum,
    dense_average,
    text_master,
    text_momentum,
    text_average,
    code_master,
    code_momentum,
    code_average,
    gain_master,
    gain_momentum,
    gain_average,
):
    n = lax.axis_size("dp")
    z, image, part = lax.axis_index("dp"), lax.axis_index("img"), lax.axis_index("t")
    attention_shape = attention_master.shape[1:]
    dense_shape = dense_master.shape[1:]
    code_shape = code_master.shape[1:]
    images, length = code_ids.shape
    caption_rows, caption_length = caption_ids.shape
    text_rows, text_width = text_master.shape
    text_count = caption_ids.size
    mask = code_mask.astype(jnp.float32)
    encoder_attention, encoder_dense, code_table = (
        lax.all_gather(attention_master[0].astype(jnp.bfloat16), "dp", axis=1, tiled=True),
        lax.all_gather(dense_master[0].astype(jnp.bfloat16), "dp", axis=1, tiled=True),
        lax.all_gather(code_master[0].astype(jnp.bfloat16), "dp", axis=1, tiled=True),
    )
    self_weights, cross_weights, dense_weights, out_table = gather(
        [
            attention_master[1].astype(jnp.bfloat16),
            attention_master[2].astype(jnp.bfloat16),
            dense_master[1].astype(jnp.bfloat16),
            code_master[1:2].astype(jnp.bfloat16),
        ],
        [False, False, False, True],
        n,
        1.0,
        0,
    )
    out_table = out_table[0]
    self_weights, cross_weights, dense_weights = (
        matrices_of(weights, n) for weights in (self_weights, cross_weights, dense_weights)
    )
    previous = jnp.concatenate(
        [jnp.zeros((images, 1), jnp.int32), code_ids[:, :-1]], axis=1
    ).reshape(-1)
    starting = jnp.broadcast_to(jnp.arange(length) > 0, (images, length)).reshape(-1)
    code_table, self_weights, encoder_attention, encoder_dense = lax.optimization_barrier(
        (code_table, self_weights, encoder_attention, encoder_dense)
    )
    decoder_in = code_forward(previous, starting, code_table)
    gain_width = gain_master.shape[1]
    note = jnp.zeros((16, 128), jnp.float32)
    note = note.at[:7, :gain_width].set(gain_master)
    note = note.at[7, 0].set(jnp.sum(mask))
    note = note.at[8 : 8 + text_count // 128].set(
        caption_ids.astype(jnp.float32).reshape(-1, 128)
    )
    notes = share(note)
    gain_set = (
        jnp.transpose(notes[:, :, :7, :gain_width], (2, 0, 1, 3))
        .reshape(7, D)
    )
    gain_set = lax.reduce_precision(gain_set, exponent_bits=8, mantissa_bits=7)
    count = jnp.sum(notes[:, 0, 7, 0])
    all_text = notes[:, 0, 8 : 8 + text_count // 128].reshape(-1).astype(jnp.int32)
    segments = caption_segments.reshape(-1)
    same = (segments[:, None] == segments[None, :]).astype(jnp.float32)
    row = jnp.sum(jnp.where(jnp.arange(images) == image, image_row, 0)) - z * caption_rows
    owners = lax.dynamic_index_in_dim(caption_segments, row, 0, False)
    cross_context = {"allowed": (owners == z * images + image)[None, None, :]}
    text_local = all_text - lax.axis_index(ROW) * text_rows
    text_inside = (text_local >= 0) & (text_local < text_rows)
    picked = jnp.take(text_master, jnp.clip(text_local, 0, text_rows - 1), axis=0)
    picked = jnp.where(text_inside[:, None], picked, 0.0).astype(jnp.bfloat16)
    encoder_gains = jnp.concatenate([gain_set, jnp.zeros((1, D), jnp.float32)])
    encoded, encoder_keep = encoder_forward(
        picked.reshape(n, text_count, text_width),
        encoder_gains,
        encoder_attention,
        encoder_dense,
        same,
    )
    decoder_in, encoded = lax.optimization_barrier((decoder_in, encoded))
    caption = lax.dynamic_slice_in_dim(encoded, row * caption_length, caption_length, 0)
    branch, self_keep = attention_forward(
        decoder_in, gain_set[3], self_weights, "self", "t", None
    )
    decoder_one = decoder_in + branch
    branch, cross_keep = attention_forward(
        decoder_one, gain_set[4], cross_weights, "cross", "t", cross_context, caption
    )
    decoder_two = decoder_one + branch
    branch, decoder_dense_keep = dense_forward(decoder_two, gain_set[5], dense_weights, "t")
    decoder_top = decoder_two + branch
    final = spread(rms_norm(decoder_top, gain_set[6]).astype(jnp.bfloat16), "t")
    logits = product(final, out_table, LAST)
    rows = code_shape[0]
    codes = lax.dynamic_index_in_dim(code_ids, image, 0, False)
    held = codes // rows
    local_target = jnp.where(
        held % lax.axis_size("t") == part, held // lax.axis_size("t") * rows + codes % rows, -1
    )
    hits = jnp.arange(logits.shape[1], dtype=jnp.int32)[None, :] == local_target[:, None]
    highest = jnp.max(logits, axis=-1)
    highest, mass, target_logit, logit_total = joined(
        (
            highest,
            jnp.sum(jnp.exp(logits - highest[:, None]), axis=-1),
            jnp.sum(jnp.where(hits, logits, 0.0), axis=-1),
            jnp.sum(logits, axis=-1),
        )
    )
    partition = highest + jnp.log(mass)
    valid = lax.dynamic_index_in_dim(mask, image, 0, False)
    per_token = (
        partition
        - (1.0 - SMOOTH) * target_logit
        - SMOOTH * logit_total / VC
        + Z_WEIGHT * partition * partition
    )
    own_tokens = jnp.where(
        (jnp.arange(images)[:, None] == image) & (part == 0), per_token[None, :], 0.0
    )
    loss_part = jnp.sum(per_token * valid) / lax.axis_size("t")
    weighting = valid / count
    grad_logits = weighting[:, None] * (
        (1.0 + 2.0 * Z_WEIGHT * partition)[:, None] * jnp.exp(logits - partition[:, None])
        - (1.0 - SMOOTH) * hits.astype(jnp.float32)
        - SMOOTH / VC
    )
    grad_logits = grad_logits.astype(jnp.bfloat16)
    grad_out_table = product(grad_logits, final, FIRST).astype(jnp.bfloat16)
    out_grads = lax.psum_scatter(
        lax.psum_scatter(grad_out_table, "img", scatter_dimension=0, tiled=True),
        "dp",
        scatter_dimension=1,
        tiled=True,
    ).astype(jnp.float32)
    grad_final = collect(
        jnp.dot(grad_logits, out_table, preferred_element_type=jnp.float32), "t"
    )
    grad_top, gain_six = norm_back(decoder_top, gain_set[6], grad_final)
    grad_branch, gain_five, dense_one = dense_backward(
        grad_top, decoder_two, gain_set[5], "t", decoder_dense_keep
    )
    grad_two = grad_top + grad_branch
    grad_branch, gain_four, attention_two, grad_caption = attention_backward(
        grad_two, decoder_one, gain_set[4], cross_weights, "cross", "t", cross_context, cross_keep
    )
    grad_one = grad_two + grad_branch
    grad_branch, gain_three, attention_one, _ = attention_backward(
        grad_one, decoder_in, gain_set[3], self_weights, "self", "t", None, self_keep
    )
    grad_start = grad_one + grad_branch
    narrow = attention_shape[2]
    one_grads, two_grads, dense_one_grads = scatter(
        [
            [blocks_of(matrix, narrow, n) for matrix in attention_one],
            [blocks_of(matrix, narrow, n) for matrix in attention_two],
            dense_one,
        ],
        [attention_shape[1:], attention_shape[1:], dense_shape[1:]],
        n,
        1.0,
        2,
    )
    grad_code_in = code_backward(grad_start, previous, starting, code_shape[0])
    grad_encoded = lax.dynamic_update_slice_in_dim(
        jnp.zeros(encoded.shape, jnp.float32), grad_caption, row * caption_length, 0
    )
    text_rows_back, encoder_gain_grads, attention_zero, dense_zero = encoder_backward(
        grad_encoded, encoder_gains, encoder_attention, encoder_dense, same, encoder_keep
    )
    text_hits = jnp.arange(text_rows, dtype=jnp.int32)[:, None] == text_local[None, :]
    text_grads = jnp.dot(
        text_hits.astype(jnp.bfloat16),
        text_rows_back.reshape(-1, text_width),
        preferred_element_type=jnp.float32,
    )

    def owned(values, axis):
        return lax.psum_scatter(
            values.astype(jnp.bfloat16), "dp", scatter_dimension=axis, tiled=True
        ).astype(jnp.float32)

    attention_grads = jnp.stack(
        [
            owned(attention_zero, 1),
            one_grads.reshape(attention_shape),
            two_grads.reshape(attention_shape),
        ]
    )
    dense_grads = jnp.stack([owned(dense_zero, 1), dense_one_grads.reshape(dense_shape)])
    code_grads = jnp.stack([owned(grad_code_in, 1), out_grads.reshape(code_shape)])
    squares = (
        jnp.sum(attention_grads * attention_grads)
        + jnp.sum(dense_grads * dense_grads)
        + jnp.sum(text_grads * text_grads)
        + jnp.sum(code_grads * code_grads)
    )
    sums = jnp.concatenate(
        [
            encoder_gain_grads[:3],
            jnp.stack([gain_three, gain_four, gain_five, gain_six]),
        ]
    )
    tail = jnp.zeros((1, D), jnp.float32).at[0, 0].set(squares).at[0, 1].set(loss_part)
    own_tokens = jnp.concatenate([own_tokens, jnp.zeros((8 - images, D), jnp.float32)])
    sums, row_sums = total_of(jnp.concatenate([sums, tail, own_tokens], axis=0), 8)
    per_image = row_sums[8 : 8 + images]
    gain_sums = sums[:7]
    loss = sums[7, 1] / count
    norm = jnp.sqrt(sums[7, 0] + jnp.sum(gain_sums * gain_sums))
    gain_grads = lax.dynamic_slice_in_dim(
        gain_sums, lax.axis_index(("dp",) + ROW) * gain_width, gain_width, 1
    )
    factor = jnp.minimum(1.0, CLIP / norm)
    rate = 0.012 * math.sqrt(12 * D * D + 4 * D * FF + VT * D + 2 * VC * D + 7 * D) / CLIP
    attention_out = update(
        attention_master, attention_momentum, attention_average, attention_grads, factor, rate
    )
    dense_out = update(dense_master, dense_momentum, dense_average, dense_grads, factor, rate)
    text_out = update(text_master, text_momentum, text_average, text_grads, factor, rate)
    code_out = update(code_master, code_momentum, code_average, code_grads, factor, rate)
    gain_out = update(gain_master, gain_momentum, gain_average, gain_grads, factor, rate)
    return (
        loss,
        norm,
        attention_out[0],
        attention_out[1],
        attention_out[2],
        attention_out[3],
        dense_out[0],
        dense_out[1],
        dense_out[2],
        dense_out[3],
        text_out[0],
        text_out[1],
        text_out[2],
        text_out[3],
        code_out[0],
        code_out[1],
        code_out[2],
        code_out[3],
        gain_out[0],
        gain_out[1],
        gain_out[2],
        gain_out[3],
        per_image,
    )


def solution(mesh):
    n, m = mesh.shape["dp"], mesh.shape["mp"]
    view = Mesh(mesh.devices.reshape(n, 4, m // 4), ("dp",) + ROW)
    return jax.shard_map(
        per_device,
        mesh=view,
        in_specs=(
            P("dp", None),
            P("dp", None),
            P("dp", None),
            P("dp", None),
            P("dp"),
            P(None, None, "dp", ROW),
            P(None, None, "dp", ROW),
            P(None, None, "dp", ROW),
            P(None, None, "dp", ROW),
            P(None, None, "dp", ROW),
            P(None, None, "dp", ROW),
            P(ROW, "dp"),
            P(ROW, "dp"),
            P(ROW, "dp"),
            P(None, ROW, "dp"),
            P(None, ROW, "dp"),
            P(None, ROW, "dp"),
            P(None, ("dp",) + ROW),
            P(None, ("dp",) + ROW),
            P(None, ("dp",) + ROW),
        ),
        out_specs=(
            P(),
            P(),
            P(None, None, "dp", ROW),
            P(None, None, "dp", ROW),
            P(None, None, "dp", ROW),
            P(None, None, "dp", ROW),
            P(None, None, "dp", ROW),
            P(None, None, "dp", ROW),
            P(None, None, "dp", ROW),
            P(None, None, "dp", ROW),
            P(ROW, "dp"),
            P(ROW, "dp"),
            P(ROW, "dp"),
            P(ROW, "dp"),
            P(None, ROW, "dp"),
            P(None, ROW, "dp"),
            P(None, ROW, "dp"),
            P(None, ROW, "dp"),
            P(None, ("dp",) + ROW),
            P(None, ("dp",) + ROW),
            P(None, ("dp",) + ROW),
            P(None, ("dp",) + ROW),
            P("dp", None),
        ),
        check_vma=False,
    )
```

```python
from functools import partial
import math

import jax
import jax.numpy as jnp
from jax import lax
from jax.experimental import pallas as pl
from jax.experimental.pallas import tpu as pltpu
from jax.sharding import Mesh, PartitionSpec as P

D = 1024
HEAD_DIM = 64
FF = 4096
VC = 8192
VT = 16000


EPS = 1e-06
CLIP = 0.01
MOMENT = 0.9
DECAY = 0.75
SMOOTH = 0.1
Z_WEIGHT = 0.01
NEGATIVE = -1e30
LAST = (((1,), (1,)), ((), ()))
FIRST = (((0,), (0,)), ((), ()))


MESH = pl.DeviceIdType.MESH
ORDERS = ((0, 1, 2), (0, 2, 1))


def sources(n):
    return [(far, bits) for far in range(1 - n, n) for bits in range(4)]


def hops(far, bits):
    return abs(far) + (bits & 1) + (bits >> 1)


def arrival(order, far, bits):
    last = None
    for dim in order:
        if (dim == 0 and far != 0) or (dim > 0 and bits & dim):
            last = dim
    return last


def passes(order, far, bits):
    came = arrival(order, far, bits)
    place = -1 if came is None else order.index(came)
    found = [(0, -1 if far > 0 else 1)] if came == 0 else []
    for dim in order[place + 1 :]:
        found += [(0, 1), (0, -1)] if dim == 0 else [(dim, 0)]
    return found


def cut_slabs(shapes, gap):
    slabs = []
    base = 0.0
    for which, (rows, _) in enumerate(shapes):
        size = rows // len(ORDERS)
        for part, order in enumerate(ORDERS):
            slabs.append((which, part * size, size, order, base))
        base += gap
    return slabs


def wide(shape, table, n):
    _, rows, columns = shape
    if table:
        return (4 * rows, n * columns)
    return (n * rows, 4 * columns) if columns % 128 == 0 else (4 * n * rows, columns)


def placed(whole, shape, table, z, i, begin, rows):
    if table or shape[2] % 128 == 0:
        down, right = (i, z) if table else (z, i)
        return whole.at[
            :,
            pl.ds(pl.multiple_of(down * shape[1] + begin, 16), rows),
            pl.ds(pl.multiple_of(right * shape[2], 128), shape[2]),
        ]
    return whole.at[:, pl.ds(pl.multiple_of((z * 4 + i) * shape[1] + begin, 16), rows)]


class Here:
    def __init__(self, n):
        self.n = n
        self.z = lax.axis_index("dp")
        self.i = lax.axis_index("img")
        self.t = lax.axis_index("t")

    def device(self, dim, step):
        if dim == 0:
            return (self.z + step, self.i, self.t)
        return (self.z, jnp.bitwise_xor(self.i, dim), self.t)

    def below(self):
        return self.z > 0

    def above(self):
        return self.z < self.n - 1

    def side(self, step):
        return self.above() if step > 0 else self.below()

    def greet(self):
        barrier = pltpu.get_barrier_semaphore()

        def tell(device):
            pl.semaphore_signal(barrier, inc=1, device_id=device, device_id_type=MESH)

        pl.when(self.below())(lambda: tell(self.device(0, -1)))
        pl.when(self.above())(lambda: tell(self.device(0, 1)))
        tell(self.device(1, 0))
        tell(self.device(2, 0))
        pl.semaphore_wait(
            barrier, 2 + jnp.where(self.below(), 1, 0) + jnp.where(self.above(), 1, 0)
        )

    def exists(self, far):
        if far == 0:
            return None
        return (self.z + far >= 0) if far < 0 else (self.z + far < self.n)


def guarded(condition, action):
    if condition is None:
        action()
    else:
        pl.when(condition)(action)


def both(first, second):
    if first is None or second is None:
        return second if first is None else first
    return jnp.logical_and(first, second)


def gather_kernel(n, slabs, tables, *refs):
    count = len(tables)
    ins, outs = refs[:count], refs[count : 2 * count]
    send_sem, recv_sem, local_sem = refs[2 * count :]
    here = Here(n)
    here.greet()
    local = []
    for which in range(count):
        shape = ins[which].shape
        copy = pltpu.make_async_copy(
            ins[which],
            placed(outs[which], shape, tables[which], here.z, here.i, 0, shape[1]),
            local_sem.at[which],
        )
        copy.start()
        local.append(copy)

    def block(slab, far, bits):
        which, begin, rows = slabs[slab][:3]
        z, i = here.z + far, jnp.bitwise_xor(here.i, bits)
        return placed(outs[which], ins[which].shape, tables[which], z, i, begin, rows)

    def name(far, bits):
        return (here.z + far) * 4 + jnp.bitwise_xor(here.i, bits)

    def copy_of(slab, far, bits, dim, step):
        which, begin, rows = slabs[slab][:3]
        target = block(slab, far, bits)
        own = far == 0 and bits == 0
        return pltpu.make_async_remote_copy(
            src_ref=ins[which].at[:, pl.ds(begin, rows)] if own else target,
            dst_ref=target,
            send_sem=send_sem.at[slab, name(far, bits), (1 + step) // 2 if dim == 0 else 1 + dim],
            recv_sem=recv_sem.at[slab, name(far, bits)],
            device_id=here.device(dim, step),
            device_id_type=MESH,
        )

    def arrive(slab, far, bits):
        target = block(slab, far, bits)
        pltpu.make_async_remote_copy(
            src_ref=target,
            dst_ref=target,
            send_sem=send_sem.at[slab, 0, 0],
            recv_sem=recv_sem.at[slab, name(far, bits)],
            device_id=here.device(1, 0),
            device_id_type=MESH,
        ).wait_recv()

    events = sorted(
        (slabs[slab][4] + hops(far, bits), slab, far, bits)
        for slab in range(len(slabs))
        for far, bits in sources(n)
    )
    sent = []
    final = []
    for _, slab, far, bits in events:
        onward = passes(slabs[slab][3], far, bits)
        own = far == 0 and bits == 0
        if not onward:
            final.append((slab, far, bits))
            continue

        def act(slab=slab, far=far, bits=bits, onward=onward, own=own):
            if not own:
                arrive(slab, far, bits)
            for dim, step in onward:
                guarded(
                    here.side(step) if dim == 0 else None,
                    lambda dim=dim, step=step: copy_of(slab, far, bits, dim, step).start(),
                )

        guarded(here.exists(far), act)
        sent += [(slab, far, bits, dim, step) for dim, step in onward]
    for slab, far, bits in final:
        guarded(here.exists(far), lambda at=(slab, far, bits): arrive(*at))
    for slab, far, bits, dim, step in sent:
        guarded(
            both(here.exists(far), here.side(step) if dim == 0 else None),
            lambda at=(slab, far, bits, dim, step): copy_of(*at).wait_send(),
        )
    for copy in local:
        copy.wait()


def gather(arrays, tables, n, gap, collective_id):
    count = len(arrays)
    slabs = cut_slabs([a.shape[1:] for a in arrays], gap)
    size = sum(a.size * a.dtype.itemsize for a in arrays) * 4 * n
    return pl.pallas_call(
        partial(gather_kernel, n, slabs, tables),
        out_shape=[
            jax.ShapeDtypeStruct((a.shape[0],) + wide(a.shape, table, n), a.dtype)
            for a, table in zip(arrays, tables)
        ],
        in_specs=[pl.BlockSpec(memory_space=pl.ANY)] * count,
        out_specs=[pl.BlockSpec(memory_space=pl.ANY)] * count,
        scratch_shapes=[
            pltpu.SemaphoreType.DMA((len(slabs), 4 * n, 4)),
            pltpu.SemaphoreType.DMA((len(slabs), 4 * n)),
            pltpu.SemaphoreType.DMA((count,)),
        ],
        compiler_params=pltpu.CompilerParams(
            collective_id=collective_id, has_side_effects=True
        ),
        cost_estimate=pl.CostEstimate(flops=0, bytes_accessed=size * 16, transcendentals=0),
        name="gather",
    )(*arrays)


def places(n, order):
    table = {}
    used = 0
    line = [b for b in range(4) if any(dim == 0 for dim, _ in passes(order, 0, b))]
    for rank, bits in enumerate(line):
        for far in range(1 - n, n):
            for dim, step in passes(order, far, bits):
                if dim == 0:
                    second = far == 0 and step < 0
                    table[far, bits, dim, step] = (
                        (used + n, False) if second else (used + far, True)
                    )
        used += n + 1
    for flip in (1, 2):
        pairs = [p for p in sources(n) if (flip, 0) in passes(order, *p)]
        spread = any(far for far, _ in pairs)
        for bits in sorted({b for _, b in pairs}):
            for far, other in pairs:
                if other == bits:
                    table[far, bits, flip, 0] = (used + far, True) if spread else (used, False)
            used += n if spread else 1
    return table, used


def scatter_kernel(n, slabs, members, *refs):
    total = sum(members)
    count = len(members)
    ins, refs = refs[:total], refs[total:]
    outs, owns, gots = refs[:count], refs[count : 2 * count], refs[2 * count : 3 * count]
    send_sem, recv_sem, local_sem = refs[3 * count :]
    here = Here(n)
    tables = {order: places(n, order)[0] for order in ORDERS}
    loads = []
    for which in range(count):
        for member in range(members[which]):
            matrix = ins[sum(members[:which]) + member]
            rows = owns[which].shape[2] // members[which]
            columns = owns[which].shape[3]
            for z in range(n):
                for i in range(4):
                    copy = pltpu.make_async_copy(
                        matrix.at[pl.ds(z * rows, rows), pl.ds(i * columns, columns)]
                        if matrix.shape[0] == n * rows
                        else matrix.at[pl.ds((z * 4 + i) * rows, rows)],
                        owns[which].at[z, i, pl.ds(member * rows, rows)],
                        local_sem.at[len(loads)],
                    )
                    copy.start()
                    loads.append(copy)
    here.greet()
    for copy in loads:
        copy.wait()

    def own(slab, far, bits):
        which, begin, rows = slabs[slab][:3]
        return owns[which].at[
            here.z + far, jnp.bitwise_xor(here.i, bits), pl.ds(begin, rows)
        ]

    def slot(slab, number):
        which, _, rows, _, _, first = slabs[slab]
        return gots[which].at[pl.ds(pl.multiple_of(first + number * rows, 16), rows)]

    def number_at(order, z, key):
        constant, counts = tables[order][key]
        return constant + z if counts else constant

    def copy_of(slab, far, bits):
        order = slabs[slab][3]
        dim = arrival(order, far, bits)
        step = 0 if dim else (1 if far > 0 else -1)
        number = number_at(order, here.z + step, (far - step, bits ^ dim, dim, -step))
        return pltpu.make_async_remote_copy(
            src_ref=own(slab, far, bits),
            dst_ref=slot(slab, number),
            send_sem=send_sem.at[slab, (here.z + far) * 4 + bits],
            recv_sem=recv_sem.at[slab, number],
            device_id=here.device(dim, step),
            device_id_type=MESH,
        )

    events = sorted(
        (slabs[slab][4] + n + 1 - hops(far, bits), slab, far, bits)
        for slab in range(len(slabs))
        for far, bits in sources(n)
    )

    def add_up(slab, far, bits, parts):
        which, begin, rows, order = slabs[slab][:4]
        numbers = [number_at(order, here.z, (far, bits) + part) for part in parts]
        for number in numbers:
            landed = slot(slab, number)
            pltpu.make_async_remote_copy(
                src_ref=landed,
                dst_ref=landed,
                send_sem=send_sem.at[slab, 0],
                recv_sem=recv_sem.at[slab, number],
                device_id=here.device(1, 0),
                device_id_type=MESH,
            ).wait_recv()
        root = far == 0 and bits == 0
        if not parts and not root:
            return
        mine = own(slab, far, bits)
        landed = [slot(slab, number) for number in numbers]

        @pl.loop(0, rows // 16)
        def _(row):
            at = pl.ds(pl.multiple_of(row * 16, 16), 16)
            added = mine[at].astype(jnp.float32)
            for part in landed:
                added = added + part[at].astype(jnp.float32)
            if root:
                outs[which][pl.ds(pl.multiple_of(begin + row * 16, 16), 16)] = added
            else:
                mine[at] = added.astype(jnp.bfloat16)

    for _, slab, far, bits in events:

        def act(slab=slab, far=far, bits=bits):
            parts = passes(slabs[slab][3], far, bits)
            fixed = [p for p in parts if p[0]]
            line = [p for p in parts if not p[0]]
            if not line:
                add_up(slab, far, bits, fixed)
            elif len(line) == 1:
                there = here.side(line[0][1])
                pl.when(there)(lambda: add_up(slab, far, bits, line + fixed))
                pl.when(jnp.logical_not(there))(lambda: add_up(slab, far, bits, fixed))
            else:
                low, high = here.below(), here.above()
                up, down = line
                pl.when(jnp.logical_and(low, high))(
                    lambda: add_up(slab, far, bits, line + fixed)
                )
                pl.when(jnp.logical_not(low))(lambda: add_up(slab, far, bits, [up] + fixed))
                pl.when(jnp.logical_not(high))(lambda: add_up(slab, far, bits, [down] + fixed))
            if far or bits:
                copy_of(slab, far, bits).start()

        guarded(here.exists(far), act)
    for _, slab, far, bits in events:
        if far or bits:
            guarded(
                here.exists(far),
                lambda at=(slab, far, bits): copy_of(*at).wait_send(),
            )


def scatter(groups, shapes, n, gap, collective_id):
    members = [len(group) for group in groups]
    slabs = []
    totals = [0] * len(groups)
    most = 0
    sizes = [(m * rows, columns) for m, (rows, columns) in zip(members, shapes)]
    for which, begin, rows, order, base in cut_slabs(sizes, gap):
        used = places(n, order)[1]
        slabs.append((which, begin, rows, order, base, totals[which]))
        totals[which] += rows * used
        most = max(most, used)
    size = sum(rows * columns for rows, columns in sizes) * 8 * n
    return pl.pallas_call(
        partial(scatter_kernel, n, slabs, members),
        out_shape=[jax.ShapeDtypeStruct(size, jnp.float32) for size in sizes],
        in_specs=[pl.BlockSpec(memory_space=pl.ANY)] * sum(members),
        out_specs=[pl.BlockSpec(memory_space=pltpu.VMEM)] * len(groups),
        scratch_shapes=[pltpu.VMEM((n, 4) + size, jnp.bfloat16) for size in sizes]
        + [pltpu.VMEM((total, size[1]), jnp.bfloat16) for size, total in zip(sizes, totals)]
        + [
            pltpu.SemaphoreType.DMA((len(slabs), 4 * n)),
            pltpu.SemaphoreType.DMA((len(slabs), most)),
            pltpu.SemaphoreType.DMA((4 * n * sum(members),)),
        ],
        compiler_params=pltpu.CompilerParams(
            collective_id=collective_id, has_side_effects=True, vmem_limit_bytes=58 * 2**20
        ),
        cost_estimate=pl.CostEstimate(flops=0, bytes_accessed=size * 16, transcendentals=0),
        name="scatter",
    )(*[matrix for group in groups for matrix in group])


class Row:
    def __init__(self, size):
        self.size = size
        self.parts = size // 4
        self.me = lax.axis_index("img") * self.parts + lax.axis_index("t")

    def other(self, step):
        return lax.rem(self.me + step, self.size)

    def device(self, index):
        return (lax.axis_index("dp"), index // self.parts, lax.rem(index, self.parts))


class Along:
    def __init__(self, axis, size):
        self.axis, self.size = axis, size
        self.me = lax.axis_index(axis)

    def other(self, step):
        return lax.rem(self.me + step, self.size)

    def device(self, index):
        return tuple(
            index if axis == self.axis else lax.axis_index(axis) for axis in ("dp",) + ROW
        )


def Column(size):
    return Along("dp", size)


def greet(*groups):
    barrier = pltpu.get_barrier_semaphore()
    for group in groups:
        for step in range(1, group.size):
            pl.semaphore_signal(
                barrier, inc=1, device_id=group.device(group.other(step)), device_id_type=MESH
            )
    pl.semaphore_wait(barrier, sum(group.size - 1 for group in groups))


class Exchange:
    def __init__(self, group, source, target, send_sem, recv_sem):
        self.group, self.source, self.target = group, source, target
        self.send_sem, self.recv_sem = send_sem, recv_sem

    def copy_of(self, step):
        index = self.group.other(step)
        return pltpu.make_async_remote_copy(
            src_ref=self.source(index),
            dst_ref=self.target(self.group.me),
            send_sem=self.send_sem.at[step],
            recv_sem=self.recv_sem.at[self.group.me],
            device_id=self.group.device(index),
            device_id_type=MESH,
        )

    def start(self):
        for step in range(1, self.group.size):
            self.copy_of(step).start()
        return self

    def finish(self):
        for step in range(1, self.group.size):
            index = self.group.other(step)
            pltpu.make_async_remote_copy(
                src_ref=self.target(index),
                dst_ref=self.target(index),
                send_sem=self.send_sem.at[step],
                recv_sem=self.recv_sem.at[index],
                device_id=self.group.device(index),
                device_id_type=MESH,
            ).wait_recv()
        for step in range(1, self.group.size):
            self.copy_of(step).wait_send()


def exchange(*parts):
    Exchange(*parts).start().finish()


def row_block(ref, rows, index):
    return ref.at[pl.ds(pl.multiple_of(index * rows, 16), rows)]


def small_call(kernel, out_shape, scratch, operands, collective_id, name):
    vmem = pl.BlockSpec(memory_space=pltpu.VMEM)
    return pl.pallas_call(
        kernel,
        out_shape=out_shape,
        in_specs=[vmem] * len(operands),
        out_specs=[vmem] * len(out_shape) if isinstance(out_shape, list) else vmem,
        scratch_shapes=scratch,
        compiler_params=pltpu.CompilerParams(
            collective_id=collective_id, has_side_effects=True
        ),
        cost_estimate=pl.CostEstimate(flops=0, bytes_accessed=2**24, transcendentals=0),
        name=name,
    )(*operands)


def semaphores(size):
    return [pltpu.SemaphoreType.DMA((size,)), pltpu.SemaphoreType.DMA((size,))]


class RowSpread:
    def __init__(self, row, mine, every, *sems):
        self.mine, self.every, self.rows, self.me = mine, every, mine.shape[0], row.me
        self.work = Exchange(row, lambda _: mine, self.block, *sems)

    def block(self, index):
        return row_block(self.every, self.rows, index)

    def start(self, values):
        self.mine[...] = values
        self.block(self.me)[...] = values
        self.work.start()

    def finish(self):
        self.work.finish()
        return self.every[...]


class RowSum:
    def __init__(self, row, short, got, rows, *sems):
        self.short, self.got, self.rows, self.row = short, got, rows, row
        self.work = Exchange(
            row,
            lambda index: row_block(short, rows, index),
            lambda index: row_block(got, rows, index),
            *sems,
        )

    def start(self, values=None):
        if values is not None:
            self.short[...] = values.astype(jnp.bfloat16)
        mine = row_block(self.short, self.rows, self.row.me)
        row_block(self.got, self.rows, self.row.me)[...] = mine[...]
        self.work.start()

    def finish(self):
        self.work.finish()
        total = self.got[pl.ds(0, self.rows)].astype(jnp.float32)
        for index in range(1, self.row.size):
            total = total + self.got[pl.ds(index * self.rows, self.rows)].astype(jnp.float32)
        return total


def head_lanes(width):
    lanes = lax.broadcasted_iota(jnp.int32, (1, width), 1) // HEAD_DIM
    return [lanes == head for head in range(width // HEAD_DIM)]


def only(lanes, values):
    return jnp.where(lanes, values, jnp.zeros_like(values))


def full_shares(query, key, allowed, lanes):
    scores = product(only(lanes, query), key, LAST) * HEAD_DIM ** (-0.5)
    scores = jnp.where(allowed > 0, scores, NEGATIVE)
    weight = jnp.exp(scores - jnp.max(scores, axis=-1, keepdims=True))
    return weight / jnp.sum(weight, axis=-1, keepdims=True)


def encoder_kernel(
    n, size, picked, gains, attention, dense, allowed,
    encoded, first, middle, top, inputs, query, key, value, mixed, dense_in, hidden, active,
    short, mine, got_text, got_mixed, got_dense, *sems,
):
    row, column = Row(size), Column(n)
    rows, width = first.shape[0], picked.shape[2]
    greet(row, column)

    def columns(index):
        return short.at[:, pl.ds(pl.multiple_of(index * width, 128), width)]

    columns(column.me)[...] = picked[column.me]
    exchange(column, lambda index: picked.at[index], columns, *sems[:2])
    text = RowSum(row, short, got_text, rows, *sems[2:4])
    text.start()
    values = text.finish()
    first[...] = values
    spread_one = RowSpread(row, mine, inputs, *sems[4:6])
    spread_one.start(rms_norm(values, gains[0:1]).astype(jnp.bfloat16))
    every = spread_one.finish()
    query[...] = jnp.dot(
        every, attention[0], preferred_element_type=jnp.float32
    ).astype(jnp.bfloat16)
    key[...] = jnp.dot(every, attention[1], preferred_element_type=jnp.float32).astype(jnp.bfloat16)
    value[...] = jnp.dot(
        every, attention[2], preferred_element_type=jnp.float32
    ).astype(jnp.bfloat16)
    out = jnp.zeros(query.shape, jnp.float32)
    for lanes in head_lanes(query.shape[1]):
        shares = full_shares(query[...], key[...], allowed[...], lanes).astype(jnp.bfloat16)
        out = out + jnp.dot(shares, only(lanes, value[...]), preferred_element_type=jnp.float32)
    mixed[...] = out.astype(jnp.bfloat16)
    branch = RowSum(row, short, got_mixed, rows, *sems[6:8])
    branch.start(product(mixed[...], attention[3], LAST))
    values = values + branch.finish()
    middle[...] = values
    spread_two = RowSpread(row, mine, dense_in, *sems[8:10])
    spread_two.start(rms_norm(values, gains[1:2]).astype(jnp.bfloat16))
    every = spread_two.finish()
    hidden[...] = jnp.dot(every, dense[0], preferred_element_type=jnp.float32)
    inner = hidden[...]
    active[...] = (0.5 * inner * (1.0 + lax.erf(inner * math.sqrt(0.5)))).astype(jnp.bfloat16)
    branch = RowSum(row, short, got_dense, rows, *sems[10:12])
    branch.start(product(active[...], dense[1], LAST))
    values = values + branch.finish()
    top[...] = values
    spread_three = RowSpread(row, mine, encoded, *sems[12:14])
    spread_three.start(rms_norm(values, gains[2:3]).astype(jnp.bfloat16))
    spread_three.finish()


def encoder_call(kernel, out_shape, scratch, operands, collective_id, name):
    vmem = pl.BlockSpec(memory_space=pltpu.VMEM)
    return pl.pallas_call(
        kernel,
        out_shape=out_shape,
        in_specs=[vmem] * len(operands),
        out_specs=[vmem] * len(out_shape),
        scratch_shapes=scratch,
        compiler_params=pltpu.CompilerParams(
            collective_id=collective_id, has_side_effects=True, vmem_limit_bytes=48 * 2**20
        ),
        cost_estimate=pl.CostEstimate(flops=0, bytes_accessed=2**27, transcendentals=0),
        name=name,
    )(*operands)


def encoder_forward(picked, gains, attention, dense, allowed):
    n, tokens, _ = picked.shape
    size = lax.axis_size("img") * lax.axis_size("t")
    width, inner = attention.shape[2], dense.shape[2]
    own = jax.ShapeDtypeStruct((tokens // size, D), jnp.float32)
    every = jax.ShapeDtypeStruct((tokens, D), jnp.bfloat16)
    head = jax.ShapeDtypeStruct((tokens, width), jnp.bfloat16)
    wide_out = [jax.ShapeDtypeStruct((tokens, inner), kind) for kind in (jnp.float32, jnp.bfloat16)]
    whole = pltpu.VMEM((tokens, D), jnp.bfloat16)
    outs = encoder_call(
        partial(encoder_kernel, n, size),
        [every, own, own, own, every, head, head, head, head, every] + wide_out,
        [whole, pltpu.VMEM((tokens // size, D), jnp.bfloat16), whole, whole, whole]
        + semaphores(n)
        + semaphores(size) * 6,
        [picked, gains, attention, dense, allowed],
        3,
        "encoder",
    )
    return outs[0], outs[1:]


def norm_back_sums(values, gain, upstream):
    scale = lax.rsqrt(jnp.mean(values * values, axis=-1, keepdims=True) + EPS)
    unit = values * scale
    inner = upstream * gain
    grad = scale * (inner - unit * jnp.mean(inner * unit, axis=-1, keepdims=True))
    return grad, jnp.sum(upstream * unit, axis=0, keepdims=True)


def encoder_back_kernel(
    n, size, grad_encoded, gains, attention, dense, allowed,
    first, middle, top, inputs, query, key, value, mixed, dense_in, hidden, active,
    text_rows, gain_grads, attention_grads, dense_grads,
    short, mine, got_encoded, got_dense, got_mixed, every_dense, every_mixed, every_text, *sems,
):
    row, column = Row(size), Column(n)
    rows, width = first.shape[0], text_rows.shape[2]
    short[...] = grad_encoded[...].astype(jnp.bfloat16)
    greet(row, column)
    gain_grads[...] = jnp.zeros(gain_grads.shape, jnp.float32)
    work = RowSum(row, short, got_encoded, rows, *sems[:2])
    work.start()
    grad, gain = norm_back_sums(top[...], gains[2:3], work.finish())
    gain_grads[2:3] = gain
    work = RowSpread(row, mine, every_dense, *sems[2:4])
    work.start(grad.astype(jnp.bfloat16))
    upstream = work.finish()
    inner = hidden[...]
    share = 0.5 * (1.0 + lax.erf(inner * math.sqrt(0.5)))
    slope = share + inner * jnp.exp(-0.5 * inner * inner) * (1.0 / math.sqrt(2.0 * math.pi))
    grad_hidden = (
        slope * jnp.dot(upstream, dense[1], preferred_element_type=jnp.float32)
    ).astype(jnp.bfloat16)
    work = RowSum(row, short, got_dense, rows, *sems[4:6])
    work.start(product(grad_hidden, dense[0], LAST))
    dense_grads[0] = product(dense_in[...], grad_hidden, FIRST).astype(jnp.bfloat16)
    dense_grads[1] = product(upstream, active[...], FIRST).astype(jnp.bfloat16)
    part, gain = norm_back_sums(middle[...], gains[1:2], work.finish())
    gain_grads[1:2] = gain
    grad = grad + part
    work = RowSpread(row, mine, every_mixed, *sems[6:8])
    work.start(grad.astype(jnp.bfloat16))
    upstream = work.finish()
    grad_mixed = jnp.dot(upstream, attention[3], preferred_element_type=jnp.float32).astype(
        jnp.bfloat16
    )
    scale = HEAD_DIM ** (-0.5)
    grad_query = grad_key = grad_value = jnp.zeros(query.shape, jnp.float32)
    for lanes in head_lanes(query.shape[1]):
        shares = full_shares(query[...], key[...], allowed[...], lanes)
        head_up = only(lanes, grad_mixed)
        grad_value = grad_value + product(shares.astype(jnp.bfloat16), head_up, FIRST)
        grad_shares = product(head_up, value[...], LAST)
        delta = jnp.sum(shares * grad_shares, axis=-1, keepdims=True)
        grad_scores = (shares * (grad_shares - delta)).astype(jnp.bfloat16)
        grad_query = grad_query + scale * jnp.dot(
            grad_scores, only(lanes, key[...]), preferred_element_type=jnp.float32
        )
        grad_key = grad_key + scale * product(grad_scores, only(lanes, query[...]), FIRST)
    grad_query = grad_query.astype(jnp.bfloat16)
    grad_key = grad_key.astype(jnp.bfloat16)
    grad_value = grad_value.astype(jnp.bfloat16)
    work = RowSum(row, short, got_mixed, rows, *sems[8:10])
    work.start(
        product(grad_query, attention[0], LAST)
        + product(grad_key, attention[1], LAST)
        + product(grad_value, attention[2], LAST)
    )
    for which, part in enumerate((grad_query, grad_key, grad_value)):
        attention_grads[which] = product(inputs[...], part, FIRST).astype(jnp.bfloat16)
    attention_grads[3] = product(upstream, mixed[...], FIRST).astype(jnp.bfloat16)
    part, gain = norm_back_sums(first[...], gains[0:1], work.finish())
    gain_grads[0:1] = gain
    work = RowSpread(row, mine, every_text, *sems[10:12])
    work.start((grad + part).astype(jnp.bfloat16))
    work.finish()

    def columns(index):
        return every_text.at[:, pl.ds(pl.multiple_of(index * width, 128), width)]

    text_rows[column.me] = columns(column.me)[...]
    exchange(column, columns, lambda index: text_rows.at[index], *sems[12:14])


def encoder_backward(grad_encoded, gains, attention, dense, allowed, kept):
    n = lax.axis_size("dp")
    tokens = grad_encoded.shape[0]
    size = lax.axis_size("img") * lax.axis_size("t")
    whole = pltpu.VMEM((tokens, D), jnp.bfloat16)
    return encoder_call(
        partial(encoder_back_kernel, n, size),
        [
            jax.ShapeDtypeStruct((n, tokens, D // n), jnp.bfloat16),
            jax.ShapeDtypeStruct((8, D), jnp.float32),
            jax.ShapeDtypeStruct(attention.shape, jnp.bfloat16),
            jax.ShapeDtypeStruct(dense.shape, jnp.bfloat16),
        ],
        [whole, pltpu.VMEM((tokens // size, D), jnp.bfloat16)]
        + [whole] * 6
        + semaphores(size) * 6
        + semaphores(n),
        [grad_encoded, gains, attention, dense, allowed, *kept],
        4,
        "encoder_back",
    )


def causal_kernel(query, key, value, mixed, partition):
    length = query.shape[0]
    block = min(256, length)
    scale = HEAD_DIM ** (-0.5)
    halves = head_lanes(query.shape[1])
    for begin in range(0, length, block):
        at, end = pl.ds(begin, block), begin + block
        ahead = lax.broadcasted_iota(jnp.int32, (block, end), 1) > begin + (
            lax.broadcasted_iota(jnp.int32, (block, end), 0)
        )
        out = jnp.zeros((block, query.shape[1]), jnp.float32)
        logs = jnp.zeros((block, query.shape[1]), jnp.float32)
        for lanes in halves:
            scores = product(only(lanes, query[at]), key[:end], LAST) * scale
            scores = jnp.where(ahead, NEGATIVE, scores)
            highest = jnp.max(scores, axis=-1, keepdims=True)
            weight = jnp.exp(scores - highest)
            total = jnp.sum(weight, axis=-1, keepdims=True)
            shares = (weight * (1.0 / total)).astype(jnp.bfloat16)
            out = out + jnp.dot(
                shares, only(lanes, value[:end]), preferred_element_type=jnp.float32
            )
            logs = jnp.where(lanes, highest + jnp.log(total), logs)
        mixed[at] = out.astype(jnp.bfloat16)
        partition[at] = logs


def causal_back_kernel(
    query, key, value, upstream, partition, out_query, out_key, out_value, grad_key, grad_value
):
    length = query.shape[0]
    block = min(256, length)
    scale = HEAD_DIM ** (-0.5)
    halves = head_lanes(query.shape[1])
    grad_key[...] = jnp.zeros(grad_key.shape, jnp.float32)
    grad_value[...] = jnp.zeros(grad_value.shape, jnp.float32)
    for begin in range(0, length, block):
        at, end = pl.ds(begin, block), begin + block
        ahead = lax.broadcasted_iota(jnp.int32, (block, end), 1) > begin + (
            lax.broadcasted_iota(jnp.int32, (block, end), 0)
        )
        grad_query = jnp.zeros((block, query.shape[1]), jnp.float32)
        for head, lanes in enumerate(halves):
            head_query, head_up = only(lanes, query[at]), only(lanes, upstream[at])
            log = partition[at, head * HEAD_DIM : head * HEAD_DIM + 1]
            scores = product(head_query, key[:end], LAST) * scale
            shares = jnp.exp(jnp.where(ahead, NEGATIVE, scores) - log)
            grad_value[:end] += product(shares.astype(jnp.bfloat16), head_up, FIRST)
            grad_shares = product(head_up, value[:end], LAST)
            delta = jnp.sum(shares * grad_shares, axis=-1, keepdims=True)
            grad_scores = (shares * (grad_shares - delta)).astype(jnp.bfloat16)
            grad_query = grad_query + jnp.dot(
                grad_scores, only(lanes, key[:end]), preferred_element_type=jnp.float32
            )
            grad_key[:end] += product(grad_scores, head_query, FIRST)
        out_query[at] = (grad_query * scale).astype(jnp.bfloat16)
    out_key[...] = (grad_key[...] * scale).astype(jnp.bfloat16)
    out_value[...] = grad_value[...].astype(jnp.bfloat16)


def by_heads(kernel, operands, kinds, scratch):
    length, width = operands[0].shape
    lanes = min(128, width)
    spec = pl.BlockSpec((length, lanes), lambda pair: (0, pair))
    return pl.pallas_call(
        kernel,
        grid=(width // lanes,),
        out_shape=[jax.ShapeDtypeStruct((length, width), kind) for kind in kinds],
        in_specs=[spec] * len(operands),
        out_specs=[spec] * len(kinds),
        scratch_shapes=[pltpu.VMEM((length, lanes), jnp.float32)] * scratch,
        compiler_params=pltpu.CompilerParams(vmem_limit_bytes=40 * 2**20),
        cost_estimate=pl.CostEstimate(
            flops=4 * length * length * width, bytes_accessed=2**25, transcendentals=length * length
        ),
        name="causal",
    )(*operands)


def causal_forward(query, key, value):
    return by_heads(causal_kernel, (query, key, value), (jnp.bfloat16, jnp.float32), 0)


def causal_backward(query, key, value, partition, upstream):
    return by_heads(
        causal_back_kernel, (query, key, value, upstream, partition), (jnp.bfloat16,) * 3, 2
    )


def share_kernel(n, size, mine, every, *sems):
    row, column = Row(size), Column(n)
    greet(row, column)
    every[column.me, row.me] = mine[...]
    exchange(row, lambda _: mine, lambda index: every.at[column.me, index], *sems[:2])
    exchange(
        column, lambda _: every.at[column.me], lambda index: every.at[index], *sems[2:]
    )


def share(values):
    n = lax.axis_size("dp")
    size = lax.axis_size("img") * lax.axis_size("t")
    return small_call(
        partial(share_kernel, n, size),
        jax.ShapeDtypeStruct((n, size) + values.shape, values.dtype),
        semaphores(size) + semaphores(n),
        [values],
        7,
        "share",
    )


def total_kernel(sizes, mine, result, row_result, *refs):
    groups = [Along(axis, size) for axis, size in sizes]
    parts, gots, sems = refs[:3], refs[3:6], refs[6:]
    greet(*groups)
    parts[0][...] = mine[...]
    for turn, group in enumerate(groups):
        rows = gots[turn].shape[1]
        source = parts[turn].at[pl.ds(0, rows)]
        got = gots[turn]
        got[group.me] = source[...]
        exchange(
            group,
            lambda _, source=source: source,
            lambda index, got=got: got.at[index],
            *sems[2 * turn : 2 * turn + 2],
        )
        added = got[0]
        for index in range(1, group.size):
            added = added + got[index]
        if turn < 2:
            parts[turn + 1][...] = added
        else:
            result[...] = added
    row_result[...] = parts[2][...]


def total_of(values, rows):
    sizes = [(axis, lax.axis_size(axis)) for axis in ("t", "img", "dp")]
    shape = values.shape
    short = (rows, shape[1])
    shapes = [shape, shape, short]
    return small_call(
        partial(total_kernel, sizes),
        [jax.ShapeDtypeStruct(short, values.dtype), jax.ShapeDtypeStruct(shape, values.dtype)],
        [pltpu.VMEM(shape, values.dtype)] * 3
        + [pltpu.VMEM((size,) + part, values.dtype) for (_, size), part in zip(sizes, shapes)]
        + [sem for _, size in sizes for sem in semaphores(size)],
        [values],
        8,
        "total",
    )


def rms_norm(values, gain):
    return values * lax.rsqrt(jnp.mean(values * values, axis=-1, keepdims=True) + EPS) * gain


def norm_back(values, gain, upstream):
    _, pull = jax.vjp(rms_norm, values, gain)
    return pull(upstream)


ROW = ("img", "t")


def spread(values, axis):
    if axis == "t" and lax.axis_size("t") == 2:
        other = lax.ppermute(values, "t", [(0, 1), (1, 0)])
        first = lax.axis_index("t") == 0
        return jnp.concatenate(
            [jnp.where(first, values, other), jnp.where(first, other, values)], axis=0
        )
    return lax.all_gather(values, axis, axis=0, tiled=True)


def collect(values, axis):
    if axis == "t" and lax.axis_size("t") == 2:
        half = values.shape[0] // 2
        place = lax.axis_index("t")
        away = lax.dynamic_slice_in_dim(values, (1 - place) * half, half, 0)
        came = lax.ppermute(away.astype(jnp.bfloat16), "t", [(0, 1), (1, 0)])
        return lax.dynamic_slice_in_dim(values, place * half, half, 0) + came.astype(jnp.float32)
    return lax.psum_scatter(
        values.astype(jnp.bfloat16), axis, scatter_dimension=0, tiled=True
    ).astype(jnp.float32)


def product(left, right, dims):
    return lax.dot_general(left, right, dims, preferred_element_type=jnp.float32)


def split_heads(values, groups):
    return values.reshape(groups, values.shape[0] // groups, values.shape[1] // HEAD_DIM, HEAD_DIM)


def core_forward(query, key, value, allowed, scale):
    scores = jnp.einsum("bqhe,bkhe->bhqk", query, key, preferred_element_type=jnp.float32) * scale
    scores = jnp.where(allowed[:, None], scores, NEGATIVE)
    highest = jnp.max(scores, axis=-1, keepdims=True)
    weight = jnp.exp(scores - highest)
    totals = jnp.sum(weight, axis=-1, keepdims=True)
    shares = (weight / totals).astype(jnp.bfloat16)
    mixed = jnp.einsum("bhqk,bkhe->bqhe", shares, value, preferred_element_type=jnp.float32)
    return (mixed.astype(jnp.bfloat16), highest + jnp.log(totals))


def core_backward(query, key, value, allowed, scale, partition, upstream):
    scores = jnp.einsum("bqhe,bkhe->bhqk", query, key, preferred_element_type=jnp.float32) * scale
    scores = jnp.where(allowed[:, None], scores, NEGATIVE)
    shares = jnp.exp(scores - partition)
    grad_value = jnp.einsum(
        "bhqk,bqhe->bkhe", shares.astype(jnp.bfloat16), upstream, preferred_element_type=jnp.float32
    )
    grad_shares = jnp.einsum("bqhe,bkhe->bhqk", upstream, value, preferred_element_type=jnp.float32)
    inner = jnp.sum(shares * grad_shares, axis=-1, keepdims=True)
    grad_scores = (shares * (grad_shares - inner)).astype(jnp.bfloat16)
    grad_query = (
        jnp.einsum("bhqk,bkhe->bqhe", grad_scores, key, preferred_element_type=jnp.float32) * scale
    )
    grad_key = (
        jnp.einsum("bhqk,bqhe->bkhe", grad_scores, query, preferred_element_type=jnp.float32)
        * scale
    )
    return (grad_query, grad_key, grad_value)


def mix_forward(query, key, value, kind, context):
    scale = HEAD_DIM ** (-0.5)
    width = query.shape[1]
    if kind == "self":
        return causal_forward(query, key, value)
    query, key, value = (split_heads(part, 1) for part in (query, key, value))
    mixed, partition = core_forward(query, key, value, context["allowed"], scale)
    return (mixed.reshape(-1, width), partition)


def mix_backward(query, key, value, partition, upstream, kind, context):
    scale = HEAD_DIM ** (-0.5)
    width = query.shape[1]
    if kind == "self":
        return causal_backward(query, key, value, partition, upstream)
    query, key, value, upstream = (split_heads(part, 1) for part in (query, key, value, upstream))
    grads = core_backward(query, key, value, context["allowed"], scale, partition, upstream)
    return tuple(grad.reshape(-1, width).astype(jnp.bfloat16) for grad in grads)


def attention_forward(values, gain, weights, kind, axis, context, source=None):
    normed = rms_norm(values, gain).astype(jnp.bfloat16)
    inputs = spread(normed, axis)
    if source is None:
        source = inputs
    query = jnp.dot(inputs, weights[0], preferred_element_type=jnp.float32).astype(jnp.bfloat16)
    key = jnp.dot(source, weights[1], preferred_element_type=jnp.float32).astype(jnp.bfloat16)
    value = jnp.dot(source, weights[2], preferred_element_type=jnp.float32).astype(jnp.bfloat16)
    mixed, partition = mix_forward(query, key, value, kind, context)
    output = collect(product(mixed, weights[3], LAST), axis)
    return (output, (inputs, source, query, key, value, mixed, partition))


def attention_backward(upstream, values, gain, weights, kind, axis, context, kept):
    inputs, source, query, key, value, mixed, partition = kept
    grad_rows = spread(upstream.astype(jnp.bfloat16), axis)
    grad_out = product(grad_rows, mixed, FIRST)
    grad_mixed = jnp.dot(grad_rows, weights[3], preferred_element_type=jnp.float32).astype(
        jnp.bfloat16
    )
    grad_query, grad_key, grad_value = mix_backward(
        query, key, value, partition, grad_mixed, kind, context
    )
    grads = [
        product(inputs, grad_query, FIRST).astype(jnp.bfloat16),
        product(source, grad_key, FIRST).astype(jnp.bfloat16),
        product(source, grad_value, FIRST).astype(jnp.bfloat16),
        grad_out.astype(jnp.bfloat16),
    ]
    from_query = product(grad_query, weights[0], LAST)
    from_source = product(grad_key, weights[1], LAST) + product(grad_value, weights[2], LAST)
    if kind == "cross":
        grad_normed = collect(from_query, axis)
    else:
        grad_normed = collect(from_query + from_source, axis)
    grad_values, grad_gain = norm_back(values, gain, grad_normed)
    return (grad_values, grad_gain, grads, from_source)


def dense_forward(values, gain, weights, axis):
    normed = rms_norm(values, gain).astype(jnp.bfloat16)
    inputs = spread(normed, axis)
    hidden = jnp.dot(inputs, weights[0], preferred_element_type=jnp.float32)
    share_below = 0.5 * (1.0 + lax.erf(hidden * math.sqrt(0.5)))
    active = (hidden * share_below).astype(jnp.bfloat16)
    slope = share_below + hidden * jnp.exp(-0.5 * hidden * hidden) * (
        1.0 / math.sqrt(2.0 * math.pi)
    )
    output = collect(product(active, weights[1], LAST), axis)
    return (output, (inputs, weights, slope, active))


def dense_backward(upstream, values, gain, axis, kept):
    inputs, matrices, slope, active = kept
    grad_rows = spread(upstream.astype(jnp.bfloat16), axis)
    grad_active = jnp.dot(grad_rows, matrices[1], preferred_element_type=jnp.float32)
    grad_hidden = (grad_active * slope).astype(jnp.bfloat16)
    grads = [
        product(inputs, grad_hidden, FIRST).astype(jnp.bfloat16),
        product(grad_rows, active, FIRST).astype(jnp.bfloat16),
    ]
    grad_normed = collect(product(grad_hidden, matrices[0], LAST), axis)
    grad_values, grad_gain = norm_back(values, gain, grad_normed)
    return (grad_values, grad_gain, grads)


def code_hits(token_ids, usable, vocab):
    local = token_ids - lax.axis_index(ROW) * vocab
    places = jnp.arange(vocab, dtype=jnp.int32)
    return ((local[:, None] == places[None, :]) & usable[:, None]).astype(jnp.bfloat16)


def code_forward(token_ids, usable, table):
    hits = code_hits(token_ids, usable, table.shape[0])
    picked = jnp.dot(hits, table, preferred_element_type=jnp.float32).astype(jnp.bfloat16)
    return lax.psum_scatter(picked, ROW, scatter_dimension=0, tiled=True).astype(jnp.float32)


def code_backward(upstream, token_ids, usable, vocab):
    rows = lax.all_gather(upstream.astype(jnp.bfloat16), ROW, axis=0, tiled=True)
    return product(code_hits(token_ids, usable, vocab), rows, FIRST)


def merge_stats(first, second):
    highest = jnp.maximum(first[0], second[0])
    mass = first[1] * jnp.exp(first[0] - highest) + second[1] * jnp.exp(second[0] - highest)
    return (highest, mass, first[2] + second[2], first[3] + second[3])


def joined(stats):
    if lax.axis_size("t") == 2:
        other = lax.ppermute(jnp.stack(stats), "t", [(0, 1), (1, 0)])
        return merge_stats(stats, tuple(other))
    every = lax.all_gather(jnp.stack(stats), "t")
    state = tuple(every[0])
    for place in range(1, every.shape[0]):
        state = merge_stats(state, tuple(every[place]))
    return state


def matrices_of(gathered, n):
    count, rows, columns = gathered.shape
    if rows <= D:
        return gathered
    parts = gathered.reshape(count, n, 4, rows // n // 4, columns)
    return jnp.transpose(parts, (0, 1, 3, 2, 4)).reshape(count, rows // 4, 4 * columns)


def blocks_of(matrix, columns, n):
    if columns % 128 == 0:
        return matrix
    rows = matrix.shape[0]
    parts = matrix.reshape(n, rows // n, 4, columns)
    return jnp.transpose(parts, (0, 2, 1, 3)).reshape(4 * rows, columns)


def update(master, moment, average, gradient, factor, rate):
    clipped = gradient * factor
    moment_new = MOMENT * moment + clipped
    master_new = master - rate * (clipped + MOMENT * moment_new)
    average_new = DECAY * average + (1.0 - DECAY) * master_new
    return (master_new, moment_new, average_new, master_new.astype(jnp.bfloat16))


def per_device(
    code_ids,
    code_mask,
    caption_ids,
    caption_segments,
    image_row,
    attention_master,
    attention_momentum,
    attention_average,
    dense_master,
    dense_momentum,
    dense_average,
    text_master,
    text_momentum,
    text_average,
    code_master,
    code_momentum,
    code_average,
    gain_master,
    gain_momentum,
    gain_average,
):
    n = lax.axis_size("dp")
    z, image, part = lax.axis_index("dp"), lax.axis_index("img"), lax.axis_index("t")
    attention_shape = attention_master.shape[1:]
    dense_shape = dense_master.shape[1:]
    code_shape = code_master.shape[1:]
    images, length = code_ids.shape
    caption_rows, caption_length = caption_ids.shape
    text_rows, text_width = text_master.shape
    text_count = caption_ids.size
    mask = code_mask.astype(jnp.float32)
    encoder_attention, encoder_dense, code_table = (
        lax.all_gather(attention_master[0].astype(jnp.bfloat16), "dp", axis=1, tiled=True),
        lax.all_gather(dense_master[0].astype(jnp.bfloat16), "dp", axis=1, tiled=True),
        lax.all_gather(code_master[0].astype(jnp.bfloat16), "dp", axis=1, tiled=True),
    )
    self_weights, cross_weights, dense_weights, out_table = gather(
        [
            attention_master[1].astype(jnp.bfloat16),
            attention_master[2].astype(jnp.bfloat16),
            dense_master[1].astype(jnp.bfloat16),
            code_master[1:2].astype(jnp.bfloat16),
        ],
        [False, False, False, True],
        n,
        1.0,
        0,
    )
    out_table = out_table[0]
    self_weights, cross_weights, dense_weights = (
        matrices_of(weights, n) for weights in (self_weights, cross_weights, dense_weights)
    )
    previous = jnp.concatenate(
        [jnp.zeros((images, 1), jnp.int32), code_ids[:, :-1]], axis=1
    ).reshape(-1)
    starting = jnp.broadcast_to(jnp.arange(length) > 0, (images, length)).reshape(-1)
    code_table, self_weights, encoder_attention, encoder_dense = lax.optimization_barrier(
        (code_table, self_weights, encoder_attention, encoder_dense)
    )
    decoder_in = code_forward(previous, starting, code_table)
    gain_width = gain_master.shape[1]
    note = jnp.zeros((16, 128), jnp.float32)
    note = note.at[:7, :gain_width].set(gain_master)
    note = note.at[7, 0].set(jnp.sum(mask))
    note = note.at[8 : 8 + text_count // 128].set(
        caption_ids.astype(jnp.float32).reshape(-1, 128)
    )
    notes = share(note)
    gain_set = (
        jnp.transpose(notes[:, :, :7, :gain_width], (2, 0, 1, 3))
        .reshape(7, D)
    )
    gain_set = lax.reduce_precision(gain_set, exponent_bits=8, mantissa_bits=7)
    count = jnp.sum(notes[:, 0, 7, 0])
    all_text = notes[:, 0, 8 : 8 + text_count // 128].reshape(-1).astype(jnp.int32)
    segments = caption_segments.reshape(-1)
    same = (segments[:, None] == segments[None, :]).astype(jnp.float32)
    row = jnp.sum(jnp.where(jnp.arange(images) == image, image_row, 0)) - z * caption_rows
    owners = lax.dynamic_index_in_dim(caption_segments, row, 0, False)
    cross_context = {"allowed": (owners == z * images + image)[None, None, :]}
    text_local = all_text - lax.axis_index(ROW) * text_rows
    text_inside = (text_local >= 0) & (text_local < text_rows)
    picked = jnp.take(text_master, jnp.clip(text_local, 0, text_rows - 1), axis=0)
    picked = jnp.where(text_inside[:, None], picked, 0.0).astype(jnp.bfloat16)
    encoder_gains = jnp.concatenate([gain_set, jnp.zeros((1, D), jnp.float32)])
    encoded, encoder_keep = encoder_forward(
        picked.reshape(n, text_count, text_width),
        encoder_gains,
        encoder_attention,
        encoder_dense,
        same,
    )
    decoder_in, encoded = lax.optimization_barrier((decoder_in, encoded))
    caption = lax.dynamic_slice_in_dim(encoded, row * caption_length, caption_length, 0)
    branch, self_keep = attention_forward(
        decoder_in, gain_set[3], self_weights, "self", "t", None
    )
    decoder_one = decoder_in + branch
    branch, cross_keep = attention_forward(
        decoder_one, gain_set[4], cross_weights, "cross", "t", cross_context, caption
    )
    decoder_two = decoder_one + branch
    branch, decoder_dense_keep = dense_forward(decoder_two, gain_set[5], dense_weights, "t")
    decoder_top = decoder_two + branch
    final = spread(rms_norm(decoder_top, gain_set[6]).astype(jnp.bfloat16), "t")
    logits = product(final, out_table, LAST)
    rows = code_shape[0]
    codes = lax.dynamic_index_in_dim(code_ids, image, 0, False)
    held = codes // rows
    local_target = jnp.where(
        held % lax.axis_size("t") == part, held // lax.axis_size("t") * rows + codes % rows, -1
    )
    hits = jnp.arange(logits.shape[1], dtype=jnp.int32)[None, :] == local_target[:, None]
    highest = jnp.max(logits, axis=-1)
    highest, mass, target_logit, logit_total = joined(
        (
            highest,
            jnp.sum(jnp.exp(logits - highest[:, None]), axis=-1),
            jnp.sum(jnp.where(hits, logits, 0.0), axis=-1),
            jnp.sum(logits, axis=-1),
        )
    )
    partition = highest + jnp.log(mass)
    valid = lax.dynamic_index_in_dim(mask, image, 0, False)
    per_token = (
        partition
        - (1.0 - SMOOTH) * target_logit
        - SMOOTH * logit_total / VC
        + Z_WEIGHT * partition * partition
    )
    own_tokens = jnp.where(
        (jnp.arange(images)[:, None] == image) & (part == 0), per_token[None, :], 0.0
    )
    loss_part = jnp.sum(per_token * valid) / lax.axis_size("t")
    weighting = valid / count
    grad_logits = weighting[:, None] * (
        (1.0 + 2.0 * Z_WEIGHT * partition)[:, None] * jnp.exp(logits - partition[:, None])
        - (1.0 - SMOOTH) * hits.astype(jnp.float32)
        - SMOOTH / VC
    )
    grad_logits = grad_logits.astype(jnp.bfloat16)
    grad_out_table = product(grad_logits, final, FIRST).astype(jnp.bfloat16)
    out_grads = lax.psum_scatter(
        lax.psum_scatter(grad_out_table, "img", scatter_dimension=0, tiled=True),
        "dp",
        scatter_dimension=1,
        tiled=True,
    ).astype(jnp.float32)
    grad_final = collect(
        jnp.dot(grad_logits, out_table, preferred_element_type=jnp.float32), "t"
    )
    grad_top, gain_six = norm_back(decoder_top, gain_set[6], grad_final)
    grad_branch, gain_five, dense_one = dense_backward(
        grad_top, decoder_two, gain_set[5], "t", decoder_dense_keep
    )
    grad_two = grad_top + grad_branch
    grad_branch, gain_four, attention_two, grad_caption = attention_backward(
        grad_two, decoder_one, gain_set[4], cross_weights, "cross", "t", cross_context, cross_keep
    )
    grad_one = grad_two + grad_branch
    grad_branch, gain_three, attention_one, _ = attention_backward(
        grad_one, decoder_in, gain_set[3], self_weights, "self", "t", None, self_keep
    )
    grad_start = grad_one + grad_branch
    narrow = attention_shape[2]
    one_grads, two_grads, dense_one_grads = scatter(
        [
            [blocks_of(matrix, narrow, n) for matrix in attention_one],
            [blocks_of(matrix, narrow, n) for matrix in attention_two],
            dense_one,
        ],
        [attention_shape[1:], attention_shape[1:], dense_shape[1:]],
        n,
        1.0,
        2,
    )
    grad_code_in = code_backward(grad_start, previous, starting, code_shape[0])
    grad_encoded = lax.dynamic_update_slice_in_dim(
        jnp.zeros(encoded.shape, jnp.float32), grad_caption, row * caption_length, 0
    )
    text_rows_back, encoder_gain_grads, attention_zero, dense_zero = encoder_backward(
        grad_encoded, encoder_gains, encoder_attention, encoder_dense, same, encoder_keep
    )
    text_hits = jnp.arange(text_rows, dtype=jnp.int32)[:, None] == text_local[None, :]
    text_grads = jnp.dot(
        text_hits.astype(jnp.bfloat16),
        text_rows_back.reshape(-1, text_width),
        preferred_element_type=jnp.float32,
    )

    def owned(values, axis):
        return lax.psum_scatter(
            values.astype(jnp.bfloat16), "dp", scatter_dimension=axis, tiled=True
        ).astype(jnp.float32)

    attention_grads = jnp.stack(
        [
            owned(attention_zero, 1),
            one_grads.reshape(attention_shape),
            two_grads.reshape(attention_shape),
        ]
    )
    dense_grads = jnp.stack([owned(dense_zero, 1), dense_one_grads.reshape(dense_shape)])
    code_grads = jnp.stack([owned(grad_code_in, 1), out_grads.reshape(code_shape)])
    squares = (
        jnp.sum(attention_grads * attention_grads)
        + jnp.sum(dense_grads * dense_grads)
        + jnp.sum(text_grads * text_grads)
        + jnp.sum(code_grads * code_grads)
    )
    sums = jnp.concatenate(
        [
            encoder_gain_grads[:3],
            jnp.stack([gain_three, gain_four, gain_five, gain_six]),
        ]
    )
    tail = jnp.zeros((1, D), jnp.float32).at[0, 0].set(squares).at[0, 1].set(loss_part)
    own_tokens = jnp.concatenate([own_tokens, jnp.zeros((8 - images, D), jnp.float32)])
    sums, row_sums = total_of(jnp.concatenate([sums, tail, own_tokens], axis=0), 8)
    per_image = row_sums[8 : 8 + images]
    gain_sums = sums[:7]
    loss = sums[7, 1] / count
    norm = jnp.sqrt(sums[7, 0] + jnp.sum(gain_sums * gain_sums))
    gain_grads = lax.dynamic_slice_in_dim(
        gain_sums, lax.axis_index(("dp",) + ROW) * gain_width, gain_width, 1
    )
    factor = jnp.minimum(1.0, CLIP / norm)
    rate = 0.012 * math.sqrt(12 * D * D + 4 * D * FF + VT * D + 2 * VC * D + 7 * D) / CLIP
    attention_out = update(
        attention_master, attention_momentum, attention_average, attention_grads, factor, rate
    )
    dense_out = update(dense_master, dense_momentum, dense_average, dense_grads, factor, rate)
    text_out = update(text_master, text_momentum, text_average, text_grads, factor, rate)
    code_out = update(code_master, code_momentum, code_average, code_grads, factor, rate)
    gain_out = update(gain_master, gain_momentum, gain_average, gain_grads, factor, rate)
    return (
        loss,
        norm,
        attention_out[0],
        attention_out[1],
        attention_out[2],
        attention_out[3],
        dense_out[0],
        dense_out[1],
        dense_out[2],
        dense_out[3],
        text_out[0],
        text_out[1],
        text_out[2],
        text_out[3],
        code_out[0],
        code_out[1],
        code_out[2],
        code_out[3],
        gain_out[0],
        gain_out[1],
        gain_out[2],
        gain_out[3],
        per_image,
    )


def solution(mesh):
    n, m = mesh.shape["dp"], mesh.shape["mp"]
    view = Mesh(mesh.devices.reshape(n, 4, m // 4), ("dp",) + ROW)
    return jax.shard_map(
        per_device,
        mesh=view,
        in_specs=(
            P("dp", None),
            P("dp", None),
            P("dp", None),
            P("dp", None),
            P("dp"),
            P(None, None, "dp", ROW),
            P(None, None, "dp", ROW),
            P(None, None, "dp", ROW),
            P(None, None, "dp", ROW),
            P(None, None, "dp", ROW),
            P(None, None, "dp", ROW),
            P(ROW, "dp"),
            P(ROW, "dp"),
            P(ROW, "dp"),
            P(None, ROW, "dp"),
            P(None, ROW, "dp"),
            P(None, ROW, "dp"),
            P(None, ("dp",) + ROW),
            P(None, ("dp",) + ROW),
            P(None, ("dp",) + ROW),
        ),
        out_specs=(
            P(),
            P(),
            P(None, None, "dp", ROW),
            P(None, None, "dp", ROW),
            P(None, None, "dp", ROW),
            P(None, None, "dp", ROW),
            P(None, None, "dp", ROW),
            P(None, None, "dp", ROW),
            P(None, None, "dp", ROW),
            P(None, None, "dp", ROW),
            P(ROW, "dp"),
            P(ROW, "dp"),
            P(ROW, "dp"),
            P(ROW, "dp"),
            P(None, ROW, "dp"),
            P(None, ROW, "dp"),
            P(None, ROW, "dp"),
            P(None, ROW, "dp"),
            P(None, ("dp",) + ROW),
            P(None, ("dp",) + ROW),
            P(None, ("dp",) + ROW),
            P(None, ("dp",) + ROW),
            P("dp", None),
        ),
        check_vma=False,
    )
```

```python
from functools import partial
import math

import jax
import jax.numpy as jnp
from jax import lax
from jax.experimental import pallas as pl
from jax.experimental.pallas import tpu as pltpu
from jax.sharding import Mesh, PartitionSpec as P

D = 1024
HEAD_DIM = 64
FF = 4096
VC = 8192
VT = 16000


EPS = 1e-06
CLIP = 0.01
MOMENT = 0.9
DECAY = 0.75
SMOOTH = 0.1
Z_WEIGHT = 0.01
NEGATIVE = -1e30
LAST = (((1,), (1,)), ((), ()))
FIRST = (((0,), (0,)), ((), ()))


MESH = pl.DeviceIdType.MESH
ORDERS = ((0, 1, 2), (0, 2, 1))


def sources(n):
    return [(far, bits) for far in range(1 - n, n) for bits in range(4)]


def hops(far, bits):
    return abs(far) + (bits & 1) + (bits >> 1)


def arrival(order, far, bits):
    last = None
    for dim in order:
        if (dim == 0 and far != 0) or (dim > 0 and bits & dim):
            last = dim
    return last


def passes(order, far, bits):
    came = arrival(order, far, bits)
    place = -1 if came is None else order.index(came)
    found = [(0, -1 if far > 0 else 1)] if came == 0 else []
    for dim in order[place + 1 :]:
        found += [(0, 1), (0, -1)] if dim == 0 else [(dim, 0)]
    return found


def cut_slabs(shapes, gap):
    slabs = []
    base = 0.0
    for which, (rows, _) in enumerate(shapes):
        size = rows // len(ORDERS)
        for part, order in enumerate(ORDERS):
            slabs.append((which, part * size, size, order, base))
        base += gap
    return slabs


def wide(shape, table, n):
    _, rows, columns = shape
    if table:
        return (4 * rows, n * columns)
    return (n * rows, 4 * columns) if columns % 128 == 0 else (4 * n * rows, columns)


def placed(whole, shape, table, z, i, begin, rows):
    if table or shape[2] % 128 == 0:
        down, right = (i, z) if table else (z, i)
        return whole.at[
            :,
            pl.ds(pl.multiple_of(down * shape[1] + begin, 16), rows),
            pl.ds(pl.multiple_of(right * shape[2], 128), shape[2]),
        ]
    return whole.at[:, pl.ds(pl.multiple_of((z * 4 + i) * shape[1] + begin, 16), rows)]


class Here:
    def __init__(self, n):
        self.n = n
        self.z = lax.axis_index("dp")
        self.i = lax.axis_index("img")
        self.t = lax.axis_index("t")

    def device(self, dim, step):
        if dim == 0:
            return (self.z + step, self.i, self.t)
        return (self.z, jnp.bitwise_xor(self.i, dim), self.t)

    def below(self):
        return self.z > 0

    def above(self):
        return self.z < self.n - 1

    def side(self, step):
        return self.above() if step > 0 else self.below()

    def greet(self):
        barrier = pltpu.get_barrier_semaphore()

        def tell(device):
            pl.semaphore_signal(barrier, inc=1, device_id=device, device_id_type=MESH)

        pl.when(self.below())(lambda: tell(self.device(0, -1)))
        pl.when(self.above())(lambda: tell(self.device(0, 1)))
        tell(self.device(1, 0))
        tell(self.device(2, 0))
        pl.semaphore_wait(
            barrier, 2 + jnp.where(self.below(), 1, 0) + jnp.where(self.above(), 1, 0)
        )

    def exists(self, far):
        if far == 0:
            return None
        return (self.z + far >= 0) if far < 0 else (self.z + far < self.n)


def guarded(condition, action):
    if condition is None:
        action()
    else:
        pl.when(condition)(action)


def both(first, second):
    if first is None or second is None:
        return second if first is None else first
    return jnp.logical_and(first, second)


def gather_kernel(n, slabs, tables, *refs):
    count = len(tables)
    ins, outs = refs[:count], refs[count : 2 * count]
    send_sem, recv_sem, local_sem = refs[2 * count :]
    here = Here(n)
    here.greet()
    local = []
    for which in range(count):
        shape = ins[which].shape
        copy = pltpu.make_async_copy(
            ins[which],
            placed(outs[which], shape, tables[which], here.z, here.i, 0, shape[1]),
            local_sem.at[which],
        )
        copy.start()
        local.append(copy)

    def block(slab, far, bits):
        which, begin, rows = slabs[slab][:3]
        z, i = here.z + far, jnp.bitwise_xor(here.i, bits)
        return placed(outs[which], ins[which].shape, tables[which], z, i, begin, rows)

    def name(far, bits):
        return (here.z + far) * 4 + jnp.bitwise_xor(here.i, bits)

    def copy_of(slab, far, bits, dim, step):
        which, begin, rows = slabs[slab][:3]
        target = block(slab, far, bits)
        own = far == 0 and bits == 0
        return pltpu.make_async_remote_copy(
            src_ref=ins[which].at[:, pl.ds(begin, rows)] if own else target,
            dst_ref=target,
            send_sem=send_sem.at[slab, name(far, bits), (1 + step) // 2 if dim == 0 else 1 + dim],
            recv_sem=recv_sem.at[slab, name(far, bits)],
            device_id=here.device(dim, step),
            device_id_type=MESH,
        )

    def arrive(slab, far, bits):
        target = block(slab, far, bits)
        pltpu.make_async_remote_copy(
            src_ref=target,
            dst_ref=target,
            send_sem=send_sem.at[slab, 0, 0],
            recv_sem=recv_sem.at[slab, name(far, bits)],
            device_id=here.device(1, 0),
            device_id_type=MESH,
        ).wait_recv()

    events = sorted(
        (slabs[slab][4] + hops(far, bits), slab, far, bits)
        for slab in range(len(slabs))
        for far, bits in sources(n)
    )
    sent = []
    final = []
    for _, slab, far, bits in events:
        onward = passes(slabs[slab][3], far, bits)
        own = far == 0 and bits == 0
        if not onward:
            final.append((slab, far, bits))
            continue

        def act(slab=slab, far=far, bits=bits, onward=onward, own=own):
            if not own:
                arrive(slab, far, bits)
            for dim, step in onward:
                guarded(
                    here.side(step) if dim == 0 else None,
                    lambda dim=dim, step=step: copy_of(slab, far, bits, dim, step).start(),
                )

        guarded(here.exists(far), act)
        sent += [(slab, far, bits, dim, step) for dim, step in onward]
    for slab, far, bits in final:
        guarded(here.exists(far), lambda at=(slab, far, bits): arrive(*at))
    for slab, far, bits, dim, step in sent:
        guarded(
            both(here.exists(far), here.side(step) if dim == 0 else None),
            lambda at=(slab, far, bits, dim, step): copy_of(*at).wait_send(),
        )
    for copy in local:
        copy.wait()


def gather(arrays, tables, n, gap, collective_id):
    count = len(arrays)
    slabs = cut_slabs([a.shape[1:] for a in arrays], gap)
    size = sum(a.size * a.dtype.itemsize for a in arrays) * 4 * n
    return pl.pallas_call(
        partial(gather_kernel, n, slabs, tables),
        out_shape=[
            jax.ShapeDtypeStruct((a.shape[0],) + wide(a.shape, table, n), a.dtype)
            for a, table in zip(arrays, tables)
        ],
        in_specs=[pl.BlockSpec(memory_space=pl.ANY)] * count,
        out_specs=[pl.BlockSpec(memory_space=pl.ANY)] * count,
        scratch_shapes=[
            pltpu.SemaphoreType.DMA((len(slabs), 4 * n, 4)),
            pltpu.SemaphoreType.DMA((len(slabs), 4 * n)),
            pltpu.SemaphoreType.DMA((count,)),
        ],
        compiler_params=pltpu.CompilerParams(
            collective_id=collective_id, has_side_effects=True
        ),
        cost_estimate=pl.CostEstimate(flops=0, bytes_accessed=size * 16, transcendentals=0),
        name="gather",
    )(*arrays)


def places(n, order):
    table = {}
    used = 0
    line = [b for b in range(4) if any(dim == 0 for dim, _ in passes(order, 0, b))]
    for rank, bits in enumerate(line):
        for far in range(1 - n, n):
            for dim, step in passes(order, far, bits):
                if dim == 0:
                    second = far == 0 and step < 0
                    table[far, bits, dim, step] = (
                        (used + n, False) if second else (used + far, True)
                    )
        used += n + 1
    for flip in (1, 2):
        pairs = [p for p in sources(n) if (flip, 0) in passes(order, *p)]
        spread = any(far for far, _ in pairs)
        for bits in sorted({b for _, b in pairs}):
            for far, other in pairs:
                if other == bits:
                    table[far, bits, flip, 0] = (used + far, True) if spread else (used, False)
            used += n if spread else 1
    return table, used


def scatter_kernel(n, slabs, members, *refs):
    total = sum(members)
    count = len(members)
    ins, refs = refs[:total], refs[total:]
    outs, owns, gots = refs[:count], refs[count : 2 * count], refs[2 * count : 3 * count]
    send_sem, recv_sem, local_sem = refs[3 * count :]
    here = Here(n)
    tables = {order: places(n, order)[0] for order in ORDERS}
    loads = []
    for which in range(count):
        for member in range(members[which]):
            matrix = ins[sum(members[:which]) + member]
            rows = owns[which].shape[2] // members[which]
            columns = owns[which].shape[3]
            for z in range(n):
                for i in range(4):
                    copy = pltpu.make_async_copy(
                        matrix.at[pl.ds(z * rows, rows), pl.ds(i * columns, columns)]
                        if matrix.shape[0] == n * rows
                        else matrix.at[pl.ds((z * 4 + i) * rows, rows)],
                        owns[which].at[z, i, pl.ds(member * rows, rows)],
                        local_sem.at[len(loads)],
                    )
                    copy.start()
                    loads.append(copy)
    here.greet()
    for copy in loads:
        copy.wait()

    def own(slab, far, bits):
        which, begin, rows = slabs[slab][:3]
        return owns[which].at[
            here.z + far, jnp.bitwise_xor(here.i, bits), pl.ds(begin, rows)
        ]

    def slot(slab, number):
        which, _, rows, _, _, first = slabs[slab]
        return gots[which].at[pl.ds(pl.multiple_of(first + number * rows, 16), rows)]

    def number_at(order, z, key):
        constant, counts = tables[order][key]
        return constant + z if counts else constant

    def copy_of(slab, far, bits):
        order = slabs[slab][3]
        dim = arrival(order, far, bits)
        step = 0 if dim else (1 if far > 0 else -1)
        number = number_at(order, here.z + step, (far - step, bits ^ dim, dim, -step))
        return pltpu.make_async_remote_copy(
            src_ref=own(slab, far, bits),
            dst_ref=slot(slab, number),
            send_sem=send_sem.at[slab, (here.z + far) * 4 + bits],
            recv_sem=recv_sem.at[slab, number],
            device_id=here.device(dim, step),
            device_id_type=MESH,
        )

    events = sorted(
        (slabs[slab][4] + n + 1 - hops(far, bits), slab, far, bits)
        for slab in range(len(slabs))
        for far, bits in sources(n)
    )

    def add_up(slab, far, bits, parts):
        which, begin, rows, order = slabs[slab][:4]
        numbers = [number_at(order, here.z, (far, bits) + part) for part in parts]
        for number in numbers:
            landed = slot(slab, number)
            pltpu.make_async_remote_copy(
                src_ref=landed,
                dst_ref=landed,
                send_sem=send_sem.at[slab, 0],
                recv_sem=recv_sem.at[slab, number],
                device_id=here.device(1, 0),
                device_id_type=MESH,
            ).wait_recv()
        root = far == 0 and bits == 0
        if not parts and not root:
            return
        mine = own(slab, far, bits)
        landed = [slot(slab, number) for number in numbers]

        @pl.loop(0, rows // 16)
        def _(row):
            at = pl.ds(pl.multiple_of(row * 16, 16), 16)
            added = mine[at].astype(jnp.float32)
            for part in landed:
                added = added + part[at].astype(jnp.float32)
            if root:
                outs[which][pl.ds(pl.multiple_of(begin + row * 16, 16), 16)] = added
            else:
                mine[at] = added.astype(jnp.bfloat16)

    for _, slab, far, bits in events:

        def act(slab=slab, far=far, bits=bits):
            parts = passes(slabs[slab][3], far, bits)
            fixed = [p for p in parts if p[0]]
            line = [p for p in parts if not p[0]]
            if not line:
                add_up(slab, far, bits, fixed)
            elif len(line) == 1:
                there = here.side(line[0][1])
                pl.when(there)(lambda: add_up(slab, far, bits, line + fixed))
                pl.when(jnp.logical_not(there))(lambda: add_up(slab, far, bits, fixed))
            else:
                low, high = here.below(), here.above()
                up, down = line
                pl.when(jnp.logical_and(low, high))(
                    lambda: add_up(slab, far, bits, line + fixed)
                )
                pl.when(jnp.logical_not(low))(lambda: add_up(slab, far, bits, [up] + fixed))
                pl.when(jnp.logical_not(high))(lambda: add_up(slab, far, bits, [down] + fixed))
            if far or bits:
                copy_of(slab, far, bits).start()

        guarded(here.exists(far), act)
    for _, slab, far, bits in events:
        if far or bits:
            guarded(
                here.exists(far),
                lambda at=(slab, far, bits): copy_of(*at).wait_send(),
            )


def scatter(groups, shapes, n, gap, collective_id):
    members = [len(group) for group in groups]
    slabs = []
    totals = [0] * len(groups)
    most = 0
    sizes = [(m * rows, columns) for m, (rows, columns) in zip(members, shapes)]
    for which, begin, rows, order, base in cut_slabs(sizes, gap):
        used = places(n, order)[1]
        slabs.append((which, begin, rows, order, base, totals[which]))
        totals[which] += rows * used
        most = max(most, used)
    size = sum(rows * columns for rows, columns in sizes) * 8 * n
    return pl.pallas_call(
        partial(scatter_kernel, n, slabs, members),
        out_shape=[jax.ShapeDtypeStruct(size, jnp.float32) for size in sizes],
        in_specs=[pl.BlockSpec(memory_space=pl.ANY)] * sum(members),
        out_specs=[pl.BlockSpec(memory_space=pltpu.VMEM)] * len(groups),
        scratch_shapes=[pltpu.VMEM((n, 4) + size, jnp.bfloat16) for size in sizes]
        + [pltpu.VMEM((total, size[1]), jnp.bfloat16) for size, total in zip(sizes, totals)]
        + [
            pltpu.SemaphoreType.DMA((len(slabs), 4 * n)),
            pltpu.SemaphoreType.DMA((len(slabs), most)),
            pltpu.SemaphoreType.DMA((4 * n * sum(members),)),
        ],
        compiler_params=pltpu.CompilerParams(
            collective_id=collective_id, has_side_effects=True, vmem_limit_bytes=58 * 2**20
        ),
        cost_estimate=pl.CostEstimate(flops=0, bytes_accessed=size * 16, transcendentals=0),
        name="scatter",
    )(*[matrix for group in groups for matrix in group])


class Row:
    def __init__(self, size):
        self.size = size
        self.parts = size // 4
        self.me = lax.axis_index("img") * self.parts + lax.axis_index("t")

    def other(self, step):
        return lax.rem(self.me + step, self.size)

    def device(self, index):
        return (lax.axis_index("dp"), index // self.parts, lax.rem(index, self.parts))


class Along:
    def __init__(self, axis, size):
        self.axis, self.size = axis, size
        self.me = lax.axis_index(axis)

    def other(self, step):
        return lax.rem(self.me + step, self.size)

    def device(self, index):
        return tuple(
            index if axis == self.axis else lax.axis_index(axis) for axis in ("dp",) + ROW
        )


def Column(size):
    return Along("dp", size)


def greet(*groups):
    barrier = pltpu.get_barrier_semaphore()
    for group in groups:
        for step in range(1, group.size):
            pl.semaphore_signal(
                barrier, inc=1, device_id=group.device(group.other(step)), device_id_type=MESH
            )
    pl.semaphore_wait(barrier, sum(group.size - 1 for group in groups))


class Exchange:
    def __init__(self, group, source, target, send_sem, recv_sem):
        self.group, self.source, self.target = group, source, target
        self.send_sem, self.recv_sem = send_sem, recv_sem

    def copy_of(self, step):
        index = self.group.other(step)
        return pltpu.make_async_remote_copy(
            src_ref=self.source(index),
            dst_ref=self.target(self.group.me),
            send_sem=self.send_sem.at[step],
            recv_sem=self.recv_sem.at[self.group.me],
            device_id=self.group.device(index),
            device_id_type=MESH,
        )

    def start(self):
        for step in range(1, self.group.size):
            self.copy_of(step).start()
        return self

    def finish(self):
        for step in range(1, self.group.size):
            index = self.group.other(step)
            pltpu.make_async_remote_copy(
                src_ref=self.target(index),
                dst_ref=self.target(index),
                send_sem=self.send_sem.at[step],
                recv_sem=self.recv_sem.at[index],
                device_id=self.group.device(index),
                device_id_type=MESH,
            ).wait_recv()
        for step in range(1, self.group.size):
            self.copy_of(step).wait_send()


def exchange(*parts):
    Exchange(*parts).start().finish()


def row_block(ref, rows, index):
    return ref.at[pl.ds(pl.multiple_of(index * rows, 16), rows)]


def small_call(kernel, out_shape, scratch, operands, collective_id, name):
    vmem = pl.BlockSpec(memory_space=pltpu.VMEM)
    return pl.pallas_call(
        kernel,
        out_shape=out_shape,
        in_specs=[vmem] * len(operands),
        out_specs=[vmem] * len(out_shape) if isinstance(out_shape, list) else vmem,
        scratch_shapes=scratch,
        compiler_params=pltpu.CompilerParams(
            collective_id=collective_id, has_side_effects=True
        ),
        cost_estimate=pl.CostEstimate(flops=0, bytes_accessed=2**24, transcendentals=0),
        name=name,
    )(*operands)


def semaphores(size):
    return [pltpu.SemaphoreType.DMA((size,)), pltpu.SemaphoreType.DMA((size,))]


class RowSpread:
    def __init__(self, row, mine, every, *sems):
        self.mine, self.every, self.rows, self.me = mine, every, mine.shape[0], row.me
        self.work = Exchange(row, lambda _: mine, self.block, *sems)

    def block(self, index):
        return row_block(self.every, self.rows, index)

    def start(self, values):
        self.mine[...] = values
        self.block(self.me)[...] = values
        self.work.start()

    def finish(self):
        self.work.finish()
        return self.every[...]


class RowSum:
    def __init__(self, row, short, got, rows, *sems):
        self.short, self.got, self.rows, self.row = short, got, rows, row
        self.work = Exchange(
            row,
            lambda index: row_block(short, rows, index),
            lambda index: row_block(got, rows, index),
            *sems,
        )

    def start(self, values=None):
        if values is not None:
            self.short[...] = values.astype(jnp.bfloat16)
        mine = row_block(self.short, self.rows, self.row.me)
        row_block(self.got, self.rows, self.row.me)[...] = mine[...]
        self.work.start()

    def finish(self):
        self.work.finish()
        total = self.got[pl.ds(0, self.rows)].astype(jnp.float32)
        for index in range(1, self.row.size):
            total = total + self.got[pl.ds(index * self.rows, self.rows)].astype(jnp.float32)
        return total


def head_lanes(width):
    lanes = lax.broadcasted_iota(jnp.int32, (1, width), 1) // HEAD_DIM
    return [lanes == head for head in range(width // HEAD_DIM)]


def only(lanes, values):
    return jnp.where(lanes, values, jnp.zeros_like(values))


def full_shares(query, key, allowed, lanes):
    scores = product(only(lanes, query), key, LAST) * HEAD_DIM ** (-0.5)
    scores = jnp.where(allowed > 0, scores, NEGATIVE)
    weight = jnp.exp(scores - jnp.max(scores, axis=-1, keepdims=True))
    return weight / jnp.sum(weight, axis=-1, keepdims=True)


def encoder_kernel(
    n, size, picked, gains, attention, dense, allowed,
    encoded, first, middle, top, inputs, query, key, value, mixed, dense_in, hidden, active,
    short, mine, got_text, got_mixed, got_dense, *sems,
):
    row, column = Row(size), Column(n)
    rows, width = first.shape[0], picked.shape[2]
    greet(row, column)

    def columns(index):
        return short.at[:, pl.ds(pl.multiple_of(index * width, 128), width)]

    columns(column.me)[...] = picked[column.me]
    exchange(column, lambda index: picked.at[index], columns, *sems[:2])
    text = RowSum(row, short, got_text, rows, *sems[2:4])
    text.start()
    values = text.finish()
    first[...] = values
    spread_one = RowSpread(row, mine, inputs, *sems[4:6])
    spread_one.start(rms_norm(values, gains[0:1]).astype(jnp.bfloat16))
    every = spread_one.finish()
    query[...] = jnp.dot(
        every, attention[0], preferred_element_type=jnp.float32
    ).astype(jnp.bfloat16)
    key[...] = jnp.dot(every, attention[1], preferred_element_type=jnp.float32).astype(jnp.bfloat16)
    value[...] = jnp.dot(
        every, attention[2], preferred_element_type=jnp.float32
    ).astype(jnp.bfloat16)
    out = jnp.zeros(query.shape, jnp.float32)
    for lanes in head_lanes(query.shape[1]):
        shares = full_shares(query[...], key[...], allowed[...], lanes).astype(jnp.bfloat16)
        out = out + jnp.dot(shares, only(lanes, value[...]), preferred_element_type=jnp.float32)
    mixed[...] = out.astype(jnp.bfloat16)
    branch = RowSum(row, short, got_mixed, rows, *sems[6:8])
    branch.start(product(mixed[...], attention[3], LAST))
    values = values + branch.finish()
    middle[...] = values
    spread_two = RowSpread(row, mine, dense_in, *sems[8:10])
    spread_two.start(rms_norm(values, gains[1:2]).astype(jnp.bfloat16))
    every = spread_two.finish()
    hidden[...] = jnp.dot(every, dense[0], preferred_element_type=jnp.float32)
    inner = hidden[...]
    active[...] = (0.5 * inner * (1.0 + lax.erf(inner * math.sqrt(0.5)))).astype(jnp.bfloat16)
    branch = RowSum(row, short, got_dense, rows, *sems[10:12])
    branch.start(product(active[...], dense[1], LAST))
    values = values + branch.finish()
    top[...] = values
    spread_three = RowSpread(row, mine, encoded, *sems[12:14])
    spread_three.start(rms_norm(values, gains[2:3]).astype(jnp.bfloat16))
    spread_three.finish()


def encoder_call(kernel, out_shape, scratch, operands, collective_id, name):
    vmem = pl.BlockSpec(memory_space=pltpu.VMEM)
    return pl.pallas_call(
        kernel,
        out_shape=out_shape,
        in_specs=[vmem] * len(operands),
        out_specs=[vmem] * len(out_shape),
        scratch_shapes=scratch,
        compiler_params=pltpu.CompilerParams(
            collective_id=collective_id, has_side_effects=True, vmem_limit_bytes=48 * 2**20
        ),
        cost_estimate=pl.CostEstimate(flops=0, bytes_accessed=2**27, transcendentals=0),
        name=name,
    )(*operands)


def encoder_forward(picked, gains, attention, dense, allowed):
    n, tokens, _ = picked.shape
    size = lax.axis_size("img") * lax.axis_size("t")
    width, inner = attention.shape[2], dense.shape[2]
    own = jax.ShapeDtypeStruct((tokens // size, D), jnp.float32)
    every = jax.ShapeDtypeStruct((tokens, D), jnp.bfloat16)
    head = jax.ShapeDtypeStruct((tokens, width), jnp.bfloat16)
    wide_out = [jax.ShapeDtypeStruct((tokens, inner), kind) for kind in (jnp.float32, jnp.bfloat16)]
    whole = pltpu.VMEM((tokens, D), jnp.bfloat16)
    outs = encoder_call(
        partial(encoder_kernel, n, size),
        [every, own, own, own, every, head, head, head, head, every] + wide_out,
        [whole, pltpu.VMEM((tokens // size, D), jnp.bfloat16), whole, whole, whole]
        + semaphores(n)
        + semaphores(size) * 6,
        [picked, gains, attention, dense, allowed],
        3,
        "encoder",
    )
    return outs[0], outs[1:]


def norm_back_sums(values, gain, upstream):
    scale = lax.rsqrt(jnp.mean(values * values, axis=-1, keepdims=True) + EPS)
    unit = values * scale
    inner = upstream * gain
    grad = scale * (inner - unit * jnp.mean(inner * unit, axis=-1, keepdims=True))
    return grad, jnp.sum(upstream * unit, axis=0, keepdims=True)


def encoder_back_kernel(
    n, size, grad_encoded, gains, attention, dense, allowed,
    first, middle, top, inputs, query, key, value, mixed, dense_in, hidden, active,
    text_rows, gain_grads, attention_grads, dense_grads,
    short, mine, got_encoded, got_dense, got_mixed, every_dense, every_mixed, every_text, *sems,
):
    row, column = Row(size), Column(n)
    rows, width = first.shape[0], text_rows.shape[2]
    short[...] = grad_encoded[...].astype(jnp.bfloat16)
    greet(row, column)
    gain_grads[...] = jnp.zeros(gain_grads.shape, jnp.float32)
    work = RowSum(row, short, got_encoded, rows, *sems[:2])
    work.start()
    grad, gain = norm_back_sums(top[...], gains[2:3], work.finish())
    gain_grads[2:3] = gain
    work = RowSpread(row, mine, every_dense, *sems[2:4])
    work.start(grad.astype(jnp.bfloat16))
    upstream = work.finish()
    inner = hidden[...]
    share = 0.5 * (1.0 + lax.erf(inner * math.sqrt(0.5)))
    slope = share + inner * jnp.exp(-0.5 * inner * inner) * (1.0 / math.sqrt(2.0 * math.pi))
    grad_hidden = (
        slope * jnp.dot(upstream, dense[1], preferred_element_type=jnp.float32)
    ).astype(jnp.bfloat16)
    work = RowSum(row, short, got_dense, rows, *sems[4:6])
    work.start(product(grad_hidden, dense[0], LAST))
    dense_grads[0] = product(dense_in[...], grad_hidden, FIRST).astype(jnp.bfloat16)
    dense_grads[1] = product(upstream, active[...], FIRST).astype(jnp.bfloat16)
    part, gain = norm_back_sums(middle[...], gains[1:2], work.finish())
    gain_grads[1:2] = gain
    grad = grad + part
    work = RowSpread(row, mine, every_mixed, *sems[6:8])
    work.start(grad.astype(jnp.bfloat16))
    upstream = work.finish()
    grad_mixed = jnp.dot(upstream, attention[3], preferred_element_type=jnp.float32).astype(
        jnp.bfloat16
    )
    scale = HEAD_DIM ** (-0.5)
    grad_query = grad_key = grad_value = jnp.zeros(query.shape, jnp.float32)
    for lanes in head_lanes(query.shape[1]):
        shares = full_shares(query[...], key[...], allowed[...], lanes)
        head_up = only(lanes, grad_mixed)
        grad_value = grad_value + product(shares.astype(jnp.bfloat16), head_up, FIRST)
        grad_shares = product(head_up, value[...], LAST)
        delta = jnp.sum(shares * grad_shares, axis=-1, keepdims=True)
        grad_scores = (shares * (grad_shares - delta)).astype(jnp.bfloat16)
        grad_query = grad_query + scale * jnp.dot(
            grad_scores, only(lanes, key[...]), preferred_element_type=jnp.float32
        )
        grad_key = grad_key + scale * product(grad_scores, only(lanes, query[...]), FIRST)
    grad_query = grad_query.astype(jnp.bfloat16)
    grad_key = grad_key.astype(jnp.bfloat16)
    grad_value = grad_value.astype(jnp.bfloat16)
    work = RowSum(row, short, got_mixed, rows, *sems[8:10])
    work.start(
        product(grad_query, attention[0], LAST)
        + product(grad_key, attention[1], LAST)
        + product(grad_value, attention[2], LAST)
    )
    for which, part in enumerate((grad_query, grad_key, grad_value)):
        attention_grads[which] = product(inputs[...], part, FIRST).astype(jnp.bfloat16)
    attention_grads[3] = product(upstream, mixed[...], FIRST).astype(jnp.bfloat16)
    part, gain = norm_back_sums(first[...], gains[0:1], work.finish())
    gain_grads[0:1] = gain
    work = RowSpread(row, mine, every_text, *sems[10:12])
    work.start((grad + part).astype(jnp.bfloat16))
    work.finish()

    def columns(index):
        return every_text.at[:, pl.ds(pl.multiple_of(index * width, 128), width)]

    text_rows[column.me] = columns(column.me)[...]
    exchange(column, columns, lambda index: text_rows.at[index], *sems[12:14])


def encoder_backward(grad_encoded, gains, attention, dense, allowed, kept):
    n = lax.axis_size("dp")
    tokens = grad_encoded.shape[0]
    size = lax.axis_size("img") * lax.axis_size("t")
    whole = pltpu.VMEM((tokens, D), jnp.bfloat16)
    return encoder_call(
        partial(encoder_back_kernel, n, size),
        [
            jax.ShapeDtypeStruct((n, tokens, D // n), jnp.bfloat16),
            jax.ShapeDtypeStruct((8, D), jnp.float32),
            jax.ShapeDtypeStruct(attention.shape, jnp.bfloat16),
            jax.ShapeDtypeStruct(dense.shape, jnp.bfloat16),
        ],
        [whole, pltpu.VMEM((tokens // size, D), jnp.bfloat16)]
        + [whole] * 6
        + semaphores(size) * 6
        + semaphores(n),
        [grad_encoded, gains, attention, dense, allowed, *kept],
        4,
        "encoder_back",
    )


def causal_kernel(query, key, value, mixed, partition):
    length = query.shape[0]
    block = min(256, length)
    scale = HEAD_DIM ** (-0.5)
    halves = head_lanes(query.shape[1])
    for begin in range(0, length, block):
        at, end = pl.ds(begin, block), begin + block
        ahead = lax.broadcasted_iota(jnp.int32, (block, end), 1) > begin + (
            lax.broadcasted_iota(jnp.int32, (block, end), 0)
        )
        out = jnp.zeros((block, query.shape[1]), jnp.float32)
        logs = jnp.zeros((block, query.shape[1]), jnp.float32)
        for lanes in halves:
            scores = product(only(lanes, query[at]), key[:end], LAST) * scale
            scores = jnp.where(ahead, NEGATIVE, scores)
            highest = jnp.max(scores, axis=-1, keepdims=True)
            weight = jnp.exp(scores - highest)
            total = jnp.sum(weight, axis=-1, keepdims=True)
            shares = (weight * (1.0 / total)).astype(jnp.bfloat16)
            out = out + jnp.dot(
                shares, only(lanes, value[:end]), preferred_element_type=jnp.float32
            )
            logs = jnp.where(lanes, highest + jnp.log(total), logs)
        mixed[at] = out.astype(jnp.bfloat16)
        partition[at] = logs


def causal_back_kernel(
    query, key, value, upstream, partition, out_query, out_key, out_value, grad_key, grad_value
):
    length = query.shape[0]
    block = min(256, length)
    scale = HEAD_DIM ** (-0.5)
    halves = head_lanes(query.shape[1])
    grad_key[...] = jnp.zeros(grad_key.shape, jnp.float32)
    grad_value[...] = jnp.zeros(grad_value.shape, jnp.float32)
    for begin in range(0, length, block):
        at, end = pl.ds(begin, block), begin + block
        ahead = lax.broadcasted_iota(jnp.int32, (block, end), 1) > begin + (
            lax.broadcasted_iota(jnp.int32, (block, end), 0)
        )
        grad_query = jnp.zeros((block, query.shape[1]), jnp.float32)
        for head, lanes in enumerate(halves):
            head_query, head_up = only(lanes, query[at]), only(lanes, upstream[at])
            log = partition[at, head * HEAD_DIM : head * HEAD_DIM + 1]
            scores = product(head_query, key[:end], LAST) * scale
            shares = jnp.exp(jnp.where(ahead, NEGATIVE, scores) - log)
            grad_value[:end] += product(shares.astype(jnp.bfloat16), head_up, FIRST)
            grad_shares = product(head_up, value[:end], LAST)
            delta = jnp.sum(shares * grad_shares, axis=-1, keepdims=True)
            grad_scores = (shares * (grad_shares - delta)).astype(jnp.bfloat16)
            grad_query = grad_query + jnp.dot(
                grad_scores, only(lanes, key[:end]), preferred_element_type=jnp.float32
            )
            grad_key[:end] += product(grad_scores, head_query, FIRST)
        out_query[at] = (grad_query * scale).astype(jnp.bfloat16)
    out_key[...] = (grad_key[...] * scale).astype(jnp.bfloat16)
    out_value[...] = grad_value[...].astype(jnp.bfloat16)


def by_heads(kernel, operands, kinds, scratch):
    length, width = operands[0].shape
    lanes = min(128, width)
    spec = pl.BlockSpec((length, lanes), lambda pair: (0, pair))
    return pl.pallas_call(
        kernel,
        grid=(width // lanes,),
        out_shape=[jax.ShapeDtypeStruct((length, width), kind) for kind in kinds],
        in_specs=[spec] * len(operands),
        out_specs=[spec] * len(kinds),
        scratch_shapes=[pltpu.VMEM((length, lanes), jnp.float32)] * scratch,
        compiler_params=pltpu.CompilerParams(vmem_limit_bytes=40 * 2**20),
        cost_estimate=pl.CostEstimate(
            flops=4 * length * length * width, bytes_accessed=2**25, transcendentals=length * length
        ),
        name="causal",
    )(*operands)


def causal_forward(query, key, value):
    return by_heads(causal_kernel, (query, key, value), (jnp.bfloat16, jnp.float32), 0)


def causal_backward(query, key, value, partition, upstream):
    return by_heads(
        causal_back_kernel, (query, key, value, upstream, partition), (jnp.bfloat16,) * 3, 2
    )


def share_kernel(n, size, mine, every, *sems):
    row, column = Row(size), Column(n)
    greet(row, column)
    every[column.me, row.me] = mine[...]
    exchange(row, lambda _: mine, lambda index: every.at[column.me, index], *sems[:2])
    exchange(
        column, lambda _: every.at[column.me], lambda index: every.at[index], *sems[2:]
    )


def share(values):
    n = lax.axis_size("dp")
    size = lax.axis_size("img") * lax.axis_size("t")
    return small_call(
        partial(share_kernel, n, size),
        jax.ShapeDtypeStruct((n, size) + values.shape, values.dtype),
        semaphores(size) + semaphores(n),
        [values],
        7,
        "share",
    )


def total_kernel(sizes, mine, result, row_result, *refs):
    groups = [Along(axis, size) for axis, size in sizes]
    parts, gots, sems = refs[:3], refs[3:6], refs[6:]
    greet(*groups)
    parts[0][...] = mine[...]
    for turn, group in enumerate(groups):
        rows = gots[turn].shape[1]
        source = parts[turn].at[pl.ds(0, rows)]
        got = gots[turn]
        got[group.me] = source[...]
        exchange(
            group,
            lambda _, source=source: source,
            lambda index, got=got: got.at[index],
            *sems[2 * turn : 2 * turn + 2],
        )
        added = got[0]
        for index in range(1, group.size):
            added = added + got[index]
        if turn < 2:
            parts[turn + 1][...] = added
        else:
            result[...] = added
    row_result[...] = parts[2][...]


def total_of(values, rows):
    sizes = [(axis, lax.axis_size(axis)) for axis in ("t", "img", "dp")]
    shape = values.shape
    short = (rows, shape[1])
    shapes = [shape, shape, short]
    return small_call(
        partial(total_kernel, sizes),
        [jax.ShapeDtypeStruct(short, values.dtype), jax.ShapeDtypeStruct(shape, values.dtype)],
        [pltpu.VMEM(shape, values.dtype)] * 3
        + [pltpu.VMEM((size,) + part, values.dtype) for (_, size), part in zip(sizes, shapes)]
        + [sem for _, size in sizes for sem in semaphores(size)],
        [values],
        8,
        "total",
    )


def rms_norm(values, gain):
    return values * lax.rsqrt(jnp.mean(values * values, axis=-1, keepdims=True) + EPS) * gain


def norm_back(values, gain, upstream):
    _, pull = jax.vjp(rms_norm, values, gain)
    return pull(upstream)


ROW = ("img", "t")


def spread(values, axis):
    if axis == "t" and lax.axis_size("t") == 2:
        other = lax.ppermute(values, "t", [(0, 1), (1, 0)])
        first = lax.axis_index("t") == 0
        return jnp.concatenate(
            [jnp.where(first, values, other), jnp.where(first, other, values)], axis=0
        )
    return lax.all_gather(values, axis, axis=0, tiled=True)


def collect(values, axis):
    if axis == "t" and lax.axis_size("t") == 2:
        half = values.shape[0] // 2
        place = lax.axis_index("t")
        away = lax.dynamic_slice_in_dim(values, (1 - place) * half, half, 0)
        came = lax.ppermute(away.astype(jnp.bfloat16), "t", [(0, 1), (1, 0)])
        return lax.dynamic_slice_in_dim(values, place * half, half, 0) + came.astype(jnp.float32)
    return lax.psum_scatter(
        values.astype(jnp.bfloat16), axis, scatter_dimension=0, tiled=True
    ).astype(jnp.float32)


def product(left, right, dims):
    return lax.dot_general(left, right, dims, preferred_element_type=jnp.float32)


def split_heads(values, groups):
    return values.reshape(groups, values.shape[0] // groups, values.shape[1] // HEAD_DIM, HEAD_DIM)


def core_forward(query, key, value, allowed, scale):
    scores = jnp.einsum("bqhe,bkhe->bhqk", query, key, preferred_element_type=jnp.float32) * scale
    scores = jnp.where(allowed[:, None], scores, NEGATIVE)
    highest = jnp.max(scores, axis=-1, keepdims=True)
    weight = jnp.exp(scores - highest)
    totals = jnp.sum(weight, axis=-1, keepdims=True)
    shares = (weight / totals).astype(jnp.bfloat16)
    mixed = jnp.einsum("bhqk,bkhe->bqhe", shares, value, preferred_element_type=jnp.float32)
    return (mixed.astype(jnp.bfloat16), highest + jnp.log(totals))


def core_backward(query, key, value, allowed, scale, partition, upstream):
    scores = jnp.einsum("bqhe,bkhe->bhqk", query, key, preferred_element_type=jnp.float32) * scale
    scores = jnp.where(allowed[:, None], scores, NEGATIVE)
    shares = jnp.exp(scores - partition)
    grad_value = jnp.einsum(
        "bhqk,bqhe->bkhe", shares.astype(jnp.bfloat16), upstream, preferred_element_type=jnp.float32
    )
    grad_shares = jnp.einsum("bqhe,bkhe->bhqk", upstream, value, preferred_element_type=jnp.float32)
    inner = jnp.sum(shares * grad_shares, axis=-1, keepdims=True)
    grad_scores = (shares * (grad_shares - inner)).astype(jnp.bfloat16)
    grad_query = (
        jnp.einsum("bhqk,bkhe->bqhe", grad_scores, key, preferred_element_type=jnp.float32) * scale
    )
    grad_key = (
        jnp.einsum("bhqk,bqhe->bkhe", grad_scores, query, preferred_element_type=jnp.float32)
        * scale
    )
    return (grad_query, grad_key, grad_value)


def mix_forward(query, key, value, kind, context):
    scale = HEAD_DIM ** (-0.5)
    width = query.shape[1]
    if kind == "self":
        return causal_forward(query, key, value)
    query, key, value = (split_heads(part, 1) for part in (query, key, value))
    mixed, partition = core_forward(query, key, value, context["allowed"], scale)
    return (mixed.reshape(-1, width), partition)


def mix_backward(query, key, value, partition, upstream, kind, context):
    scale = HEAD_DIM ** (-0.5)
    width = query.shape[1]
    if kind == "self":
        return causal_backward(query, key, value, partition, upstream)
    query, key, value, upstream = (split_heads(part, 1) for part in (query, key, value, upstream))
    grads = core_backward(query, key, value, context["allowed"], scale, partition, upstream)
    return tuple(grad.reshape(-1, width).astype(jnp.bfloat16) for grad in grads)


def attention_forward(values, gain, weights, kind, axis, context, source=None):
    normed = rms_norm(values, gain).astype(jnp.bfloat16)
    inputs = spread(normed, axis)
    if source is None:
        source = inputs
    query = jnp.dot(inputs, weights[0], preferred_element_type=jnp.float32).astype(jnp.bfloat16)
    key = jnp.dot(source, weights[1], preferred_element_type=jnp.float32).astype(jnp.bfloat16)
    value = jnp.dot(source, weights[2], preferred_element_type=jnp.float32).astype(jnp.bfloat16)
    mixed, partition = mix_forward(query, key, value, kind, context)
    output = collect(product(mixed, weights[3], LAST), axis)
    return (output, (inputs, source, query, key, value, mixed, partition))


def attention_backward(upstream, values, gain, weights, kind, axis, context, kept):
    inputs, source, query, key, value, mixed, partition = kept
    grad_rows = spread(upstream.astype(jnp.bfloat16), axis)
    grad_out = product(grad_rows, mixed, FIRST)
    grad_mixed = jnp.dot(grad_rows, weights[3], preferred_element_type=jnp.float32).astype(
        jnp.bfloat16
    )
    grad_query, grad_key, grad_value = mix_backward(
        query, key, value, partition, grad_mixed, kind, context
    )
    grads = [
        product(inputs, grad_query, FIRST).astype(jnp.bfloat16),
        product(source, grad_key, FIRST).astype(jnp.bfloat16),
        product(source, grad_value, FIRST).astype(jnp.bfloat16),
        grad_out.astype(jnp.bfloat16),
    ]
    from_query = product(grad_query, weights[0], LAST)
    from_source = product(grad_key, weights[1], LAST) + product(grad_value, weights[2], LAST)
    if kind == "cross":
        grad_normed = collect(from_query, axis)
    else:
        grad_normed = collect(from_query + from_source, axis)
    grad_values, grad_gain = norm_back(values, gain, grad_normed)
    return (grad_values, grad_gain, grads, from_source)


def dense_forward(values, gain, weights, axis):
    normed = rms_norm(values, gain).astype(jnp.bfloat16)
    inputs = spread(normed, axis)
    hidden = jnp.dot(inputs, weights[0], preferred_element_type=jnp.float32)
    share_below = 0.5 * (1.0 + lax.erf(hidden * math.sqrt(0.5)))
    active = (hidden * share_below).astype(jnp.bfloat16)
    slope = share_below + hidden * jnp.exp(-0.5 * hidden * hidden) * (
        1.0 / math.sqrt(2.0 * math.pi)
    )
    output = collect(product(active, weights[1], LAST), axis)
    return (output, (inputs, weights, slope, active))


def dense_backward(upstream, values, gain, axis, kept):
    inputs, matrices, slope, active = kept
    grad_rows = spread(upstream.astype(jnp.bfloat16), axis)
    grad_active = jnp.dot(grad_rows, matrices[1], preferred_element_type=jnp.float32)
    grad_hidden = (grad_active * slope).astype(jnp.bfloat16)
    grads = [
        product(inputs, grad_hidden, FIRST).astype(jnp.bfloat16),
        product(grad_rows, active, FIRST).astype(jnp.bfloat16),
    ]
    grad_normed = collect(product(grad_hidden, matrices[0], LAST), axis)
    grad_values, grad_gain = norm_back(values, gain, grad_normed)
    return (grad_values, grad_gain, grads)


def code_hits(token_ids, usable, vocab):
    local = token_ids - lax.axis_index(ROW) * vocab
    places = jnp.arange(vocab, dtype=jnp.int32)
    return ((local[:, None] == places[None, :]) & usable[:, None]).astype(jnp.bfloat16)


def code_forward(token_ids, usable, table):
    hits = code_hits(token_ids, usable, table.shape[0])
    picked = jnp.dot(hits, table, preferred_element_type=jnp.float32).astype(jnp.bfloat16)
    return lax.psum_scatter(picked, ROW, scatter_dimension=0, tiled=True).astype(jnp.float32)


def code_backward(upstream, token_ids, usable, vocab):
    rows = lax.all_gather(upstream.astype(jnp.bfloat16), ROW, axis=0, tiled=True)
    return product(code_hits(token_ids, usable, vocab), rows, FIRST)


def merge_stats(first, second):
    highest = jnp.maximum(first[0], second[0])
    mass = first[1] * jnp.exp(first[0] - highest) + second[1] * jnp.exp(second[0] - highest)
    return (highest, mass, first[2] + second[2], first[3] + second[3])


def joined(stats):
    if lax.axis_size("t") == 2:
        other = lax.ppermute(jnp.stack(stats), "t", [(0, 1), (1, 0)])
        return merge_stats(stats, tuple(other))
    every = lax.all_gather(jnp.stack(stats), "t")
    state = tuple(every[0])
    for place in range(1, every.shape[0]):
        state = merge_stats(state, tuple(every[place]))
    return state


def matrices_of(gathered, n):
    count, rows, columns = gathered.shape
    if rows <= D:
        return gathered
    parts = gathered.reshape(count, n, 4, rows // n // 4, columns)
    return jnp.transpose(parts, (0, 1, 3, 2, 4)).reshape(count, rows // 4, 4 * columns)


def blocks_of(matrix, columns, n):
    if columns % 128 == 0:
        return matrix
    rows = matrix.shape[0]
    parts = matrix.reshape(n, rows // n, 4, columns)
    return jnp.transpose(parts, (0, 2, 1, 3)).reshape(4 * rows, columns)


def update(master, moment, average, gradient, factor, rate):
    clipped = gradient * factor
    moment_new = MOMENT * moment + clipped
    master_new = master - rate * (clipped + MOMENT * moment_new)
    average_new = DECAY * average + (1.0 - DECAY) * master_new
    return (master_new, moment_new, average_new, master_new.astype(jnp.bfloat16))


def per_device(
    code_ids,
    code_mask,
    caption_ids,
    caption_segments,
    image_row,
    attention_master,
    attention_momentum,
    attention_average,
    dense_master,
    dense_momentum,
    dense_average,
    text_master,
    text_momentum,
    text_average,
    code_master,
    code_momentum,
    code_average,
    gain_master,
    gain_momentum,
    gain_average,
):
    n = lax.axis_size("dp")
    z, image, part = lax.axis_index("dp"), lax.axis_index("img"), lax.axis_index("t")
    attention_shape = attention_master.shape[1:]
    dense_shape = dense_master.shape[1:]
    code_shape = code_master.shape[1:]
    images, length = code_ids.shape
    caption_rows, caption_length = caption_ids.shape
    text_rows, text_width = text_master.shape
    text_count = caption_ids.size
    mask = code_mask.astype(jnp.float32)
    encoder_attention, encoder_dense, code_table = (
        lax.all_gather(attention_master[0].astype(jnp.bfloat16), "dp", axis=1, tiled=True),
        lax.all_gather(dense_master[0].astype(jnp.bfloat16), "dp", axis=1, tiled=True),
        lax.all_gather(code_master[0].astype(jnp.bfloat16), "dp", axis=1, tiled=True),
    )
    self_weights, cross_weights, dense_weights, out_table = gather(
        [
            attention_master[1].astype(jnp.bfloat16),
            attention_master[2].astype(jnp.bfloat16),
            dense_master[1].astype(jnp.bfloat16),
            code_master[1:2].astype(jnp.bfloat16),
        ],
        [False, False, False, True],
        n,
        1.0,
        0,
    )
    out_table = out_table[0]
    self_weights, cross_weights, dense_weights = (
        matrices_of(weights, n) for weights in (self_weights, cross_weights, dense_weights)
    )
    previous = jnp.concatenate(
        [jnp.zeros((images, 1), jnp.int32), code_ids[:, :-1]], axis=1
    ).reshape(-1)
    starting = jnp.broadcast_to(jnp.arange(length) > 0, (images, length)).reshape(-1)
    code_table, self_weights, encoder_attention, encoder_dense = lax.optimization_barrier(
        (code_table, self_weights, encoder_attention, encoder_dense)
    )
    decoder_in = code_forward(previous, starting, code_table)
    gain_width = gain_master.shape[1]
    note = jnp.zeros((16, 128), jnp.float32)
    note = note.at[:7, :gain_width].set(gain_master)
    note = note.at[7, 0].set(jnp.sum(mask))
    note = note.at[8 : 8 + text_count // 128].set(
        caption_ids.astype(jnp.float32).reshape(-1, 128)
    )
    notes = share(note)
    gain_set = (
        jnp.transpose(notes[:, :, :7, :gain_width], (2, 0, 1, 3))
        .reshape(7, D)
    )
    gain_set = lax.reduce_precision(gain_set, exponent_bits=8, mantissa_bits=7)
    count = jnp.sum(notes[:, 0, 7, 0])
    all_text = notes[:, 0, 8 : 8 + text_count // 128].reshape(-1).astype(jnp.int32)
    segments = caption_segments.reshape(-1)
    same = (segments[:, None] == segments[None, :]).astype(jnp.float32)
    row = jnp.sum(jnp.where(jnp.arange(images) == image, image_row, 0)) - z * caption_rows
    owners = lax.dynamic_index_in_dim(caption_segments, row, 0, False)
    cross_context = {"allowed": (owners == z * images + image)[None, None, :]}
    text_local = all_text - lax.axis_index(ROW) * text_rows
    text_inside = (text_local >= 0) & (text_local < text_rows)
    picked = jnp.take(text_master, jnp.clip(text_local, 0, text_rows - 1), axis=0)
    picked = jnp.where(text_inside[:, None], picked, 0.0).astype(jnp.bfloat16)
    encoder_gains = jnp.concatenate([gain_set, jnp.zeros((1, D), jnp.float32)])
    encoded, encoder_keep = encoder_forward(
        picked.reshape(n, text_count, text_width),
        encoder_gains,
        encoder_attention,
        encoder_dense,
        same,
    )
    decoder_in, encoded = lax.optimization_barrier((decoder_in, encoded))
    caption = lax.dynamic_slice_in_dim(encoded, row * caption_length, caption_length, 0)
    branch, self_keep = attention_forward(
        decoder_in, gain_set[3], self_weights, "self", "t", None
    )
    decoder_one = decoder_in + branch
    branch, cross_keep = attention_forward(
        decoder_one, gain_set[4], cross_weights, "cross", "t", cross_context, caption
    )
    decoder_two = decoder_one + branch
    branch, decoder_dense_keep = dense_forward(decoder_two, gain_set[5], dense_weights, "t")
    decoder_top = decoder_two + branch
    final = spread(rms_norm(decoder_top, gain_set[6]).astype(jnp.bfloat16), "t")
    logits = product(final, out_table, LAST)
    rows = code_shape[0]
    codes = lax.dynamic_index_in_dim(code_ids, image, 0, False)
    held = codes // rows
    local_target = jnp.where(
        held % lax.axis_size("t") == part, held // lax.axis_size("t") * rows + codes % rows, -1
    )
    hits = jnp.arange(logits.shape[1], dtype=jnp.int32)[None, :] == local_target[:, None]
    highest = jnp.max(logits, axis=-1)
    highest, mass, target_logit, logit_total = joined(
        (
            highest,
            jnp.sum(jnp.exp(logits - highest[:, None]), axis=-1),
            jnp.sum(jnp.where(hits, logits, 0.0), axis=-1),
            jnp.sum(logits, axis=-1),
        )
    )
    partition = highest + jnp.log(mass)
    valid = lax.dynamic_index_in_dim(mask, image, 0, False)
    per_token = (
        partition
        - (1.0 - SMOOTH) * target_logit
        - SMOOTH * logit_total / VC
        + Z_WEIGHT * partition * partition
    )
    own_tokens = jnp.where(
        (jnp.arange(images)[:, None] == image) & (part == 0), per_token[None, :], 0.0
    )
    loss_part = jnp.sum(per_token * valid) / lax.axis_size("t")
    weighting = valid / count
    grad_logits = weighting[:, None] * (
        (1.0 + 2.0 * Z_WEIGHT * partition)[:, None] * jnp.exp(logits - partition[:, None])
        - (1.0 - SMOOTH) * hits.astype(jnp.float32)
        - SMOOTH / VC
    )
    grad_logits = grad_logits.astype(jnp.bfloat16)
    grad_out_table = product(grad_logits, final, FIRST).astype(jnp.bfloat16)
    out_grads = lax.psum_scatter(
        lax.psum_scatter(grad_out_table, "img", scatter_dimension=0, tiled=True),
        "dp",
        scatter_dimension=1,
        tiled=True,
    ).astype(jnp.float32)
    grad_final = collect(
        jnp.dot(grad_logits, out_table, preferred_element_type=jnp.float32), "t"
    )
    grad_top, gain_six = norm_back(decoder_top, gain_set[6], grad_final)
    grad_branch, gain_five, dense_one = dense_backward(
        grad_top, decoder_two, gain_set[5], "t", decoder_dense_keep
    )
    grad_two = grad_top + grad_branch
    grad_branch, gain_four, attention_two, grad_caption = attention_backward(
        grad_two, decoder_one, gain_set[4], cross_weights, "cross", "t", cross_context, cross_keep
    )
    grad_one = grad_two + grad_branch
    grad_branch, gain_three, attention_one, _ = attention_backward(
        grad_one, decoder_in, gain_set[3], self_weights, "self", "t", None, self_keep
    )
    grad_start = grad_one + grad_branch
    narrow = attention_shape[2]
    one_grads, two_grads, dense_one_grads = scatter(
        [
            [blocks_of(matrix, narrow, n) for matrix in attention_one],
            [blocks_of(matrix, narrow, n) for matrix in attention_two],
            dense_one,
        ],
        [attention_shape[1:], attention_shape[1:], dense_shape[1:]],
        n,
        1.0,
        2,
    )
    grad_start_late, out_grads = lax.optimization_barrier((grad_start, out_grads))
    grad_code_in = code_backward(grad_start_late, previous, starting, code_shape[0])
    grad_encoded = lax.dynamic_update_slice_in_dim(
        jnp.zeros(encoded.shape, jnp.float32), grad_caption, row * caption_length, 0
    )
    text_rows_back, encoder_gain_grads, attention_zero, dense_zero = encoder_backward(
        grad_encoded, encoder_gains, encoder_attention, encoder_dense, same, encoder_keep
    )
    text_hits = jnp.arange(text_rows, dtype=jnp.int32)[:, None] == text_local[None, :]
    text_grads = jnp.dot(
        text_hits.astype(jnp.bfloat16),
        text_rows_back.reshape(-1, text_width),
        preferred_element_type=jnp.float32,
    )

    def owned(values, axis):
        return lax.psum_scatter(
            values.astype(jnp.bfloat16), "dp", scatter_dimension=axis, tiled=True
        ).astype(jnp.float32)

    attention_grads = jnp.stack(
        [
            owned(attention_zero, 1),
            one_grads.reshape(attention_shape),
            two_grads.reshape(attention_shape),
        ]
    )
    dense_grads = jnp.stack([owned(dense_zero, 1), dense_one_grads.reshape(dense_shape)])
    code_grads = jnp.stack([owned(grad_code_in, 1), out_grads.reshape(code_shape)])
    squares = (
        jnp.sum(attention_grads * attention_grads)
        + jnp.sum(dense_grads * dense_grads)
        + jnp.sum(text_grads * text_grads)
        + jnp.sum(code_grads * code_grads)
    )
    sums = jnp.concatenate(
        [
            encoder_gain_grads[:3],
            jnp.stack([gain_three, gain_four, gain_five, gain_six]),
        ]
    )
    tail = jnp.zeros((1, D), jnp.float32).at[0, 0].set(squares).at[0, 1].set(loss_part)
    own_tokens = jnp.concatenate([own_tokens, jnp.zeros((8 - images, D), jnp.float32)])
    sums, row_sums = total_of(jnp.concatenate([sums, tail, own_tokens], axis=0), 8)
    per_image = row_sums[8 : 8 + images]
    gain_sums = sums[:7]
    loss = sums[7, 1] / count
    norm = jnp.sqrt(sums[7, 0] + jnp.sum(gain_sums * gain_sums))
    gain_grads = lax.dynamic_slice_in_dim(
        gain_sums, lax.axis_index(("dp",) + ROW) * gain_width, gain_width, 1
    )
    factor = jnp.minimum(1.0, CLIP / norm)
    rate = 0.012 * math.sqrt(12 * D * D + 4 * D * FF + VT * D + 2 * VC * D + 7 * D) / CLIP
    attention_out = update(
        attention_master, attention_momentum, attention_average, attention_grads, factor, rate
    )
    dense_out = update(dense_master, dense_momentum, dense_average, dense_grads, factor, rate)
    text_out = update(text_master, text_momentum, text_average, text_grads, factor, rate)
    code_out = update(code_master, code_momentum, code_average, code_grads, factor, rate)
    gain_out = update(gain_master, gain_momentum, gain_average, gain_grads, factor, rate)
    return (
        loss,
        norm,
        attention_out[0],
        attention_out[1],
        attention_out[2],
        attention_out[3],
        dense_out[0],
        dense_out[1],
        dense_out[2],
        dense_out[3],
        text_out[0],
        text_out[1],
        text_out[2],
        text_out[3],
        code_out[0],
        code_out[1],
        code_out[2],
        code_out[3],
        gain_out[0],
        gain_out[1],
        gain_out[2],
        gain_out[3],
        per_image,
    )


def solution(mesh):
    n, m = mesh.shape["dp"], mesh.shape["mp"]
    view = Mesh(mesh.devices.reshape(n, 4, m // 4), ("dp",) + ROW)
    return jax.shard_map(
        per_device,
        mesh=view,
        in_specs=(
            P("dp", None),
            P("dp", None),
            P("dp", None),
            P("dp", None),
            P("dp"),
            P(None, None, "dp", ROW),
            P(None, None, "dp", ROW),
            P(None, None, "dp", ROW),
            P(None, None, "dp", ROW),
            P(None, None, "dp", ROW),
            P(None, None, "dp", ROW),
            P(ROW, "dp"),
            P(ROW, "dp"),
            P(ROW, "dp"),
            P(None, ROW, "dp"),
            P(None, ROW, "dp"),
            P(None, ROW, "dp"),
            P(None, ("dp",) + ROW),
            P(None, ("dp",) + ROW),
            P(None, ("dp",) + ROW),
        ),
        out_specs=(
            P(),
            P(),
            P(None, None, "dp", ROW),
            P(None, None, "dp", ROW),
            P(None, None, "dp", ROW),
            P(None, None, "dp", ROW),
            P(None, None, "dp", ROW),
            P(None, None, "dp", ROW),
            P(None, None, "dp", ROW),
            P(None, None, "dp", ROW),
            P(ROW, "dp"),
            P(ROW, "dp"),
            P(ROW, "dp"),
            P(ROW, "dp"),
            P(None, ROW, "dp"),
            P(None, ROW, "dp"),
            P(None, ROW, "dp"),
            P(None, ROW, "dp"),
            P(None, ("dp",) + ROW),
            P(None, ("dp",) + ROW),
            P(None, ("dp",) + ROW),
            P(None, ("dp",) + ROW),
            P("dp", None),
        ),
        check_vma=False,
    )
```
